32 devices in a mesh: ctx: 8 (over z, core), exp: 4 (over y, x).
Axes of the slice: x: 2, y: 2, z: 4, core: 2. Of those that a mesh axis runs over, the one named last changes fastest.
Arguments:
- query_input: bfloat16 [1024, 8192], P('ctx', 'exp'), may hold values from -6 to 6
- key_input: bfloat16 [1024, 8192], P('ctx', 'exp'), may hold values from -6 to 6
- value_input: bfloat16 [1024, 8192], P('ctx', 'exp'), may hold values from -6 to 6
- gate_logits: float32 [2, 1024, 64], P(None, 'ctx', 'exp'), may hold values from -6 to 6
- comp_weight: float32 [2, 32, 64], P(None, None, 'exp'), may hold values from -6 to 6
- out_proj: bfloat16 [8192, 7168], P('exp', 'ctx'), may hold values from -0.0625 to 0.0625
- residual_in: bfloat16 [1024, 7168], P(('ctx', 'exp')), may hold values from -3 to 3
- ffn_gain: float32 [7168], replicated, may hold values from 0.25 to 1.75
- expert_ids: int32 [1024, 2], P(('ctx', 'exp')), may hold values from 0 to 3, all different within a row; in each aligned block of 32 rows (0 to 31, 32 to 63, ...) at most 32 rows name the same one
- route_gates: float32 [1024, 2], P(('ctx', 'exp')), may hold values from 0.2 to 1
- expert_gate: bfloat16 [4, 7168, 2048], P('exp', None, 'ctx'), may hold values from -0.0625 to 0.0625
- expert_up: bfloat16 [4, 7168, 2048], P('exp', None, 'ctx'), may hold values from -0.0625 to 0.0625
- expert_down: bfloat16 [4, 2048, 7168], P('exp', 'ctx'), may hold values from -0.125 to 0.125
Outputs:
- layer_out: bfloat16 [1024, 7168], P(('ctx', 'exp'))
The draws below stay inside these ranges and needn't reach their ends.
Inputs may be any that keep to these rules, and one draw needn't show every extreme that they name: `expert_ids`: each token names 2 different experts. In every aligned block of 32 consecutive tokens no expert is named more than 32 times, a bound that some block reaches.
All inputs are finite; a program needn't handle non-finite values.
Results may differ from the reference program's by a relative error of at most 0.0085.
Values may be sent and summed in bfloat16 or wider, within the bound.
No kernel may reach another device: no remote copies, remote signals or barrier semaphores. Data moves between devices by JAX's collectives and lax.ppermute only.
A program may use at most 128 MiB of HBM per device.

```python
import math
import jax
import jax.numpy as jnp
import numpy as np
from jax import lax

D = 7168
HEADS = 64
HD = 128
FF = 2048
BLOCK = 32
STRIDE = 16
WINDOW = 512
TOP = 2
TOK_DEV = 128
SEQ = 1024
EXPERTS = 4
CAP = 32
N_CTX = 8
N_EXP = 4


def level_of(stream_key, shape, split, least, largest):
    def one(position, shards_of):
        heights = jax.random.uniform(jax.random.fold_in(jax.random.fold_in(stream_key, 6), position), (shards_of,), jnp.float32, least / len(split), largest / len(split))
        return jnp.repeat(jnp.exp(heights), shape[position] // shards_of).reshape((-1,) + (1,) * (len(shape) - position - 1))

    loudness = one(*split[0])
    for cut in split[1:]:
        loudness = loudness * one(*cut)
    return loudness


def routed_block(key, own, number, rows, number_of, top, most, skew):
    sequence = jax.random.permutation(key, number_of)
    packed, ordinary = shares(number_of, rows * top, most, skew, True), shares(number_of, rows * top, most, skew, False)
    places = jnp.arange(number_of)

    def named(tallies, rotation):
        used = int((tallies > 0).sum())
        fixed = max(1, used // 4)
        passed = fixed + (places - fixed + rotation * (used - fixed)) % max(1, number_of - fixed)
        return jnp.zeros((number_of,), jnp.int32).at[sequence[jnp.where(places < fixed, places, passed)]].set(jnp.asarray(tallies, jnp.int32))

    tallies = jnp.where(number % 4 == 0, named(packed, number // 4), named(ordinary, number - number // 4 - 1))
    mixed = jax.random.permutation(jax.random.fold_in(own, 3), number_of)
    donor, sink = mixed[0:number_of // 2 * 2:2], mixed[1:number_of // 2 * 2:2]
    slack = jnp.minimum(tallies[donor] - 1, most - tallies[sink]) // 2
    slack = jnp.where((donor == sequence[0]) | (sink == sequence[0]) | (tallies[sink] == 0), 0, jnp.maximum(slack, 0))
    passed = jax.random.randint(jax.random.fold_in(own, 4), (number_of // 2,), 0, 1 << 20) % (slack + 1)
    tallies = tallies.at[donor].add(-passed).at[sink].add(passed)
    items = jnp.searchsorted(jnp.cumsum(tallies), jnp.arange(rows * top), side="right").astype(jnp.int32)
    listing = items.reshape(top, rows).T
    listing = listing[jax.random.permutation(jax.random.fold_in(own, 1), rows)]
    rotation = jax.random.randint(jax.random.fold_in(own, 2), (rows, 1), 0, top)
    return jnp.take_along_axis(listing, (jnp.arange(top)[None, :] + rotation) % top, axis=1)


def shares(amount, total, limit, skew, full):
    portions = [(1 << 20) // math.isqrt(standing ** skew) + 1 for standing in range(1, amount + 1)]
    largest = limit if full else min(limit, max(-(-total // amount), total * portions[0] // sum(portions)))
    least = 1 if total - largest >= amount - 1 else 0
    counts, surplus = [largest] + [least] * (amount - 1), total - largest - least * (amount - 1)
    while surplus > 0:
        movable = [i for i in range(1, amount) if counts[i] < largest] or [i for i in range(1, amount) if counts[i] < limit]
        mass, remaining = sum([portions[i] for i in movable]), surplus
        for i in movable:
            addition = min(limit - counts[i], max(1, remaining * portions[i] // mass), surplus)
            counts[i] = counts[i] + addition
            surplus = surplus - addition
    return np.array(counts)


def noise(own_key, extent, scale, reach, split=(), kind=jnp.bfloat16):
    entries = scale * jax.random.normal(own_key, extent, jnp.float32)
    if split:
        entries = entries * level_of(own_key, extent, split, -0.22, 0.18)
    return jnp.clip(entries, -reach, reach).astype(kind)


def setup_inputs(seed: int = 0) -> dict:
    seeds = jax.random.split(jax.random.key(seed), 14)
    query_input = noise(seeds[0], (SEQ, HEADS * HD), 1.0, 6.0, ((0, 8), (1, 4)))
    key_input = noise(seeds[1], (SEQ, HEADS * HD), 1.0, 6.0, ((0, 8), (1, 4)))
    value_input = noise(seeds[2], (SEQ, HEADS * HD), 1.0, 6.0, ((0, 8), (1, 4)))
    gate_logits = noise(seeds[3], (2, SEQ, HEADS), 1.5, 6.0, ((1, 8), (2, 4)), jnp.float32)
    comp_weight = noise(seeds[4], (2, BLOCK, HEADS), 1.2, 6.0, ((2, 4),), jnp.float32)
    out_proj = noise(seeds[5], (HEADS * HD, D), (HEADS * HD) ** -0.5, 0.0625, ((0, 4), (1, 8)))
    residual_in = noise(seeds[6], (SEQ, D), 0.5, 3.0, ((0, 32),))
    ffn_gain = jnp.clip(1.0 + 0.15 * jax.random.normal(seeds[7], (D,), jnp.float32), 0.25, 1.75)
    expert_ids_keys = jax.random.split(jax.random.fold_in(seeds[8], 1), SEQ // (TOK_DEV // N_EXP))
    expert_ids_turns = jax.random.permutation(jax.random.fold_in(seeds[8], 3), SEQ // (TOK_DEV // N_EXP))
    expert_ids = jax.vmap(lambda own, number: routed_block(jax.random.fold_in(seeds[8], 2), own, number, TOK_DEV // N_EXP, EXPERTS, TOP, CAP, 2))(expert_ids_keys, expert_ids_turns).reshape((SEQ, TOP))
    route_gates = jnp.clip(0.2 + 0.8 * jax.random.uniform(seeds[9], (SEQ, TOP), jnp.float32) ** level_of(seeds[9], (SEQ, TOP), ((0, 32),), -0.2, 0.2), 0.2, 1.0)
    expert_gate = noise(seeds[10], (EXPERTS, D, FF), D ** -0.5, 0.0625, ((0, 4), (2, 8)))
    expert_up = noise(seeds[11], (EXPERTS, D, FF), D ** -0.5, 0.0625, ((0, 4), (2, 8)))
    expert_down = noise(seeds[12], (EXPERTS, FF, D), FF ** -0.5, 0.125, ((0, 4), (1, 8)))
    return dict(query_input=query_input, key_input=key_input, value_input=value_input, gate_logits=gate_logits, comp_weight=comp_weight, out_proj=out_proj, residual_in=residual_in, ffn_gain=ffn_gain, expert_ids=expert_ids, route_gates=route_gates, expert_gate=expert_gate, expert_up=expert_up, expert_down=expert_down)


score_gain = 2.0
norm_eps = 1e-06

def head_norm(matrix, head_width):
    row_count = matrix.shape[0]
    shaped = matrix.reshape(row_count, -1, head_width).astype(jnp.float32)
    scaled = shaped * lax.rsqrt(lax.optimization_barrier(jnp.mean(shaped * shaped, axis=2, keepdims=True)) + norm_eps)
    return scaled.reshape(row_count, -1)

def compress(extended, position_weights, head_width):
    stride_len = position_weights.shape[0] // 2
    head_count = position_weights.shape[1]
    blocks = extended.reshape(-1, stride_len, head_count, head_width).astype(jnp.float32)
    first_half = jnp.einsum('nshd,sh->nhd', blocks[:-1], position_weights[:stride_len], precision=lax.Precision.HIGHEST)
    second_half = jnp.einsum('nshd,sh->nhd', blocks[1:], position_weights[stride_len:], precision=lax.Precision.HIGHEST)
    return (first_half + second_half).reshape(blocks.shape[0] - 1, head_count * head_width)

def reference(query_input, key_input, value_input, gate_logits, comp_weight, out_proj, residual_in, ffn_gain, expert_ids, route_gates, expert_gate, expert_up, expert_down):
    scale = score_gain / math.sqrt(HD)
    query_norm = head_norm(query_input, HD).astype(jnp.bfloat16)
    key_norm = head_norm(key_input, HD).astype(jnp.bfloat16)
    tail_rows = jnp.zeros((STRIDE, HEADS * HD), jnp.bfloat16)
    comp_keys = head_norm(compress(jnp.concatenate([key_input, tail_rows], 0), comp_weight[0], HD), HD).astype(jnp.bfloat16)
    comp_values = compress(jnp.concatenate([value_input, tail_rows], 0), comp_weight[1], HD).astype(jnp.bfloat16)
    positions = jnp.arange(SEQ, dtype=jnp.int32)
    query_heads = query_norm.reshape(SEQ, HEADS, HD).astype(jnp.float32)
    comp_count = comp_keys.shape[0]
    scores = jnp.einsum('thd,nhd->htn', query_heads, comp_keys.reshape(comp_count, HEADS, HD).astype(jnp.float32), precision=lax.Precision.HIGHEST)
    block_end = jnp.arange(comp_count, dtype=jnp.int32) * STRIDE + BLOCK - 1
    visible = block_end[None, :] <= positions[:, None]
    weights = jnp.where(visible[None], jnp.exp(scale * scores), 0.0)
    cmp_total = lax.optimization_barrier(jnp.sum(weights, axis=2)).T
    rounded = lax.optimization_barrier(weights.astype(jnp.bfloat16)).astype(jnp.float32)
    cmp_sum = jnp.einsum('htn,nhd->thd', rounded, comp_values.reshape(comp_count, HEADS, HD).astype(jnp.float32), precision=lax.Precision.HIGHEST)
    no_block = (positions < BLOCK - 1).astype(jnp.float32)
    cmp_out = cmp_sum / (cmp_total + no_block[:, None])[:, :, None]
    key_padded = jnp.concatenate([jnp.zeros((WINDOW, HEADS * HD), jnp.bfloat16), key_norm], 0)
    value_padded = jnp.concatenate([jnp.zeros((WINDOW, HEADS * HD), jnp.bfloat16), value_input], 0)

    def window_block(block_index):
        first_row = (block_index * TOK_DEV).astype(jnp.int32)
        block_queries = lax.dynamic_slice_in_dim(query_norm, first_row, TOK_DEV, 0).reshape(TOK_DEV, HEADS, HD).astype(jnp.float32)
        block_keys = lax.dynamic_slice_in_dim(key_padded, first_row, WINDOW + TOK_DEV, 0).reshape(-1, HEADS, HD).astype(jnp.float32)
        block_values = lax.dynamic_slice_in_dim(value_padded, first_row, WINDOW + TOK_DEV, 0).reshape(-1, HEADS, HD).astype(jnp.float32)
        query_pos = first_row + jnp.arange(TOK_DEV, dtype=jnp.int32)
        key_pos = first_row - WINDOW + jnp.arange(WINDOW + TOK_DEV, dtype=jnp.int32)
        local_scores = jnp.einsum('thd,shd->hts', block_queries, block_keys, precision=lax.Precision.HIGHEST)
        inside = (key_pos[None, :] <= query_pos[:, None]) & (key_pos[None, :] > query_pos[:, None] - WINDOW) & (key_pos[None, :] >= 0)
        local_weights = jnp.where(inside[None], jnp.exp(scale * local_scores), 0.0)
        local_total = lax.optimization_barrier(jnp.sum(local_weights, axis=2)).T
        local_rounded = lax.optimization_barrier(local_weights.astype(jnp.bfloat16)).astype(jnp.float32)
        local_sum = jnp.einsum('hts,shd->thd', local_rounded, block_values, precision=lax.Precision.HIGHEST)
        return local_sum / local_total[:, :, None]
    win_out = lax.map(window_block, jnp.arange(N_CTX, dtype=jnp.int32)).reshape(SEQ, HEADS, HD)
    branch_gates = jax.nn.sigmoid(gate_logits)
    attended = (branch_gates[0][:, :, None] * cmp_out + branch_gates[1][:, :, None] * win_out).reshape(SEQ, -1).astype(jnp.bfloat16)
    hidden_state = residual_in.astype(jnp.float32) + jnp.dot(attended, out_proj, preferred_element_type=jnp.float32)
    mean_square = lax.optimization_barrier(jnp.mean(hidden_state * hidden_state, axis=1, keepdims=True))
    normed = (hidden_state * lax.rsqrt(mean_square + norm_eps) * ffn_gain).astype(jnp.bfloat16)
    token_share = TOK_DEV // N_EXP
    device_count = N_CTX * N_EXP
    grouped_ids = expert_ids.reshape(device_count, token_share * TOP)
    chosen = (grouped_ids[:, :, None] == jnp.arange(EXPERTS, dtype=jnp.int32)[None, None, :]).astype(jnp.int32)
    slots = lax.optimization_barrier(jnp.sum((jnp.cumsum(chosen, axis=1) - chosen) * chosen, axis=2))
    row_index = (jnp.arange(device_count, dtype=jnp.int32)[:, None] * CAP + slots).reshape(-1)
    expert_index = grouped_ids.reshape(-1)
    token_index = jnp.arange(SEQ * TOP, dtype=jnp.int32) // TOP
    buffers = jnp.zeros((EXPERTS, device_count * CAP, D), jnp.bfloat16).at[expert_index, row_index].set(normed[token_index])
    ff_block = FF // N_CTX

    def run_expert(operands):
        expert_rows, gate_w, up_w, down_w = operands
        gate_part = jnp.dot(expert_rows, gate_w, preferred_element_type=jnp.float32)
        up_part = jnp.dot(expert_rows, up_w, preferred_element_type=jnp.float32)
        activated = (jax.nn.silu(gate_part) * up_part).astype(jnp.bfloat16)
        pieces = jnp.einsum('mcf,cfd->cmd', activated.reshape(-1, N_CTX, ff_block).astype(jnp.float32), down_w.reshape(N_CTX, ff_block, D).astype(jnp.float32), precision=lax.Precision.HIGHEST)
        rounded_pieces = lax.optimization_barrier(pieces.astype(jnp.bfloat16)).astype(jnp.float32)
        return lax.optimization_barrier(jnp.sum(rounded_pieces, axis=0)).astype(jnp.bfloat16)
    outputs = lax.map(run_expert, (buffers, expert_gate, expert_up, expert_down))
    picked = outputs[expert_index, row_index].reshape(SEQ, TOP, D).astype(jnp.float32)
    moe_out = lax.optimization_barrier(jnp.sum(route_gates[:, :, None] * picked, axis=1))
    return (hidden_state + moe_out).astype(jnp.bfloat16)
```

```python
import math

import jax
import jax.numpy as jnp
from jax import lax
from jax.sharding import PartitionSpec as P

WINDOW = 512


score_gain = 2.0
norm_eps = 1e-06


def passed_along(block, axis, distance):
    devices = range(lax.axis_size(axis))
    route = [(i - distance, i) for i in devices if i - distance in devices]
    return lax.ppermute(block, axis, route)


def head_norm(matrix, head_width):
    row_count = matrix.shape[0]
    shaped = matrix.reshape(row_count, -1, head_width).astype(jnp.float32)
    scaled = shaped * lax.rsqrt(jnp.mean(shaped * shaped, axis=2, keepdims=True) + norm_eps)
    return scaled.reshape(row_count, -1)


def compress(extended, position_weights, head_width):
    stride_len = position_weights.shape[0] // 2
    head_count = position_weights.shape[1]
    blocks = extended.reshape(-1, stride_len, head_count, head_width).astype(jnp.float32)
    first_half = jnp.einsum(
        "nshd,sh->nhd", blocks[:-1], position_weights[:stride_len], precision=lax.Precision.HIGHEST
    )
    second_half = jnp.einsum(
        "nshd,sh->nhd", blocks[1:], position_weights[stride_len:], precision=lax.Precision.HIGHEST
    )
    return (first_half + second_half).reshape(blocks.shape[0] - 1, head_count * head_width)


def window_attention(query_input, key_input, value_input, gate_logits, comp_weight):
    row_count = query_input.shape[0]
    head_count = comp_weight.shape[2]
    head_width = query_input.shape[1] // head_count
    block_len = comp_weight.shape[1]
    stride_len = block_len // 2
    exp_count = lax.axis_size("exp")
    ctx_index = lax.axis_index("ctx")
    scale = score_gain / math.sqrt(head_width)
    query_norm = head_norm(query_input, head_width).astype(jnp.bfloat16)
    key_norm = head_norm(key_input, head_width).astype(jnp.bfloat16)
    next_keys, next_values = passed_along(
        (key_input[:stride_len], value_input[:stride_len]), "ctx", -1
    )
    comp_keys = head_norm(
        compress(jnp.concatenate([key_input, next_keys], 0), comp_weight[0], head_width), head_width
    ).astype(jnp.bfloat16)
    comp_values = compress(
        jnp.concatenate([value_input, next_values], 0), comp_weight[1], head_width
    ).astype(jnp.bfloat16)
    query_pos = ctx_index * row_count + jnp.arange(row_count, dtype=jnp.int32)
    query_heads = query_norm.reshape(row_count, head_count, head_width)
    part_keys = lax.all_gather(comp_keys, "ctx", axis=0, tiled=True)
    part_values = lax.all_gather(comp_values, "ctx", axis=0, tiled=True)
    part_count = part_keys.shape[0]
    scores = jnp.einsum(
        "thd,nhd->htn",
        query_heads,
        part_keys.reshape(part_count, head_count, head_width),
        preferred_element_type=jnp.float32,
    )
    block_end = jnp.arange(part_count, dtype=jnp.int32) * stride_len + block_len - 1
    visible = block_end[None, :] <= query_pos[:, None]
    weights = jnp.where(visible[None], jnp.exp(scale * scores), 0.0)
    running_total = jnp.sum(weights, axis=2).T
    collected = jnp.einsum(
        "htn,nhd->thd",
        weights.astype(jnp.bfloat16),
        part_values.reshape(part_count, head_count, head_width),
        preferred_element_type=jnp.float32,
    )
    cmp_sum = collected.reshape(row_count, -1)
    no_block = (query_pos < block_len - 1).astype(jnp.float32)
    cmp_out = (
        cmp_sum.reshape(row_count, head_count, head_width)
        / (running_total + no_block[:, None])[:, :, None]
    )
    shift_count = max(1, WINDOW // row_count)
    earlier_keys = []
    earlier_values = []
    for distance in range(shift_count, 0, -1):
        moved_keys, moved_values = passed_along((key_norm, value_input), "ctx", distance)
        earlier_keys.append(moved_keys)
        earlier_values.append(moved_values)
    near_keys = jnp.concatenate(earlier_keys + [key_norm], 0)
    near_values = jnp.concatenate(earlier_values + [value_input], 0)
    key_pos = ctx_index * row_count - WINDOW + jnp.arange(near_keys.shape[0], dtype=jnp.int32)
    near_scores = jnp.einsum(
        "thd,shd->hts",
        query_heads,
        near_keys.reshape(-1, head_count, head_width),
        preferred_element_type=jnp.float32,
    )
    inside = (
        (key_pos[None, :] <= query_pos[:, None])
        & (key_pos[None, :] > query_pos[:, None] - WINDOW)
        & (key_pos[None, :] >= 0)
    )
    near_weights = jnp.where(inside[None], jnp.exp(scale * near_scores), 0.0)
    win_total = jnp.sum(near_weights, axis=2).T
    win_sum = jnp.einsum(
        "hts,shd->thd",
        near_weights.astype(jnp.bfloat16),
        near_values.reshape(-1, head_count, head_width),
        preferred_element_type=jnp.float32,
    )
    win_out = win_sum / win_total[:, :, None]
    branch_gates = jax.nn.sigmoid(gate_logits)
    attended = (
        (branch_gates[0][:, :, None] * cmp_out + branch_gates[1][:, :, None] * win_out)
        .reshape(row_count, -1)
        .astype(jnp.bfloat16)
    )
    return attended


def head_attention(query_input, key_input, value_input, gate_logits, comp_weight):
    row_count = query_input.shape[0]
    head_count = comp_weight.shape[2]
    head_width = query_input.shape[1] // head_count
    block_len = comp_weight.shape[1]
    stride_len = block_len // 2
    ctx_count = lax.axis_size("ctx")
    ctx_index = lax.axis_index("ctx")
    own = head_count // ctx_count
    width = own * head_width
    seq_len = ctx_count * row_count
    scale = score_gain / math.sqrt(head_width)
    packed = jnp.stack([query_input, key_input, value_input], 0).reshape(
        3, row_count, ctx_count, width
    )
    packed = jnp.transpose(packed, (2, 0, 1, 3))
    moved = lax.all_to_all(packed, "ctx", split_axis=0, concat_axis=0, tiled=True)
    moved = jnp.transpose(moved, (1, 0, 2, 3)).reshape(3, seq_len, width)
    logits = lax.all_gather(gate_logits, "ctx", axis=1, tiled=True)
    logits = lax.dynamic_slice_in_dim(logits, ctx_index * own, own, 2)
    weights_own = lax.dynamic_slice_in_dim(comp_weight, ctx_index * own, own, 2)
    queries = head_norm(moved[0], head_width).astype(jnp.bfloat16)
    keys = head_norm(moved[1], head_width).astype(jnp.bfloat16)
    values = moved[2]
    tail_rows = jnp.zeros((stride_len, width), jnp.bfloat16)
    comp_keys = head_norm(
        compress(jnp.concatenate([moved[1], tail_rows], 0), weights_own[0], head_width), head_width
    ).astype(jnp.bfloat16)
    comp_values = compress(
        jnp.concatenate([values, tail_rows], 0), weights_own[1], head_width
    ).astype(jnp.bfloat16)
    query_heads = queries.reshape(seq_len, own, head_width)
    part_count = comp_keys.shape[0]
    query_pos = jnp.arange(seq_len, dtype=jnp.int32)
    scores = jnp.einsum(
        "thd,nhd->htn",
        query_heads,
        comp_keys.reshape(part_count, own, head_width),
        preferred_element_type=jnp.float32,
    )
    block_end = jnp.arange(part_count, dtype=jnp.int32) * stride_len + block_len - 1
    visible = block_end[None, :] <= query_pos[:, None]
    weights = jnp.where(visible[None], jnp.exp(scale * scores), 0.0)
    total = jnp.sum(weights, axis=2).T
    cmp_sum = jnp.einsum(
        "htn,nhd->thd",
        weights.astype(jnp.bfloat16),
        comp_values.reshape(part_count, own, head_width),
        preferred_element_type=jnp.float32,
    )
    no_block = (query_pos < block_len - 1).astype(jnp.float32)
    cmp_out = cmp_sum / (total + no_block[:, None])[:, :, None]
    reach = WINDOW + row_count
    pad = jnp.zeros((WINDOW, width), jnp.bfloat16)
    key_pad = jnp.concatenate([pad, keys], 0)
    value_pad = jnp.concatenate([pad, values], 0)
    near_keys = jnp.stack(
        [key_pad[i * row_count : i * row_count + reach] for i in range(ctx_count)]
    ).reshape(ctx_count, reach, own, head_width)
    near_values = jnp.stack(
        [value_pad[i * row_count : i * row_count + reach] for i in range(ctx_count)]
    ).reshape(ctx_count, reach, own, head_width)
    near_scores = jnp.einsum(
        "bthd,bshd->bhts",
        query_heads.reshape(ctx_count, row_count, own, head_width),
        near_keys,
        preferred_element_type=jnp.float32,
    )
    rows = jnp.arange(row_count, dtype=jnp.int32)[None, :, None]
    cols = jnp.arange(reach, dtype=jnp.int32)[None, None, :] - WINDOW
    first = (jnp.arange(ctx_count, dtype=jnp.int32) * row_count)[:, None, None]
    inside = (cols <= rows) & (cols > rows - WINDOW) & (cols + first >= 0)
    near_weights = jnp.where(inside[:, None], jnp.exp(scale * near_scores), 0.0)
    win_total = jnp.transpose(jnp.sum(near_weights, axis=3), (0, 2, 1)).reshape(seq_len, own)
    win_sum = jnp.einsum(
        "bhts,bshd->bthd",
        near_weights.astype(jnp.bfloat16),
        near_values,
        preferred_element_type=jnp.float32,
    ).reshape(seq_len, own, head_width)
    win_out = win_sum / win_total[:, :, None]
    gates = jax.nn.sigmoid(logits)
    return (
        (gates[0][:, :, None] * cmp_out + gates[1][:, :, None] * win_out)
        .reshape(seq_len, width)
        .astype(jnp.bfloat16)
    )


def local(
    query_input,
    key_input,
    value_input,
    gate_logits,
    comp_weight,
    out_proj,
    residual_in,
    ffn_gain,
    expert_ids,
    route_gates,
    expert_gate,
    expert_up,
    expert_down,
):
    row_count = query_input.shape[0]
    ctx_count = lax.axis_size("ctx")
    exp_count = lax.axis_size("exp")
    ctx_index = lax.axis_index("ctx")
    exp_index = lax.axis_index("exp")
    share = row_count // exp_count
    seq_len = row_count * ctx_count
    cols = out_proj.shape[1]
    model_width = cols * ctx_count
    hidden_units = expert_gate.shape[2]
    own_tokens = ctx_count * share

    experts = jnp.arange(exp_count, dtype=jnp.int32)
    route_table = jnp.sum(
        jnp.where(expert_ids[:, :, None] == experts, route_gates[:, :, None], 0.0), axis=1
    )
    route_all = lax.all_gather(route_table, ("ctx", "exp"), axis=0, tiled=True)
    route_own = lax.dynamic_slice_in_dim(route_all, exp_index, 1, 1)
    residual = lax.all_to_all(residual_in, "ctx", split_axis=1, concat_axis=0, tiled=True)

    attention_args = (query_input, key_input, value_input, gate_logits, comp_weight)
    if comp_weight.shape[2] % ctx_count == 0:
        attended = head_attention(*attention_args)
        width = attended.shape[1]
        attended = jnp.transpose(
            attended.reshape(ctx_count, exp_count, share, width), (1, 0, 2, 3)
        ).reshape(seq_len, width)
        spread_heads = lax.all_gather(attended, "ctx", axis=0)
        partial = jnp.einsum(
            "csk,ckd->sd",
            spread_heads,
            out_proj.reshape(ctx_count, width, cols),
            preferred_element_type=jnp.float32,
        )
    else:
        attended = window_attention(*attention_args)
        spread_rows = lax.all_gather(
            attended.reshape(1, exp_count, share, -1), "ctx", axis=0, tiled=True
        )
        partial = jnp.einsum(
            "cerh,hd->ecrd", spread_rows, out_proj, preferred_element_type=jnp.float32
        )
    pieces = lax.all_to_all(
        partial.astype(jnp.bfloat16).reshape(exp_count, own_tokens, cols),
        "exp",
        split_axis=0,
        concat_axis=0,
        tiled=True,
    )
    hidden_state = residual.reshape(own_tokens, cols).astype(jnp.float32) + jnp.sum(
        pieces.astype(jnp.float32), axis=0
    )
    gain = lax.dynamic_slice_in_dim(ffn_gain, ctx_index * cols, cols, 0)
    scaled = (hidden_state * gain).astype(jnp.bfloat16)
    squares = jnp.sum(hidden_state * hidden_state, axis=1)
    rows = lax.all_gather(scaled, ("ctx", "exp"), axis=0, tiled=True)
    rows = rows.reshape(ctx_count, seq_len, cols)
    squares = lax.all_gather(squares, ("ctx", "exp"), axis=0, tiled=True)
    mean_square = jnp.sum(squares.reshape(ctx_count, seq_len), axis=0) / model_width
    inverse = lax.rsqrt(mean_square + norm_eps)[:, None]

    gate_part = inverse * jnp.einsum(
        "ctk,ckf->tf",
        rows,
        expert_gate.reshape(ctx_count, cols, hidden_units),
        preferred_element_type=jnp.float32,
    )
    up_part = inverse * jnp.einsum(
        "ctk,ckf->tf",
        rows,
        expert_up.reshape(ctx_count, cols, hidden_units),
        preferred_element_type=jnp.float32,
    )
    activated = (jax.nn.silu(gate_part) * up_part).astype(jnp.bfloat16)
    activated = jnp.transpose(
        activated.reshape(exp_count, ctx_count, share, hidden_units), (1, 0, 2, 3)
    ).reshape(seq_len, hidden_units)
    outs = jnp.dot(activated, expert_down[0], preferred_element_type=jnp.float32)
    outs = (outs * route_own).astype(jnp.bfloat16)
    outs = outs.reshape(ctx_count, exp_count, share, model_width)
    place = (0, exp_index, 0, ctx_index * cols)
    mine = lax.dynamic_slice(outs, place, (ctx_count, 1, share, cols))
    mine = mine.astype(jnp.float32) + hidden_state.reshape(ctx_count, 1, share, cols)
    outs = lax.dynamic_update_slice(outs, mine.astype(jnp.bfloat16), place)
    return lax.psum_scatter(
        outs.reshape(seq_len, model_width), ("ctx", "exp"), scatter_dimension=0, tiled=True
    )


def solution(mesh):
    in_specs = (
        P("ctx", "exp"),
        P("ctx", "exp"),
        P("ctx", "exp"),
        P(None, "ctx", "exp"),
        P(None, None, "exp"),
        P("exp", "ctx"),
        P(("ctx", "exp"), None),
        P(),
        P(("ctx", "exp"), None),
        P(("ctx", "exp"), None),
        P("exp", None, "ctx"),
        P("exp", None, "ctx"),
        P("exp", "ctx", None),
    )
    out_specs = P(("ctx", "exp"), None)
    return jax.shard_map(local, mesh=mesh, in_specs=in_specs, out_specs=out_specs, check_vma=False)
```

```python
import functools
import math

import jax
import jax.numpy as jnp
from jax import lax
from jax.experimental import pallas as pl
from jax.experimental.pallas import tpu as pltpu
from jax.sharding import PartitionSpec as P

WINDOW = 512


score_gain = 2.0
norm_eps = 1e-06


def passed_along(block, axis, distance):
    devices = range(lax.axis_size(axis))
    route = [(i - distance, i) for i in devices if i - distance in devices]
    return lax.ppermute(block, axis, route)


def head_norm(matrix, head_width):
    row_count = matrix.shape[0]
    shaped = matrix.reshape(row_count, -1, head_width).astype(jnp.float32)
    scaled = shaped * lax.rsqrt(jnp.mean(shaped * shaped, axis=2, keepdims=True) + norm_eps)
    return scaled.reshape(row_count, -1)


def compress(extended, position_weights, head_width):
    stride_len = position_weights.shape[0] // 2
    head_count = position_weights.shape[1]
    blocks = extended.reshape(-1, stride_len, head_count, head_width).astype(jnp.float32)
    first_half = jnp.einsum(
        "nshd,sh->nhd", blocks[:-1], position_weights[:stride_len], precision=lax.Precision.HIGHEST
    )
    second_half = jnp.einsum(
        "nshd,sh->nhd", blocks[1:], position_weights[stride_len:], precision=lax.Precision.HIGHEST
    )
    return (first_half + second_half).reshape(blocks.shape[0] - 1, head_count * head_width)


def window_attention(query_input, key_input, value_input, gate_logits, comp_weight):
    row_count = query_input.shape[0]
    head_count = comp_weight.shape[2]
    head_width = query_input.shape[1] // head_count
    block_len = comp_weight.shape[1]
    stride_len = block_len // 2
    exp_count = lax.axis_size("exp")
    ctx_index = lax.axis_index("ctx")
    scale = score_gain / math.sqrt(head_width)
    query_norm = head_norm(query_input, head_width).astype(jnp.bfloat16)
    key_norm = head_norm(key_input, head_width).astype(jnp.bfloat16)
    next_keys, next_values = passed_along(
        (key_input[:stride_len], value_input[:stride_len]), "ctx", -1
    )
    comp_keys = head_norm(
        compress(jnp.concatenate([key_input, next_keys], 0), comp_weight[0], head_width), head_width
    ).astype(jnp.bfloat16)
    comp_values = compress(
        jnp.concatenate([value_input, next_values], 0), comp_weight[1], head_width
    ).astype(jnp.bfloat16)
    query_pos = ctx_index * row_count + jnp.arange(row_count, dtype=jnp.int32)
    query_heads = query_norm.reshape(row_count, head_count, head_width)
    part_keys = lax.all_gather(comp_keys, "ctx", axis=0, tiled=True)
    part_values = lax.all_gather(comp_values, "ctx", axis=0, tiled=True)
    part_count = part_keys.shape[0]
    scores = jnp.einsum(
        "thd,nhd->htn",
        query_heads,
        part_keys.reshape(part_count, head_count, head_width),
        preferred_element_type=jnp.float32,
    )
    block_end = jnp.arange(part_count, dtype=jnp.int32) * stride_len + block_len - 1
    visible = block_end[None, :] <= query_pos[:, None]
    weights = jnp.where(visible[None], jnp.exp(scale * scores), 0.0)
    running_total = jnp.sum(weights, axis=2).T
    collected = jnp.einsum(
        "htn,nhd->thd",
        weights.astype(jnp.bfloat16),
        part_values.reshape(part_count, head_count, head_width),
        preferred_element_type=jnp.float32,
    )
    cmp_sum = collected.reshape(row_count, -1)
    no_block = (query_pos < block_len - 1).astype(jnp.float32)
    cmp_out = (
        cmp_sum.reshape(row_count, head_count, head_width)
        / (running_total + no_block[:, None])[:, :, None]
    )
    shift_count = max(1, WINDOW // row_count)
    earlier_keys = []
    earlier_values = []
    for distance in range(shift_count, 0, -1):
        moved_keys, moved_values = passed_along((key_norm, value_input), "ctx", distance)
        earlier_keys.append(moved_keys)
        earlier_values.append(moved_values)
    near_keys = jnp.concatenate(earlier_keys + [key_norm], 0)
    near_values = jnp.concatenate(earlier_values + [value_input], 0)
    key_pos = ctx_index * row_count - WINDOW + jnp.arange(near_keys.shape[0], dtype=jnp.int32)
    near_scores = jnp.einsum(
        "thd,shd->hts",
        query_heads,
        near_keys.reshape(-1, head_count, head_width),
        preferred_element_type=jnp.float32,
    )
    inside = (
        (key_pos[None, :] <= query_pos[:, None])
        & (key_pos[None, :] > query_pos[:, None] - WINDOW)
        & (key_pos[None, :] >= 0)
    )
    near_weights = jnp.where(inside[None], jnp.exp(scale * near_scores), 0.0)
    win_total = jnp.sum(near_weights, axis=2).T
    win_sum = jnp.einsum(
        "hts,shd->thd",
        near_weights.astype(jnp.bfloat16),
        near_values.reshape(-1, head_count, head_width),
        preferred_element_type=jnp.float32,
    )
    win_out = win_sum / win_total[:, :, None]
    branch_gates = jax.nn.sigmoid(gate_logits)
    attended = (
        (branch_gates[0][:, :, None] * cmp_out + branch_gates[1][:, :, None] * win_out)
        .reshape(row_count, -1)
        .astype(jnp.bfloat16)
    )
    return attended


def general(
    query_input,
    key_input,
    value_input,
    gate_logits,
    comp_weight,
    out_proj,
    residual_in,
    ffn_gain,
    expert_ids,
    route_gates,
    expert_gate,
    expert_up,
    expert_down,
):
    row_count = query_input.shape[0]
    ctx_count = lax.axis_size("ctx")
    exp_count = lax.axis_size("exp")
    ctx_index = lax.axis_index("ctx")
    exp_index = lax.axis_index("exp")
    share = row_count // exp_count
    seq_len = row_count * ctx_count
    cols = out_proj.shape[1]
    model_width = cols * ctx_count
    hidden_units = expert_gate.shape[2]
    own_tokens = ctx_count * share

    experts = jnp.arange(exp_count, dtype=jnp.int32)
    route_table = jnp.sum(
        jnp.where(expert_ids[:, :, None] == experts, route_gates[:, :, None], 0.0), axis=1
    )
    route_all = lax.all_gather(route_table, ("ctx", "exp"), axis=0, tiled=True)
    route_own = lax.dynamic_slice_in_dim(route_all, exp_index, 1, 1)
    residual = lax.all_to_all(residual_in, "ctx", split_axis=1, concat_axis=0, tiled=True)

    attention_args = (query_input, key_input, value_input, gate_logits, comp_weight)
    attended = window_attention(*attention_args)
    spread_rows = lax.all_gather(
        attended.reshape(1, exp_count, share, -1), "ctx", axis=0, tiled=True
    )
    partial = jnp.einsum(
        "cerh,hd->ecrd", spread_rows, out_proj, preferred_element_type=jnp.float32
    )
    pieces = lax.all_to_all(
        partial.astype(jnp.bfloat16).reshape(exp_count, own_tokens, cols),
        "exp",
        split_axis=0,
        concat_axis=0,
        tiled=True,
    )
    hidden_state = residual.reshape(own_tokens, cols).astype(jnp.float32) + jnp.sum(
        pieces.astype(jnp.float32), axis=0
    )
    gain = lax.dynamic_slice_in_dim(ffn_gain, ctx_index * cols, cols, 0)
    scaled = (hidden_state * gain).astype(jnp.bfloat16)
    squares = jnp.sum(hidden_state * hidden_state, axis=1)
    rows = lax.all_gather(scaled, ("ctx", "exp"), axis=0, tiled=True)
    rows = rows.reshape(ctx_count, seq_len, cols)
    squares = lax.all_gather(squares, ("ctx", "exp"), axis=0, tiled=True)
    mean_square = jnp.sum(squares.reshape(ctx_count, seq_len), axis=0) / model_width
    inverse = lax.rsqrt(mean_square + norm_eps)[:, None]

    gate_part = inverse * jnp.einsum(
        "ctk,ckf->tf",
        rows,
        expert_gate.reshape(ctx_count, cols, hidden_units),
        preferred_element_type=jnp.float32,
    )
    up_part = inverse * jnp.einsum(
        "ctk,ckf->tf",
        rows,
        expert_up.reshape(ctx_count, cols, hidden_units),
        preferred_element_type=jnp.float32,
    )
    activated = (jax.nn.silu(gate_part) * up_part).astype(jnp.bfloat16)
    activated = jnp.transpose(
        activated.reshape(exp_count, ctx_count, share, hidden_units), (1, 0, 2, 3)
    ).reshape(seq_len, hidden_units)
    outs = jnp.dot(activated, expert_down[0], preferred_element_type=jnp.float32)
    outs = (outs * route_own).astype(jnp.bfloat16)
    outs = outs.reshape(ctx_count, exp_count, share, model_width)
    place = (0, exp_index, 0, ctx_index * cols)
    mine = lax.dynamic_slice(outs, place, (ctx_count, 1, share, cols))
    mine = mine.astype(jnp.float32) + hidden_state.reshape(ctx_count, 1, share, cols)
    outs = lax.dynamic_update_slice(outs, mine.astype(jnp.bfloat16), place)
    return lax.psum_scatter(
        outs.reshape(seq_len, model_width), ("ctx", "exp"), scatter_dimension=0, tiled=True
    )


def high_low(values):
    high = lax.reduce_precision(values, 8, 7)
    return jnp.stack([high, values - high], 0).astype(jnp.bfloat16)


def unit_rows(block):
    return block * lax.rsqrt(jnp.mean(block * block, axis=1, keepdims=True) + norm_eps)


def attend_kernel(row_count, share, block_len, head_width, moved, taps, gates, out, keys, values):
    ctx_count = moved.shape[0]
    own = moved.shape[2] // head_width
    seq_len = row_count * ctx_count
    stride_len = block_len // 2
    part_count = seq_len // stride_len
    scale = score_gain / math.sqrt(head_width)

    def dot(left, right):
        return jnp.dot(left, right, preferred_element_type=jnp.float32)

    def dot_rows(left, right):
        return lax.dot_general(
            left, right, (((1,), (1,)), ((), ())), preferred_element_type=jnp.float32
        )

    def compressed(row, block):
        group = lax.broadcasted_iota(jnp.int32, (part_count, seq_len), 0)
        token_group = lax.broadcasted_iota(jnp.int32, (part_count, seq_len), 1) // stride_len
        band = jnp.where(token_group == group, taps[row : row + 1, :], 0.0)
        band = jnp.where(token_group == group + 1, taps[row + 1 : row + 2, :], band)
        high = band.astype(jnp.bfloat16)
        low = (band - high.astype(jnp.float32)).astype(jnp.bfloat16)
        return dot(high, block) + dot(low, block)

    for head in range(own):
        lanes = slice(head * head_width, (head + 1) * head_width)
        raw_keys = moved[:, row_count : 2 * row_count, lanes].reshape(seq_len, head_width)
        keys[...] = unit_rows(raw_keys.astype(jnp.float32)).astype(jnp.bfloat16)
        raw_values = moved[:, 2 * row_count : 3 * row_count, lanes].reshape(seq_len, head_width)
        values[...] = raw_values
        comp_keys = unit_rows(compressed(2 * head, raw_keys)).astype(jnp.bfloat16)
        comp_values = compressed(2 * (own + head), raw_values).astype(jnp.bfloat16)
        for block in range(ctx_count):
            query = moved[block, 0:row_count, lanes].astype(jnp.float32)
            query = unit_rows(query).astype(jnp.bfloat16)
            base = block * row_count
            rows = slice(base, base + row_count)
            spot = base + lax.broadcasted_iota(jnp.int32, (row_count, part_count), 0)
            ends = lax.broadcasted_iota(jnp.int32, (row_count, part_count), 1) * stride_len
            seen = ends + (block_len - 1) <= spot
            weight = jnp.where(seen, jnp.exp(scale * dot_rows(query, comp_keys)), 0.0)
            total = jnp.sum(weight, axis=1, keepdims=True)
            total = total + jnp.where(spot[:, :1] < block_len - 1, 1.0, 0.0)
            far = dot(weight.astype(jnp.bfloat16), comp_values) / total
            start = max(0, base - WINDOW)
            reach = base + row_count - start
            spot = base + lax.broadcasted_iota(jnp.int32, (row_count, reach), 0)
            key_spot = start + lax.broadcasted_iota(jnp.int32, (row_count, reach), 1)
            seen = (key_spot <= spot) & (key_spot > spot - WINDOW)
            score = dot_rows(query, keys[start : start + reach, :])
            weight = jnp.where(seen, jnp.exp(scale * score), 0.0)
            total = jnp.sum(weight, axis=1, keepdims=True)
            near = dot(weight.astype(jnp.bfloat16), values[start : start + reach, :]) / total
            mixed = (
                gates[rows, head : head + 1] * far
                + gates[rows, own + head : own + head + 1] * near
            ).astype(jnp.bfloat16)
            for part in range(row_count // share):
                target = (part * ctx_count + block) * share
                out[target : target + share, lanes] = mixed[part * share : (part + 1) * share]


def attend(moved, taps, gates, row_count, share, block_len, head_width):
    seq_len = moved.shape[0] * row_count
    width = moved.shape[2]
    return pl.pallas_call(
        functools.partial(attend_kernel, row_count, share, block_len, head_width),
        out_shape=jax.ShapeDtypeStruct((seq_len, width), jnp.bfloat16),
        scratch_shapes=[
            pltpu.VMEM((seq_len, head_width), jnp.bfloat16),
            pltpu.VMEM((seq_len, head_width), jnp.bfloat16),
        ],
        compiler_params=pltpu.CompilerParams(vmem_limit_bytes=48 * 2**20),
        name="attend",
    )(moved, taps, gates)


def expert_kernel(ctx_count, exp_count, share, rows, gain, gate_w, up_w, route, out, gate_acc, up_acc, squares):
    step = pl.program_id(0)

    @pl.when(step == 0)
    def _():
        gate_acc[...] = jnp.zeros_like(gate_acc)
        up_acc[...] = jnp.zeros_like(up_acc)
        squares[...] = jnp.zeros_like(squares)

    block = rows[0]
    gate_acc[...] += jnp.dot(block, gate_w[...], preferred_element_type=jnp.float32)
    up_acc[...] += jnp.dot(block, up_w[...], preferred_element_type=jnp.float32)
    lane = squares.shape[1]
    total = squares[...]
    for part in range(block.shape[1] // lane):
        lanes = slice(part * lane, (part + 1) * lane)
        plain = block[:, lanes].astype(jnp.float32) * (1.0 / gain[0, :, lanes])
        total = total + plain * plain
    squares[...] = total

    @pl.when(step == pl.num_programs(0) - 1)
    def _():
        model_width = ctx_count * rows.shape[2]
        mean_square = jnp.sum(squares[...], axis=1, keepdims=True) / model_width
        inverse = lax.rsqrt(mean_square + norm_eps)
        gate_part = gate_acc[...] * inverse
        up_part = up_acc[...] * inverse
        active = gate_part / (1.0 + jnp.exp(-gate_part)) * up_part * route[...]
        active = active.astype(jnp.bfloat16)
        half = share // 2
        for exp_spot in range(exp_count):
            for ctx_spot in range(ctx_count):
                base = (exp_spot * ctx_count + ctx_spot) * share
                target = (ctx_spot * exp_count + exp_spot) * half
                out[0, target : target + half, :] = active[base : base + half]
                target = (exp_spot * ctx_count + ctx_spot) * half
                out[1, target : target + half, :] = active[base + half : base + share]


def run_expert(rows, gain, gate_w, up_w, route, exp_count, share):
    ctx_count, seq_len, cols = rows.shape
    units = gate_w.shape[1]
    lane = math.gcd(128, cols)
    return pl.pallas_call(
        functools.partial(expert_kernel, ctx_count, exp_count, share),
        grid=(ctx_count,),
        in_specs=[
            pl.BlockSpec((1, seq_len, cols), lambda i: (i, 0, 0)),
            pl.BlockSpec((1, 1, cols), lambda i: (i, 0, 0)),
            pl.BlockSpec((cols, units), lambda i: (i, 0)),
            pl.BlockSpec((cols, units), lambda i: (i, 0)),
            pl.BlockSpec((seq_len, 1), lambda i: (0, 0)),
        ],
        out_specs=pl.BlockSpec((2, seq_len // 2, units), lambda i: (0, 0, 0)),
        out_shape=jax.ShapeDtypeStruct((2, seq_len // 2, units), jnp.bfloat16),
        scratch_shapes=[
            pltpu.VMEM((seq_len, units), jnp.float32),
            pltpu.VMEM((seq_len, units), jnp.float32),
            pltpu.VMEM((seq_len, lane), jnp.float32),
        ],
        compiler_params=pltpu.CompilerParams(vmem_limit_bytes=48 * 2**20),
        cost_estimate=pl.CostEstimate(
            flops=4 * seq_len * units * ctx_count * cols,
            bytes_accessed=2 * ctx_count * cols * (seq_len + 2 * units),
            transcendentals=seq_len * units,
        ),
        name="expert",
    )(rows, gain.reshape(ctx_count, 1, cols), gate_w, up_w, route)


def by_heads(
    query_input,
    key_input,
    value_input,
    gate_logits,
    comp_weight,
    out_proj,
    residual_in,
    ffn_gain,
    expert_ids,
    route_gates,
    expert_gate,
    expert_up,
    expert_down,
):
    row_count = query_input.shape[0]
    head_count = comp_weight.shape[2]
    head_width = query_input.shape[1] // head_count
    block_len = comp_weight.shape[1]
    stride_len = block_len // 2
    ctx_count = lax.axis_size("ctx")
    exp_count = lax.axis_size("exp")
    ctx_index = lax.axis_index("ctx")
    exp_index = lax.axis_index("exp")
    own = head_count // ctx_count
    width = own * head_width
    share = row_count // exp_count
    half = share // 2
    seq_len = row_count * ctx_count
    cols = out_proj.shape[1]
    model_width = cols * ctx_count
    own_tokens = ctx_count * share

    experts = jnp.arange(exp_count, dtype=jnp.int32)
    table = jnp.sum(
        jnp.where(expert_ids[:, :, None] == experts, route_gates[:, :, None], 0.0), axis=1
    )
    table = jnp.broadcast_to(high_low(table).reshape(1, -1), (ctx_count, 2 * share * exp_count))
    gates = high_low(jax.nn.sigmoid(gate_logits)).reshape(2, 2, row_count, ctx_count, own)
    gates = jnp.transpose(gates, (3, 0, 1, 2, 4)).reshape(ctx_count, -1)
    side = jnp.concatenate([gates, table], 1)
    side_rows = -(-side.shape[1] // width)
    residual_rows = -(-share * cols // width)
    side_rows += -(3 * row_count + residual_rows + side_rows) % 16
    side = jnp.pad(side, ((0, 0), (0, side_rows * width - side.shape[1])))
    residual = jnp.transpose(residual_in.reshape(share, ctx_count, cols), (1, 0, 2))
    residual = residual.reshape(ctx_count, share * cols)
    residual = jnp.pad(residual, ((0, 0), (0, residual_rows * width - share * cols)))
    heads = [
        jnp.transpose(block.reshape(row_count, ctx_count, width), (1, 0, 2))
        for block in (query_input, key_input, value_input)
    ]
    packed = jnp.concatenate(
        heads
        + [
            residual.reshape(ctx_count, residual_rows, width),
            side.reshape(ctx_count, side_rows, width),
        ],
        1,
    )
    moved = lax.all_to_all(packed, "ctx", split_axis=0, concat_axis=0, tiled=True)
    residual = moved[:, 3 * row_count : 3 * row_count + residual_rows].reshape(ctx_count, -1)
    residual = residual[:, : share * cols].reshape(own_tokens, cols)
    side = moved[:, 3 * row_count + residual_rows :].reshape(ctx_count, -1).astype(jnp.float32)
    gate_size = 4 * row_count * own
    gates = side[:, :gate_size].reshape(ctx_count, 2, 2, row_count, own)
    gates = jnp.transpose(gates[:, 0] + gates[:, 1], (0, 2, 1, 3)).reshape(seq_len, 2 * own)
    table = side[:, gate_size : gate_size + 2 * share * exp_count]
    table = table.reshape(ctx_count, 2, share, exp_count)

    taps = lax.dynamic_slice_in_dim(comp_weight, ctx_index * own, own, 2)
    taps = jnp.transpose(taps.reshape(2, 2, stride_len, own), (0, 3, 1, 2))
    taps = jnp.tile(taps.reshape(4 * own, stride_len), (1, seq_len // stride_len))
    attended = attend(moved, taps, gates, row_count, share, block_len, head_width)

    spread_heads = lax.all_gather(attended, "ctx", axis=0)
    partial = jnp.einsum(
        "csk,ckd->sd",
        spread_heads,
        out_proj.reshape(ctx_count, width, cols),
        preferred_element_type=jnp.float32,
    ).astype(jnp.bfloat16)
    table = jnp.transpose(table, (3, 1, 0, 2)).reshape(exp_count, -1).astype(jnp.bfloat16)
    table_rows = -(-table.shape[1] // cols)
    table_rows += -table_rows % 16
    table = jnp.pad(table, ((0, 0), (0, table_rows * cols - table.shape[1])))
    pieces = jnp.concatenate(
        [
            partial.reshape(exp_count, own_tokens, cols),
            table.reshape(exp_count, table_rows, cols),
        ],
        1,
    )
    pieces = lax.all_to_all(pieces, "exp", split_axis=0, concat_axis=0, tiled=True)
    route = pieces[:, own_tokens:].reshape(exp_count, -1)[:, : 2 * own_tokens]
    route = jnp.sum(route.reshape(exp_count, 2, own_tokens).astype(jnp.float32), axis=1)
    hidden_state = residual.astype(jnp.float32) + jnp.sum(
        pieces[:, :own_tokens].astype(jnp.float32), axis=0
    )
    gain = lax.dynamic_slice_in_dim(ffn_gain, ctx_index * cols, cols, 0)
    scaled = (hidden_state * gain).astype(jnp.bfloat16)
    rows = lax.all_gather(scaled, ("ctx", "exp"), axis=0, tiled=True)
    active = run_expert(
        rows.reshape(ctx_count, seq_len, cols),
        ffn_gain,
        expert_gate[0],
        expert_up[0],
        route.reshape(seq_len, 1),
        exp_count,
        share,
    )
    hidden_state = hidden_state.reshape(ctx_count, share, cols)

    outs = jnp.dot(active[0], expert_down[0], preferred_element_type=jnp.float32)
    outs = outs.astype(jnp.bfloat16).reshape(ctx_count, exp_count, half, model_width)
    place = (0, exp_index, 0, ctx_index * cols)
    mine = lax.dynamic_slice(outs, place, (ctx_count, 1, half, cols)).astype(jnp.float32)
    mine = mine + hidden_state[:, None, :half]
    outs = lax.dynamic_update_slice(outs, mine.astype(jnp.bfloat16), place)
    first = lax.psum_scatter(
        outs.reshape(ctx_count, exp_count * half, model_width),
        "ctx",
        scatter_dimension=0,
        tiled=True,
    )
    first = lax.all_to_all(
        first.reshape(exp_count, half, model_width), "exp", split_axis=0, concat_axis=0, tiled=True
    )
    first = jnp.sum(first.astype(jnp.float32), axis=0).astype(jnp.bfloat16)

    outs = jnp.dot(active[1], expert_down[0], preferred_element_type=jnp.float32)
    outs = outs.astype(jnp.bfloat16).reshape(exp_count, ctx_count, half, model_width)
    place = (exp_index, 0, 0, ctx_index * cols)
    mine = lax.dynamic_slice(outs, place, (1, ctx_count, half, cols)).astype(jnp.float32)
    mine = mine + hidden_state[None, :, half:]
    outs = lax.dynamic_update_slice(outs, mine.astype(jnp.bfloat16), place)
    outs = lax.all_to_all(outs, "exp", split_axis=0, concat_axis=0, tiled=True)
    outs = jnp.sum(outs.astype(jnp.float32), axis=0).astype(jnp.bfloat16)
    second = lax.psum_scatter(outs, "ctx", scatter_dimension=0, tiled=True)
    return jnp.concatenate([first, second.reshape(half, model_width)], 0)


def local(*args):
    head_count = args[4].shape[2]
    share = args[0].shape[0] // lax.axis_size("exp")
    if head_count % lax.axis_size("ctx") == 0 and share % 32 == 0:
        return by_heads(*args)
    return general(*args)


def solution(mesh):
    in_specs = (
        P("ctx", "exp"),
        P("ctx", "exp"),
        P("ctx", "exp"),
        P(None, "ctx", "exp"),
        P(None, None, "exp"),
        P("exp", "ctx"),
        P(("ctx", "exp"), None),
        P(),
        P(("ctx", "exp"), None),
        P(("ctx", "exp"), None),
        P("exp", None, "ctx"),
        P("exp", None, "ctx"),
        P("exp", "ctx", None),
    )
    out_specs = P(("ctx", "exp"), None)
    return jax.shard_map(local, mesh=mesh, in_specs=in_specs, out_specs=out_specs, check_vma=False)
```

```python
import functools
import math

import jax
import jax.numpy as jnp
from jax import lax
from jax.experimental import pallas as pl
from jax.experimental.pallas import tpu as pltpu
from jax.sharding import PartitionSpec as P

WINDOW = 512


score_gain = 2.0
norm_eps = 1e-06


def passed_along(block, axis, distance):
    devices = range(lax.axis_size(axis))
    route = [(i - distance, i) for i in devices if i - distance in devices]
    return lax.ppermute(block, axis, route)


def head_norm(matrix, head_width):
    row_count = matrix.shape[0]
    shaped = matrix.reshape(row_count, -1, head_width).astype(jnp.float32)
    scaled = shaped * lax.rsqrt(jnp.mean(shaped * shaped, axis=2, keepdims=True) + norm_eps)
    return scaled.reshape(row_count, -1)


def compress(extended, position_weights, head_width):
    stride_len = position_weights.shape[0] // 2
    head_count = position_weights.shape[1]
    blocks = extended.reshape(-1, stride_len, head_count, head_width).astype(jnp.float32)
    first_half = jnp.einsum(
        "nshd,sh->nhd", blocks[:-1], position_weights[:stride_len], precision=lax.Precision.HIGHEST
    )
    second_half = jnp.einsum(
        "nshd,sh->nhd", blocks[1:], position_weights[stride_len:], precision=lax.Precision.HIGHEST
    )
    return (first_half + second_half).reshape(blocks.shape[0] - 1, head_count * head_width)


def window_attention(query_input, key_input, value_input, gate_logits, comp_weight):
    row_count = query_input.shape[0]
    head_count = comp_weight.shape[2]
    head_width = query_input.shape[1] // head_count
    block_len = comp_weight.shape[1]
    stride_len = block_len // 2
    exp_count = lax.axis_size("exp")
    ctx_index = lax.axis_index("ctx")
    scale = score_gain / math.sqrt(head_width)
    query_norm = head_norm(query_input, head_width).astype(jnp.bfloat16)
    key_norm = head_norm(key_input, head_width).astype(jnp.bfloat16)
    next_keys, next_values = passed_along(
        (key_input[:stride_len], value_input[:stride_len]), "ctx", -1
    )
    comp_keys = head_norm(
        compress(jnp.concatenate([key_input, next_keys], 0), comp_weight[0], head_width), head_width
    ).astype(jnp.bfloat16)
    comp_values = compress(
        jnp.concatenate([value_input, next_values], 0), comp_weight[1], head_width
    ).astype(jnp.bfloat16)
    query_pos = ctx_index * row_count + jnp.arange(row_count, dtype=jnp.int32)
    query_heads = query_norm.reshape(row_count, head_count, head_width)
    part_keys = lax.all_gather(comp_keys, "ctx", axis=0, tiled=True)
    part_values = lax.all_gather(comp_values, "ctx", axis=0, tiled=True)
    part_count = part_keys.shape[0]
    scores = jnp.einsum(
        "thd,nhd->htn",
        query_heads,
        part_keys.reshape(part_count, head_count, head_width),
        preferred_element_type=jnp.float32,
    )
    block_end = jnp.arange(part_count, dtype=jnp.int32) * stride_len + block_len - 1
    visible = block_end[None, :] <= query_pos[:, None]
    weights = jnp.where(visible[None], jnp.exp(scale * scores), 0.0)
    running_total = jnp.sum(weights, axis=2).T
    collected = jnp.einsum(
        "htn,nhd->thd",
        weights.astype(jnp.bfloat16),
        part_values.reshape(part_count, head_count, head_width),
        preferred_element_type=jnp.float32,
    )
    cmp_sum = collected.reshape(row_count, -1)
    no_block = (query_pos < block_len - 1).astype(jnp.float32)
    cmp_out = (
        cmp_sum.reshape(row_count, head_count, head_width)
        / (running_total + no_block[:, None])[:, :, None]
    )
    shift_count = max(1, WINDOW // row_count)
    earlier_keys = []
    earlier_values = []
    for distance in range(shift_count, 0, -1):
        moved_keys, moved_values = passed_along((key_norm, value_input), "ctx", distance)
        earlier_keys.append(moved_keys)
        earlier_values.append(moved_values)
    near_keys = jnp.concatenate(earlier_keys + [key_norm], 0)
    near_values = jnp.concatenate(earlier_values + [value_input], 0)
    key_pos = ctx_index * row_count - WINDOW + jnp.arange(near_keys.shape[0], dtype=jnp.int32)
    near_scores = jnp.einsum(
        "thd,shd->hts",
        query_heads,
        near_keys.reshape(-1, head_count, head_width),
        preferred_element_type=jnp.float32,
    )
    inside = (
        (key_pos[None, :] <= query_pos[:, None])
        & (key_pos[None, :] > query_pos[:, None] - WINDOW)
        & (key_pos[None, :] >= 0)
    )
    near_weights = jnp.where(inside[None], jnp.exp(scale * near_scores), 0.0)
    win_total = jnp.sum(near_weights, axis=2).T
    win_sum = jnp.einsum(
        "hts,shd->thd",
        near_weights.astype(jnp.bfloat16),
        near_values.reshape(-1, head_count, head_width),
        preferred_element_type=jnp.float32,
    )
    win_out = win_sum / win_total[:, :, None]
    branch_gates = jax.nn.sigmoid(gate_logits)
    attended = (
        (branch_gates[0][:, :, None] * cmp_out + branch_gates[1][:, :, None] * win_out)
        .reshape(row_count, -1)
        .astype(jnp.bfloat16)
    )
    return attended


def general(
    query_input,
    key_input,
    value_input,
    gate_logits,
    comp_weight,
    out_proj,
    residual_in,
    ffn_gain,
    expert_ids,
    route_gates,
    expert_gate,
    expert_up,
    expert_down,
):
    row_count = query_input.shape[0]
    ctx_count = lax.axis_size("ctx")
    exp_count = lax.axis_size("exp")
    ctx_index = lax.axis_index("ctx")
    exp_index = lax.axis_index("exp")
    share = row_count // exp_count
    seq_len = row_count * ctx_count
    cols = out_proj.shape[1]
    model_width = cols * ctx_count
    hidden_units = expert_gate.shape[2]
    own_tokens = ctx_count * share

    experts = jnp.arange(exp_count, dtype=jnp.int32)
    route_table = jnp.sum(
        jnp.where(expert_ids[:, :, None] == experts, route_gates[:, :, None], 0.0), axis=1
    )
    route_all = lax.all_gather(route_table, ("ctx", "exp"), axis=0, tiled=True)
    route_own = lax.dynamic_slice_in_dim(route_all, exp_index, 1, 1)
    residual = lax.all_to_all(residual_in, "ctx", split_axis=1, concat_axis=0, tiled=True)

    attention_args = (query_input, key_input, value_input, gate_logits, comp_weight)
    attended = window_attention(*attention_args)
    spread_rows = lax.all_gather(
        attended.reshape(1, exp_count, share, -1), "ctx", axis=0, tiled=True
    )
    partial = jnp.einsum(
        "cerh,hd->ecrd", spread_rows, out_proj, preferred_element_type=jnp.float32
    )
    pieces = lax.all_to_all(
        partial.astype(jnp.bfloat16).reshape(exp_count, own_tokens, cols),
        "exp",
        split_axis=0,
        concat_axis=0,
        tiled=True,
    )
    hidden_state = residual.reshape(own_tokens, cols).astype(jnp.float32) + jnp.sum(
        pieces.astype(jnp.float32), axis=0
    )
    gain = lax.dynamic_slice_in_dim(ffn_gain, ctx_index * cols, cols, 0)
    scaled = (hidden_state * gain).astype(jnp.bfloat16)
    squares = jnp.sum(hidden_state * hidden_state, axis=1)
    rows = lax.all_gather(scaled, ("ctx", "exp"), axis=0, tiled=True)
    rows = rows.reshape(ctx_count, seq_len, cols)
    squares = lax.all_gather(squares, ("ctx", "exp"), axis=0, tiled=True)
    mean_square = jnp.sum(squares.reshape(ctx_count, seq_len), axis=0) / model_width
    inverse = lax.rsqrt(mean_square + norm_eps)[:, None]

    gate_part = inverse * jnp.einsum(
        "ctk,ckf->tf",
        rows,
        expert_gate.reshape(ctx_count, cols, hidden_units),
        preferred_element_type=jnp.float32,
    )
    up_part = inverse * jnp.einsum(
        "ctk,ckf->tf",
        rows,
        expert_up.reshape(ctx_count, cols, hidden_units),
        preferred_element_type=jnp.float32,
    )
    activated = (jax.nn.silu(gate_part) * up_part).astype(jnp.bfloat16)
    activated = jnp.transpose(
        activated.reshape(exp_count, ctx_count, share, hidden_units), (1, 0, 2, 3)
    ).reshape(seq_len, hidden_units)
    outs = jnp.dot(activated, expert_down[0], preferred_element_type=jnp.float32)
    outs = (outs * route_own).astype(jnp.bfloat16)
    outs = outs.reshape(ctx_count, exp_count, share, model_width)
    place = (0, exp_index, 0, ctx_index * cols)
    mine = lax.dynamic_slice(outs, place, (ctx_count, 1, share, cols))
    mine = mine.astype(jnp.float32) + hidden_state.reshape(ctx_count, 1, share, cols)
    outs = lax.dynamic_update_slice(outs, mine.astype(jnp.bfloat16), place)
    return lax.psum_scatter(
        outs.reshape(seq_len, model_width), ("ctx", "exp"), scatter_dimension=0, tiled=True
    )


def high_low(values):
    high = lax.reduce_precision(values, 8, 7)
    return jnp.stack([high, values - high], 0).astype(jnp.bfloat16)


def unit_rows(block):
    return block * lax.rsqrt(jnp.mean(block * block, axis=1, keepdims=True) + norm_eps)


def attend_kernel(row_count, share, block_len, head_width, moved, taps, gates, out, keys, values):
    ctx_count = moved.shape[0]
    own = moved.shape[2] // head_width
    seq_len = row_count * ctx_count
    stride_len = block_len // 2
    part_count = seq_len // stride_len
    scale = score_gain / math.sqrt(head_width)

    def dot(left, right):
        return jnp.dot(left, right, preferred_element_type=jnp.float32)

    def dot_rows(left, right):
        return lax.dot_general(
            left, right, (((1,), (1,)), ((), ())), preferred_element_type=jnp.float32
        )

    def compressed(row, block):
        group = lax.broadcasted_iota(jnp.int32, (part_count, seq_len), 0)
        token_group = lax.broadcasted_iota(jnp.int32, (part_count, seq_len), 1) // stride_len
        band = jnp.where(token_group == group, taps[row : row + 1, :], 0.0)
        band = jnp.where(token_group == group + 1, taps[row + 1 : row + 2, :], band)
        high = band.astype(jnp.bfloat16)
        low = (band - high.astype(jnp.float32)).astype(jnp.bfloat16)
        return dot(high, block) + dot(low, block)

    for head in range(own):
        lanes = slice(head * head_width, (head + 1) * head_width)
        raw_keys = moved[:, row_count : 2 * row_count, lanes].reshape(seq_len, head_width)
        keys[...] = unit_rows(raw_keys.astype(jnp.float32)).astype(jnp.bfloat16)
        raw_values = moved[:, 2 * row_count : 3 * row_count, lanes].reshape(seq_len, head_width)
        values[...] = raw_values
        comp_keys = unit_rows(compressed(2 * head, raw_keys)).astype(jnp.bfloat16)
        comp_values = compressed(2 * (own + head), raw_values).astype(jnp.bfloat16)
        for block in range(ctx_count):
            query = moved[block, 0:row_count, lanes].astype(jnp.float32)
            query = unit_rows(query).astype(jnp.bfloat16)
            base = block * row_count
            rows = slice(base, base + row_count)
            spot = base + lax.broadcasted_iota(jnp.int32, (row_count, part_count), 0)
            ends = lax.broadcasted_iota(jnp.int32, (row_count, part_count), 1) * stride_len
            seen = ends + (block_len - 1) <= spot
            weight = jnp.where(seen, jnp.exp(scale * dot_rows(query, comp_keys)), 0.0)
            total = jnp.sum(weight, axis=1, keepdims=True)
            total = total + jnp.where(spot[:, :1] < block_len - 1, 1.0, 0.0)
            far = dot(weight.astype(jnp.bfloat16), comp_values) / total
            start = max(0, base - WINDOW)
            reach = base + row_count - start
            spot = base + lax.broadcasted_iota(jnp.int32, (row_count, reach), 0)
            key_spot = start + lax.broadcasted_iota(jnp.int32, (row_count, reach), 1)
            seen = (key_spot <= spot) & (key_spot > spot - WINDOW)
            score = dot_rows(query, keys[start : start + reach, :])
            weight = jnp.where(seen, jnp.exp(scale * score), 0.0)
            total = jnp.sum(weight, axis=1, keepdims=True)
            near = dot(weight.astype(jnp.bfloat16), values[start : start + reach, :]) / total
            mixed = (
                gates[rows, head : head + 1] * far
                + gates[rows, own + head : own + head + 1] * near
            ).astype(jnp.bfloat16)
            for part in range(row_count // share):
                target = (part * ctx_count + block) * share
                out[target : target + share, lanes] = mixed[part * share : (part + 1) * share]


def attend(moved, taps, gates, row_count, share, block_len, head_width):
    seq_len = moved.shape[0] * row_count
    width = moved.shape[2]
    return pl.pallas_call(
        functools.partial(attend_kernel, row_count, share, block_len, head_width),
        out_shape=jax.ShapeDtypeStruct((seq_len, width), jnp.bfloat16),
        scratch_shapes=[
            pltpu.VMEM((seq_len, head_width), jnp.bfloat16),
            pltpu.VMEM((seq_len, head_width), jnp.bfloat16),
        ],
        compiler_params=pltpu.CompilerParams(vmem_limit_bytes=48 * 2**20),
        name="attend",
    )(moved, taps, gates)


def expert_kernel(exp_count, share, rows, gain, gate_w, up_w, gate_v, up_v, route, out, total, squares):
    step = pl.program_id(0)

    @pl.when(step == 0)
    def _():
        total[...] = jnp.zeros_like(total)
        squares[...] = jnp.zeros_like(squares)

    block = rows[0]
    for spot, weight in enumerate((gate_w, up_w, gate_v, up_v)):
        total[spot] += jnp.dot(block, weight[...], preferred_element_type=jnp.float32)
    lane = squares.shape[1]
    collected = squares[...]
    for part in range(block.shape[1] // lane):
        lanes = slice(part * lane, (part + 1) * lane)
        plain = block[:, lanes].astype(jnp.float32) * (1.0 / gain[0, :, lanes])
        collected = collected + plain * plain
    squares[...] = collected

    @pl.when(step == pl.num_programs(0) - 1)
    def _():
        model_width = pl.num_programs(0) * block.shape[1]
        mean_square = jnp.sum(squares[...], axis=1, keepdims=True) / model_width
        inverse = lax.rsqrt(mean_square + norm_eps)
        half = share // 2
        chip_count = block.shape[0] // (exp_count * share)
        for core in range(2):
            gate_part = total[2 * core] * inverse
            up_part = total[2 * core + 1] * inverse
            active = gate_part / (1.0 + jnp.exp(-gate_part)) * up_part * route[...]
            active = active.astype(jnp.bfloat16)
            for exp_spot in range(exp_count):
                for chip in range(chip_count):
                    base = (exp_spot * chip_count + chip) * share
                    target = (chip * exp_count + exp_spot) * half
                    out[0, core, target : target + half, :] = active[base : base + half]
                    target = (exp_spot * chip_count + chip) * half
                    out[1, core, target : target + half, :] = active[base + half : base + share]


def run_expert(rows, gain, weights, route, exp_count, share):
    chip_count, row_total, wide = rows.shape
    cols = wide // 2
    steps = 2 * chip_count
    units = weights[0].shape[1]
    lane = math.gcd(128, cols)
    by_cols = pl.BlockSpec((cols, units), lambda i: (i, 0))
    return pl.pallas_call(
        functools.partial(expert_kernel, exp_count, share),
        grid=(steps,),
        in_specs=[
            pl.BlockSpec((1, row_total, cols), lambda i: (i // 2, 0, i % 2)),
            pl.BlockSpec((1, 1, cols), lambda i: (i, 0, 0)),
            by_cols,
            by_cols,
            by_cols,
            by_cols,
            pl.BlockSpec((row_total, 1), lambda i: (0, 0)),
        ],
        out_specs=pl.BlockSpec((2, 2, row_total // 2, units), lambda i: (0, 0, 0, 0)),
        out_shape=jax.ShapeDtypeStruct((2, 2, row_total // 2, units), jnp.bfloat16),
        scratch_shapes=[
            pltpu.VMEM((4, row_total, units), jnp.float32),
            pltpu.VMEM((row_total, lane), jnp.float32),
        ],
        compiler_params=pltpu.CompilerParams(vmem_limit_bytes=48 * 2**20),
        cost_estimate=pl.CostEstimate(
            flops=8 * row_total * units * steps * cols,
            bytes_accessed=2 * steps * cols * (row_total + 4 * units),
            transcendentals=2 * row_total * units,
        ),
        name="expert",
    )(rows, gain.reshape(steps, 1, cols), *weights, route)


def down_kernel(exp_dim, spots, active, down_w, down_v, hidden, out):
    step = pl.program_id(0)
    sums = jnp.dot(active[0], down_w[...], preferred_element_type=jnp.float32)
    sums += jnp.dot(active[1], down_v[...], preferred_element_type=jnp.float32)
    out[...] = sums.astype(out.dtype).reshape(out.shape)

    @pl.when(step // 2 == spots[0])
    def _():
        spot = pl.ds(spots[1], 1)
        place = (spot,) if exp_dim == 0 else (slice(None), spot)
        piece = out[place].astype(jnp.float32)
        out[place] = (piece + hidden[...].reshape(piece.shape)).astype(out.dtype)


def run_down(spots, active, down_w, down_v, hidden, exp_count, exp_dim):
    units, model_width = down_w.shape
    chip_count, half, wide = hidden.shape
    cols = wide // 2
    lead = (exp_count, chip_count) if exp_dim == 0 else (chip_count, exp_count)
    by_cols = pl.BlockSpec((units, cols), lambda i, _: (0, i))
    rows = active.shape[1]
    return pl.pallas_call(
        functools.partial(down_kernel, exp_dim),
        grid_spec=pltpu.PrefetchScalarGridSpec(
            num_scalar_prefetch=1,
            grid=(model_width // cols,),
            in_specs=[
                pl.BlockSpec((2, rows, units), lambda i, _: (0, 0, 0)),
                by_cols,
                by_cols,
                pl.BlockSpec((chip_count, half, cols), lambda i, _: (0, 0, i % 2)),
            ],
            out_specs=pl.BlockSpec(lead + (half, cols), lambda i, _: (0, 0, 0, i)),
        ),
        out_shape=jax.ShapeDtypeStruct(lead + (half, model_width), jnp.bfloat16),
        compiler_params=pltpu.CompilerParams(vmem_limit_bytes=48 * 2**20),
        cost_estimate=pl.CostEstimate(
            flops=4 * rows * units * model_width,
            bytes_accessed=2 * model_width * (rows + 2 * units),
            transcendentals=0,
        ),
        name="down",
    )(spots, active, down_w, down_v, hidden)


def sibling(block):
    return lax.ppermute(block, "core", [(0, 1), (1, 0)])


def by_heads(
    query_input,
    key_input,
    value_input,
    gate_logits,
    comp_weight,
    out_proj,
    residual_in,
    ffn_gain,
    expert_ids,
    route_gates,
    expert_gate,
    expert_up,
    expert_down,
):
    row_count = query_input.shape[0]
    head_count = comp_weight.shape[2]
    head_width = query_input.shape[1] // head_count
    block_len = comp_weight.shape[1]
    stride_len = block_len // 2
    ctx = ("z", "core")
    chip_count = lax.axis_size("z")
    ctx_count = chip_count * lax.axis_size("core")
    exp_count = lax.axis_size("exp")
    chip_index = lax.axis_index("z")
    core_index = lax.axis_index("core")
    ctx_index = 2 * chip_index + core_index
    exp_index = lax.axis_index("exp")
    own = head_count // ctx_count
    width = own * head_width
    share = row_count // exp_count
    half = share // 2
    seq_len = row_count * ctx_count
    cols = out_proj.shape[1]
    model_width = cols * ctx_count
    own_tokens = ctx_count * share

    other_gate = sibling(expert_gate[0])
    other_up = sibling(expert_up[0])
    other_down = sibling(expert_down[0])

    experts = jnp.arange(exp_count, dtype=jnp.int32)
    table = jnp.sum(
        jnp.where(expert_ids[:, :, None] == experts, route_gates[:, :, None], 0.0), axis=1
    )
    table = jnp.broadcast_to(high_low(table).reshape(1, -1), (ctx_count, 2 * share * exp_count))
    gates = high_low(jax.nn.sigmoid(gate_logits)).reshape(2, 2, row_count, ctx_count, own)
    gates = jnp.transpose(gates, (3, 0, 1, 2, 4)).reshape(ctx_count, -1)
    side = jnp.concatenate([gates, table], 1)
    side_rows = -(-side.shape[1] // width)
    residual_rows = -(-share * cols // width)
    side_rows += -(3 * row_count + residual_rows + side_rows) % 16
    side = jnp.pad(side, ((0, 0), (0, side_rows * width - side.shape[1])))
    residual = jnp.transpose(residual_in.reshape(share, ctx_count, cols), (1, 0, 2))
    residual = residual.reshape(ctx_count, share * cols)
    residual = jnp.pad(residual, ((0, 0), (0, residual_rows * width - share * cols)))
    heads = [
        jnp.transpose(block.reshape(row_count, ctx_count, width), (1, 0, 2))
        for block in (query_input, key_input, value_input)
    ]
    packed = jnp.concatenate(
        heads
        + [
            residual.reshape(ctx_count, residual_rows, width),
            side.reshape(ctx_count, side_rows, width),
        ],
        1,
    )
    moved = lax.all_to_all(packed, ctx, split_axis=0, concat_axis=0, tiled=True)
    residual = moved[:, 3 * row_count : 3 * row_count + residual_rows].reshape(ctx_count, -1)
    residual = residual[:, : share * cols].reshape(own_tokens, cols)
    side = moved[:, 3 * row_count + residual_rows :].reshape(ctx_count, -1).astype(jnp.float32)
    gate_size = 4 * row_count * own
    gates = side[:, :gate_size].reshape(ctx_count, 2, 2, row_count, own)
    gates = jnp.transpose(gates[:, 0] + gates[:, 1], (0, 2, 1, 3)).reshape(seq_len, 2 * own)
    table = side[:, gate_size : gate_size + 2 * share * exp_count]
    table = table.reshape(chip_count, 2, 2, share, exp_count)
    table = lax.dynamic_index_in_dim(table, core_index, 1, keepdims=False)

    taps = lax.dynamic_slice_in_dim(comp_weight, ctx_index * own, own, 2)
    taps = jnp.transpose(taps.reshape(2, 2, stride_len, own), (0, 3, 1, 2))
    taps = jnp.tile(taps.reshape(4 * own, stride_len), (1, seq_len // stride_len))
    attended = attend(moved, taps, gates, row_count, share, block_len, head_width)

    spread_heads = lax.all_gather(attended, ctx, axis=0)
    partial = jnp.einsum(
        "csk,ckd->sd",
        spread_heads,
        out_proj.reshape(ctx_count, width, cols),
        preferred_element_type=jnp.float32,
    ).astype(jnp.bfloat16)
    table = jnp.transpose(table, (3, 1, 0, 2)).reshape(exp_count, -1).astype(jnp.bfloat16)
    table_rows = -(-table.shape[1] // cols)
    table_rows += -table_rows % 16
    table = jnp.pad(table, ((0, 0), (0, table_rows * cols - table.shape[1])))
    pieces = jnp.concatenate(
        [
            partial.reshape(exp_count, own_tokens, cols),
            table.reshape(exp_count, table_rows, cols),
        ],
        1,
    )
    pieces = lax.all_to_all(pieces, "exp", split_axis=0, concat_axis=0, tiled=True)
    chip_tokens = chip_count * share
    route = pieces[:, own_tokens:].reshape(exp_count, -1)[:, : 2 * chip_tokens]
    route = jnp.sum(route.reshape(exp_count, 2, chip_tokens).astype(jnp.float32), axis=1)
    hidden_state = residual.astype(jnp.float32) + jnp.sum(
        pieces[:, :own_tokens].astype(jnp.float32), axis=0
    )
    hidden_state = hidden_state.reshape(chip_count, 2, share, cols)
    kept = lax.dynamic_index_in_dim(hidden_state, core_index, 1, keepdims=False)
    given = lax.dynamic_index_in_dim(hidden_state, 1 - core_index, 1, keepdims=False)
    given = sibling(given)
    hidden_state = jnp.concatenate(
        [jnp.where(core_index == 0, kept, given), jnp.where(core_index == 0, given, kept)], 2
    )
    gain = lax.dynamic_slice_in_dim(ffn_gain, chip_index * 2 * cols, 2 * cols, 0)
    scaled = (hidden_state * gain).astype(jnp.bfloat16).reshape(chip_tokens, 2 * cols)
    rows = lax.all_gather(scaled, ("z", "exp"), axis=0, tiled=True)
    active = run_expert(
        rows.reshape(chip_count, exp_count * chip_tokens, 2 * cols),
        ffn_gain,
        (expert_gate[0], expert_up[0], other_gate, other_up),
        route.reshape(exp_count * chip_tokens, 1),
        exp_count,
        share,
    )
    spots = jnp.stack([chip_index, exp_index]).astype(jnp.int32)

    outs = run_down(
        spots, active[0], expert_down[0], other_down, hidden_state[:, :half], exp_count, 1
    )
    first = lax.psum_scatter(
        outs.reshape(chip_count, exp_count * half, model_width),
        "z",
        scatter_dimension=0,
        tiled=True,
    )
    first = lax.all_to_all(
        first.reshape(exp_count, half, model_width), "exp", split_axis=0, concat_axis=0, tiled=True
    )
    first = jnp.sum(first.astype(jnp.float32), axis=0).astype(jnp.bfloat16)

    outs = run_down(
        spots, active[1], expert_down[0], other_down, hidden_state[:, half:], exp_count, 0
    )
    outs = lax.all_to_all(outs, "exp", split_axis=0, concat_axis=0, tiled=True)
    outs = jnp.sum(outs.astype(jnp.float32), axis=0).astype(jnp.bfloat16)
    second = lax.psum_scatter(outs, "z", scatter_dimension=0, tiled=True)
    return jnp.concatenate([first, second.reshape(half, model_width)], 0)


def specs(ctx):
    in_specs = (
        P(ctx, "exp"),
        P(ctx, "exp"),
        P(ctx, "exp"),
        P(None, ctx, "exp"),
        P(None, None, "exp"),
        P("exp", ctx),
        P((*ctx, "exp"), None),
        P(),
        P((*ctx, "exp"), None),
        P((*ctx, "exp"), None),
        P("exp", None, ctx),
        P("exp", None, ctx),
        P("exp", ctx, None),
    )
    return in_specs, P((*ctx, "exp"), None)


def solution(mesh):
    ctx_count, exp_count = mesh.shape["ctx"], mesh.shape["exp"]

    def run(*args):
        head_count = args[4].shape[2] // exp_count
        share = args[0].shape[0] // (ctx_count * exp_count)
        body, axes, where = general, ("ctx",), mesh
        if head_count % ctx_count == 0 and share % 32 == 0 and ctx_count % 2 == 0:
            split = mesh.devices.reshape(ctx_count // 2, 2, exp_count)
            where = jax.sharding.Mesh(split, ("z", "core", "exp"))
            body, axes = by_heads, ("z", "core")
        in_specs, out_specs = specs(axes)
        return jax.shard_map(
            body, mesh=where, in_specs=in_specs, out_specs=out_specs, check_vma=False
        )(*args)

    return run
```

```python
import functools
import math

import jax
import jax.numpy as jnp
from jax import lax
from jax.experimental import pallas as pl
from jax.experimental.pallas import tpu as pltpu
from jax.sharding import PartitionSpec as P

WINDOW = 512


score_gain = 2.0
norm_eps = 1e-06


def passed_along(block, axis, distance):
    devices = range(lax.axis_size(axis))
    route = [(i - distance, i) for i in devices if i - distance in devices]
    return lax.ppermute(block, axis, route)


def head_norm(matrix, head_width):
    row_count = matrix.shape[0]
    shaped = matrix.reshape(row_count, -1, head_width).astype(jnp.float32)
    scaled = shaped * lax.rsqrt(jnp.mean(shaped * shaped, axis=2, keepdims=True) + norm_eps)
    return scaled.reshape(row_count, -1)


def compress(extended, position_weights, head_width):
    stride_len = position_weights.shape[0] // 2
    head_count = position_weights.shape[1]
    blocks = extended.reshape(-1, stride_len, head_count, head_width).astype(jnp.float32)
    first_half = jnp.einsum(
        "nshd,sh->nhd", blocks[:-1], position_weights[:stride_len], precision=lax.Precision.HIGHEST
    )
    second_half = jnp.einsum(
        "nshd,sh->nhd", blocks[1:], position_weights[stride_len:], precision=lax.Precision.HIGHEST
    )
    return (first_half + second_half).reshape(blocks.shape[0] - 1, head_count * head_width)


def window_attention(query_input, key_input, value_input, gate_logits, comp_weight):
    row_count = query_input.shape[0]
    head_count = comp_weight.shape[2]
    head_width = query_input.shape[1] // head_count
    block_len = comp_weight.shape[1]
    stride_len = block_len // 2
    exp_count = lax.axis_size("exp")
    ctx_index = lax.axis_index("ctx")
    scale = score_gain / math.sqrt(head_width)
    query_norm = head_norm(query_input, head_width).astype(jnp.bfloat16)
    key_norm = head_norm(key_input, head_width).astype(jnp.bfloat16)
    next_keys, next_values = passed_along(
        (key_input[:stride_len], value_input[:stride_len]), "ctx", -1
    )
    comp_keys = head_norm(
        compress(jnp.concatenate([key_input, next_keys], 0), comp_weight[0], head_width), head_width
    ).astype(jnp.bfloat16)
    comp_values = compress(
        jnp.concatenate([value_input, next_values], 0), comp_weight[1], head_width
    ).astype(jnp.bfloat16)
    query_pos = ctx_index * row_count + jnp.arange(row_count, dtype=jnp.int32)
    query_heads = query_norm.reshape(row_count, head_count, head_width)
    part_keys = lax.all_gather(comp_keys, "ctx", axis=0, tiled=True)
    part_values = lax.all_gather(comp_values, "ctx", axis=0, tiled=True)
    part_count = part_keys.shape[0]
    scores = jnp.einsum(
        "thd,nhd->htn",
        query_heads,
        part_keys.reshape(part_count, head_count, head_width),
        preferred_element_type=jnp.float32,
    )
    block_end = jnp.arange(part_count, dtype=jnp.int32) * stride_len + block_len - 1
    visible = block_end[None, :] <= query_pos[:, None]
    weights = jnp.where(visible[None], jnp.exp(scale * scores), 0.0)
    running_total = jnp.sum(weights, axis=2).T
    collected = jnp.einsum(
        "htn,nhd->thd",
        weights.astype(jnp.bfloat16),
        part_values.reshape(part_count, head_count, head_width),
        preferred_element_type=jnp.float32,
    )
    cmp_sum = collected.reshape(row_count, -1)
    no_block = (query_pos < block_len - 1).astype(jnp.float32)
    cmp_out = (
        cmp_sum.reshape(row_count, head_count, head_width)
        / (running_total + no_block[:, None])[:, :, None]
    )
    shift_count = max(1, WINDOW // row_count)
    earlier_keys = []
    earlier_values = []
    for distance in range(shift_count, 0, -1):
        moved_keys, moved_values = passed_along((key_norm, value_input), "ctx", distance)
        earlier_keys.append(moved_keys)
        earlier_values.append(moved_values)
    near_keys = jnp.concatenate(earlier_keys + [key_norm], 0)
    near_values = jnp.concatenate(earlier_values + [value_input], 0)
    key_pos = ctx_index * row_count - WINDOW + jnp.arange(near_keys.shape[0], dtype=jnp.int32)
    near_scores = jnp.einsum(
        "thd,shd->hts",
        query_heads,
        near_keys.reshape(-1, head_count, head_width),
        preferred_element_type=jnp.float32,
    )
    inside = (
        (key_pos[None, :] <= query_pos[:, None])
        & (key_pos[None, :] > query_pos[:, None] - WINDOW)
        & (key_pos[None, :] >= 0)
    )
    near_weights = jnp.where(inside[None], jnp.exp(scale * near_scores), 0.0)
    win_total = jnp.sum(near_weights, axis=2).T
    win_sum = jnp.einsum(
        "hts,shd->thd",
        near_weights.astype(jnp.bfloat16),
        near_values.reshape(-1, head_count, head_width),
        preferred_element_type=jnp.float32,
    )
    win_out = win_sum / win_total[:, :, None]
    branch_gates = jax.nn.sigmoid(gate_logits)
    attended = (
        (branch_gates[0][:, :, None] * cmp_out + branch_gates[1][:, :, None] * win_out)
        .reshape(row_count, -1)
        .astype(jnp.bfloat16)
    )
    return attended


def general(
    query_input,
    key_input,
    value_input,
    gate_logits,
    comp_weight,
    out_proj,
    residual_in,
    ffn_gain,
    expert_ids,
    route_gates,
    expert_gate,
    expert_up,
    expert_down,
):
    row_count = query_input.shape[0]
    ctx_count = lax.axis_size("ctx")
    exp_count = lax.axis_size("exp")
    ctx_index = lax.axis_index("ctx")
    exp_index = lax.axis_index("exp")
    share = row_count // exp_count
    seq_len = row_count * ctx_count
    cols = out_proj.shape[1]
    model_width = cols * ctx_count
    hidden_units = expert_gate.shape[2]
    own_tokens = ctx_count * share

    experts = jnp.arange(exp_count, dtype=jnp.int32)
    route_table = jnp.sum(
        jnp.where(expert_ids[:, :, None] == experts, route_gates[:, :, None], 0.0), axis=1
    )
    route_all = lax.all_gather(route_table, ("ctx", "exp"), axis=0, tiled=True)
    route_own = lax.dynamic_slice_in_dim(route_all, exp_index, 1, 1)
    residual = lax.all_to_all(residual_in, "ctx", split_axis=1, concat_axis=0, tiled=True)

    attention_args = (query_input, key_input, value_input, gate_logits, comp_weight)
    attended = window_attention(*attention_args)
    spread_rows = lax.all_gather(
        attended.reshape(1, exp_count, share, -1), "ctx", axis=0, tiled=True
    )
    partial = jnp.einsum(
        "cerh,hd->ecrd", spread_rows, out_proj, preferred_element_type=jnp.float32
    )
    pieces = lax.all_to_all(
        partial.astype(jnp.bfloat16).reshape(exp_count, own_tokens, cols),
        "exp",
        split_axis=0,
        concat_axis=0,
        tiled=True,
    )
    hidden_state = residual.reshape(own_tokens, cols).astype(jnp.float32) + jnp.sum(
        pieces.astype(jnp.float32), axis=0
    )
    gain = lax.dynamic_slice_in_dim(ffn_gain, ctx_index * cols, cols, 0)
    scaled = (hidden_state * gain).astype(jnp.bfloat16)
    squares = jnp.sum(hidden_state * hidden_state, axis=1)
    rows = lax.all_gather(scaled, ("ctx", "exp"), axis=0, tiled=True)
    rows = rows.reshape(ctx_count, seq_len, cols)
    squares = lax.all_gather(squares, ("ctx", "exp"), axis=0, tiled=True)
    mean_square = jnp.sum(squares.reshape(ctx_count, seq_len), axis=0) / model_width
    inverse = lax.rsqrt(mean_square + norm_eps)[:, None]

    gate_part = inverse * jnp.einsum(
        "ctk,ckf->tf",
        rows,
        expert_gate.reshape(ctx_count, cols, hidden_units),
        preferred_element_type=jnp.float32,
    )
    up_part = inverse * jnp.einsum(
        "ctk,ckf->tf",
        rows,
        expert_up.reshape(ctx_count, cols, hidden_units),
        preferred_element_type=jnp.float32,
    )
    activated = (jax.nn.silu(gate_part) * up_part).astype(jnp.bfloat16)
    activated = jnp.transpose(
        activated.reshape(exp_count, ctx_count, share, hidden_units), (1, 0, 2, 3)
    ).reshape(seq_len, hidden_units)
    outs = jnp.dot(activated, expert_down[0], preferred_element_type=jnp.float32)
    outs = (outs * route_own).astype(jnp.bfloat16)
    outs = outs.reshape(ctx_count, exp_count, share, model_width)
    place = (0, exp_index, 0, ctx_index * cols)
    mine = lax.dynamic_slice(outs, place, (ctx_count, 1, share, cols))
    mine = mine.astype(jnp.float32) + hidden_state.reshape(ctx_count, 1, share, cols)
    outs = lax.dynamic_update_slice(outs, mine.astype(jnp.bfloat16), place)
    return lax.psum_scatter(
        outs.reshape(seq_len, model_width), ("ctx", "exp"), scatter_dimension=0, tiled=True
    )


def high_low(values):
    high = lax.reduce_precision(values, 8, 7)
    return jnp.stack([high, values - high], 0).astype(jnp.bfloat16)


def unit_rows(block):
    return block * lax.rsqrt(jnp.mean(block * block, axis=1, keepdims=True) + norm_eps)


def attend_kernel(row_count, share, block_len, head_width, moved, taps, gates, out, keys, values):
    ctx_count = moved.shape[0]
    own = moved.shape[2] // head_width
    seq_len = row_count * ctx_count
    stride_len = block_len // 2
    part_count = seq_len // stride_len
    scale = score_gain / math.sqrt(head_width)

    def dot(left, right):
        return jnp.dot(left, right, preferred_element_type=jnp.float32)

    def dot_rows(left, right):
        return lax.dot_general(
            left, right, (((1,), (1,)), ((), ())), preferred_element_type=jnp.float32
        )

    def compressed(row, block):
        group = lax.broadcasted_iota(jnp.int32, (part_count, seq_len), 0)
        token_group = lax.broadcasted_iota(jnp.int32, (part_count, seq_len), 1) // stride_len
        band = jnp.where(token_group == group, taps[row : row + 1, :], 0.0)
        band = jnp.where(token_group == group + 1, taps[row + 1 : row + 2, :], band)
        high = band.astype(jnp.bfloat16)
        low = (band - high.astype(jnp.float32)).astype(jnp.bfloat16)
        return dot(high, block) + dot(low, block)

    for head in range(own):
        lanes = slice(head * head_width, (head + 1) * head_width)
        raw_keys = moved[:, row_count : 2 * row_count, lanes].reshape(seq_len, head_width)
        keys[...] = unit_rows(raw_keys.astype(jnp.float32)).astype(jnp.bfloat16)
        raw_values = moved[:, 2 * row_count : 3 * row_count, lanes].reshape(seq_len, head_width)
        values[...] = raw_values
        comp_keys = unit_rows(compressed(2 * head, raw_keys)).astype(jnp.bfloat16)
        comp_values = compressed(2 * (own + head), raw_values).astype(jnp.bfloat16)
        for block in range(ctx_count):
            query = moved[block, 0:row_count, lanes].astype(jnp.float32)
            query = unit_rows(query).astype(jnp.bfloat16)
            base = block * row_count
            rows = slice(base, base + row_count)
            spot = base + lax.broadcasted_iota(jnp.int32, (row_count, part_count), 0)
            ends = lax.broadcasted_iota(jnp.int32, (row_count, part_count), 1) * stride_len
            seen = ends + (block_len - 1) <= spot
            weight = jnp.where(seen, jnp.exp(scale * dot_rows(query, comp_keys)), 0.0)
            total = jnp.sum(weight, axis=1, keepdims=True)
            total = total + jnp.where(spot[:, :1] < block_len - 1, 1.0, 0.0)
            far = dot(weight.astype(jnp.bfloat16), comp_values) / total
            start = max(0, base - WINDOW)
            reach = base + row_count - start
            spot = base + lax.broadcasted_iota(jnp.int32, (row_count, reach), 0)
            key_spot = start + lax.broadcasted_iota(jnp.int32, (row_count, reach), 1)
            seen = (key_spot <= spot) & (key_spot > spot - WINDOW)
            score = dot_rows(query, keys[start : start + reach, :])
            weight = jnp.where(seen, jnp.exp(scale * score), 0.0)
            total = jnp.sum(weight, axis=1, keepdims=True)
            near = dot(weight.astype(jnp.bfloat16), values[start : start + reach, :]) / total
            mixed = (
                gates[rows, head : head + 1] * far
                + gates[rows, own + head : own + head + 1] * near
            ).astype(jnp.bfloat16)
            half = share // 2
            for part in range(row_count // share):
                for group in range(2):
                    target = (part * ctx_count + block) * half
                    base = part * share + group * half
                    out[group, target : target + half, lanes] = mixed[base : base + half]


def attend(moved, taps, gates, row_count, share, block_len, head_width):
    seq_len = moved.shape[0] * row_count
    width = moved.shape[2]
    return pl.pallas_call(
        functools.partial(attend_kernel, row_count, share, block_len, head_width),
        out_shape=jax.ShapeDtypeStruct((2, seq_len // 2, width), jnp.bfloat16),
        scratch_shapes=[
            pltpu.VMEM((seq_len, head_width), jnp.bfloat16),
            pltpu.VMEM((seq_len, head_width), jnp.bfloat16),
        ],
        compiler_params=pltpu.CompilerParams(vmem_limit_bytes=48 * 2**20),
        name="attend",
    )(moved, taps, gates)


def expert_kernel(exp_dim, spots, own, along, across, far_a, far_b, gain, gate_w, up_w, gate_v, up_v, route, out, total, squares):
    step = pl.program_id(0)

    @pl.when(step == 0)
    def _():
        total[...] = jnp.zeros_like(total)
        squares[...] = jnp.zeros_like(squares)

    far = jnp.where(step < pl.num_programs(0) // 2, far_a[0], far_b[0])
    block = jnp.concatenate([own[0], along[0], across[0], far], 0)
    for spot, weight in enumerate((gate_w, up_w, gate_v, up_v)):
        total[spot] += jnp.dot(block, weight[...], preferred_element_type=jnp.float32)
    lane = squares.shape[1]
    collected = squares[...]
    for part in range(block.shape[1] // lane):
        lanes = slice(part * lane, (part + 1) * lane)
        plain = block[:, lanes].astype(jnp.float32) * (1.0 / gain[0, :, lanes])
        collected = collected + plain * plain
    squares[...] = collected

    @pl.when(step == pl.num_programs(0) - 1)
    def _():
        model_width = pl.num_programs(0) * block.shape[1]
        mean_square = jnp.sum(squares[...], axis=1, keepdims=True) / model_width
        inverse = lax.rsqrt(mean_square + norm_eps)
        tokens = own.shape[1]
        for core in range(2):
            gate_part = total[2 * core] * inverse
            up_part = total[2 * core + 1] * inverse
            active = gate_part / (1.0 + jnp.exp(-gate_part)) * up_part
            for source in range(block.shape[0] // tokens):
                spot = pl.ds(jnp.bitwise_xor(spots[1], source), 1)
                piece = active[source * tokens : (source + 1) * tokens] * route[spot][0]
                piece = piece.astype(jnp.bfloat16)
                if exp_dim == 0:
                    out[core, spot] = piece.reshape((1,) + out.shape[2:])
                else:
                    out[core, :, spot] = piece.reshape(out.shape[1], 1, *out.shape[3:])


def run_expert(spots, blocks, gain, weights, route, half, exp_dim):
    chip_count, tokens, wide = blocks[0].shape
    cols = wide // 2
    middle = chip_count // 2
    steps = 2 * chip_count
    units = weights[0].shape[1]
    exp_count = route.shape[0]
    row_total = exp_count * tokens
    lane = math.gcd(128, cols)
    lead = (exp_count, tokens // half) if exp_dim == 0 else (tokens // half, exp_count)
    by_chip = pl.BlockSpec((1, tokens, cols), lambda i, _: (i // 2, 0, i % 2))
    by_cols = pl.BlockSpec((cols, units), lambda i, _: (i, 0))
    out = pl.pallas_call(
        functools.partial(expert_kernel, exp_dim),
        grid_spec=pltpu.PrefetchScalarGridSpec(
            num_scalar_prefetch=1,
            grid=(steps,),
            in_specs=[
                by_chip,
                by_chip,
                by_chip,
                pl.BlockSpec(
                    (1, tokens, cols), lambda i, _: (jnp.minimum(i // 2, middle - 1), 0, i % 2)
                ),
                pl.BlockSpec(
                    (1, tokens, cols), lambda i, _: (jnp.maximum(i // 2 - middle, 0), 0, i % 2)
                ),
                pl.BlockSpec((1, 1, cols), lambda i, _: (i, 0, 0)),
                by_cols,
                by_cols,
                by_cols,
                by_cols,
                pl.BlockSpec((exp_count, tokens, 1), lambda i, _: (0, 0, 0)),
            ],
            out_specs=pl.BlockSpec((2,) + lead + (half, units), lambda i, _: (0, 0, 0, 0, 0)),
            scratch_shapes=[
                pltpu.VMEM((4, row_total, units), jnp.float32),
                pltpu.VMEM((row_total, lane), jnp.float32),
            ],
        ),
        out_shape=jax.ShapeDtypeStruct((2,) + lead + (half, units), jnp.bfloat16),
        compiler_params=pltpu.CompilerParams(vmem_limit_bytes=40 * 2**20),
        cost_estimate=pl.CostEstimate(
            flops=8 * row_total * units * steps * cols,
            bytes_accessed=2 * steps * cols * (row_total + 4 * units),
            transcendentals=2 * row_total * units,
        ),
        name="expert",
    )(spots, *blocks, gain.reshape(steps, 1, cols), *weights, route)
    return out.reshape(2, row_total, units)


def down_kernel(exp_dim, spots, active, down_w, down_v, hidden, out):
    sums = jnp.dot(active[0], down_w[...], preferred_element_type=jnp.float32)
    sums += jnp.dot(active[1], down_v[...], preferred_element_type=jnp.float32)
    out[...] = sums.astype(out.dtype).reshape(out.shape)

    @pl.when(pl.program_id(0) == spots[0])
    def _():
        spot = pl.ds(spots[1], 1)
        place = (spot,) if exp_dim == 0 else (slice(None), spot)
        piece = out[place].astype(jnp.float32)
        out[place] = (piece + hidden[...].reshape(piece.shape)).astype(out.dtype)


def run_down(spots, active, down_w, down_v, hidden, exp_count, exp_dim):
    units, model_width = down_w.shape
    chip_count, half, wide = hidden.shape
    cols = wide
    lead = (exp_count, chip_count) if exp_dim == 0 else (chip_count, exp_count)
    by_cols = pl.BlockSpec((units, cols), lambda i, _: (0, i))
    rows = active.shape[1]
    return pl.pallas_call(
        functools.partial(down_kernel, exp_dim),
        grid_spec=pltpu.PrefetchScalarGridSpec(
            num_scalar_prefetch=1,
            grid=(model_width // cols,),
            in_specs=[
                pl.BlockSpec((2, rows, units), lambda i, _: (0, 0, 0)),
                by_cols,
                by_cols,
                pl.BlockSpec((chip_count, half, cols), lambda i, _: (0, 0, 0)),
            ],
            out_specs=pl.BlockSpec(lead + (half, cols), lambda i, _: (0, 0, 0, i)),
        ),
        out_shape=jax.ShapeDtypeStruct(lead + (half, model_width), jnp.bfloat16),
        compiler_params=pltpu.CompilerParams(vmem_limit_bytes=40 * 2**20),
        cost_estimate=pl.CostEstimate(
            flops=4 * rows * units * model_width,
            bytes_accessed=2 * model_width * (rows + 2 * units),
            transcendentals=0,
        ),
        name="down",
    )(spots, active, down_w, down_v, hidden)


def sibling(block):
    return lax.ppermute(block, "core", [(0, 1), (1, 0)])


def plane_step(block, step):
    count = lax.axis_size("exp")
    return lax.ppermute(block, "exp", [(i, i ^ step) for i in range(count)])


def by_heads(
    query_input,
    key_input,
    value_input,
    gate_logits,
    comp_weight,
    out_proj,
    residual_in,
    ffn_gain,
    expert_ids,
    route_gates,
    expert_gate,
    expert_up,
    expert_down,
):
    row_count = query_input.shape[0]
    head_count = comp_weight.shape[2]
    head_width = query_input.shape[1] // head_count
    block_len = comp_weight.shape[1]
    stride_len = block_len // 2
    ctx = ("z", "core")
    chip_count = lax.axis_size("z")
    ctx_count = chip_count * lax.axis_size("core")
    exp_count = lax.axis_size("exp")
    chip_index = lax.axis_index("z")
    core_index = lax.axis_index("core")
    ctx_index = 2 * chip_index + core_index
    exp_index = lax.axis_index("exp")
    own = head_count // ctx_count
    width = own * head_width
    share = row_count // exp_count
    half = share // 2
    seq_len = row_count * ctx_count
    cols = out_proj.shape[1]
    model_width = cols * ctx_count
    own_tokens = ctx_count * share

    other_gate = sibling(expert_gate[0])
    other_up = sibling(expert_up[0])
    other_down = sibling(expert_down[0])

    experts = jnp.arange(exp_count, dtype=jnp.int32)
    table = jnp.sum(
        jnp.where(expert_ids[:, :, None] == experts, route_gates[:, :, None], 0.0), axis=1
    )
    table = jnp.broadcast_to(high_low(table).reshape(1, -1), (ctx_count, 2 * share * exp_count))
    gates = high_low(jax.nn.sigmoid(gate_logits)).reshape(2, 2, row_count, ctx_count, own)
    gates = jnp.transpose(gates, (3, 0, 1, 2, 4)).reshape(ctx_count, -1)
    side = jnp.concatenate([gates, table], 1)
    side_rows = -(-side.shape[1] // width)
    residual_rows = -(-share * cols // width)
    side_rows += -(3 * row_count + residual_rows + side_rows) % 16
    side = jnp.pad(side, ((0, 0), (0, side_rows * width - side.shape[1])))
    residual = jnp.transpose(residual_in.reshape(share, ctx_count, cols), (1, 0, 2))
    residual = residual.reshape(ctx_count, share * cols)
    residual = jnp.pad(residual, ((0, 0), (0, residual_rows * width - share * cols)))
    heads = [
        jnp.transpose(block.reshape(row_count, ctx_count, width), (1, 0, 2))
        for block in (query_input, key_input, value_input)
    ]
    packed = jnp.concatenate(
        heads
        + [
            residual.reshape(ctx_count, residual_rows, width),
            side.reshape(ctx_count, side_rows, width),
        ],
        1,
    )
    moved = lax.all_to_all(packed, ctx, split_axis=0, concat_axis=0, tiled=True)
    residual = moved[:, 3 * row_count : 3 * row_count + residual_rows].reshape(ctx_count, -1)
    residual = residual[:, : share * cols].reshape(own_tokens, cols)
    side = moved[:, 3 * row_count + residual_rows :].reshape(ctx_count, -1).astype(jnp.float32)
    gate_size = 4 * row_count * own
    gates = side[:, :gate_size].reshape(ctx_count, 2, 2, row_count, own)
    gates = jnp.transpose(gates[:, 0] + gates[:, 1], (0, 2, 1, 3)).reshape(seq_len, 2 * own)
    table = side[:, gate_size : gate_size + 2 * share * exp_count]
    table = table.reshape(chip_count, 2, 2, share, exp_count)
    table = lax.dynamic_index_in_dim(table, core_index, 1, keepdims=False)

    taps = lax.dynamic_slice_in_dim(comp_weight, ctx_index * own, own, 2)
    taps = jnp.transpose(taps.reshape(2, 2, stride_len, own), (0, 3, 1, 2))
    taps = jnp.tile(taps.reshape(4 * own, stride_len), (1, seq_len // stride_len))
    attended = attend(moved, taps, gates, row_count, share, block_len, head_width)

    table = jnp.transpose(table, (3, 1, 0, 2)).reshape(exp_count, -1).astype(jnp.bfloat16)
    table_rows = -(-table.shape[1] // cols)
    table_rows += -table_rows % 16
    table = jnp.pad(table, ((0, 0), (0, table_rows * cols - table.shape[1])))
    table = table.reshape(exp_count, table_rows, cols)
    gain = lax.dynamic_slice_in_dim(ffn_gain, chip_index * 2 * cols, 2 * cols, 0)
    spots = jnp.stack([chip_index, exp_index]).astype(jnp.int32)
    group_tokens = ctx_count * half
    hidden, blocks = [], []
    for group in range(2):
        spread_heads = lax.all_gather(attended[group], ctx, axis=0)
        pieces = jnp.einsum(
            "csk,ckd->sd",
            spread_heads,
            out_proj.reshape(ctx_count, width, cols),
            preferred_element_type=jnp.float32,
        ).astype(jnp.bfloat16)
        pieces = pieces.reshape(exp_count, group_tokens, cols)
        if group == 0:
            pieces = jnp.concatenate([pieces, table], 1)
        else:
            pieces, _ = lax.optimization_barrier((pieces, scaled))
        pieces = lax.all_to_all(pieces, "exp", split_axis=0, concat_axis=0, tiled=True)
        if group == 0:
            route = pieces[:, group_tokens:].reshape(exp_count, -1)[:, : 2 * chip_count * share]
            route = jnp.sum(
                route.reshape(exp_count, 2, chip_count, 2, half).astype(jnp.float32), axis=1
            )
        sums = jnp.sum(pieces[:, :group_tokens].astype(jnp.float32), axis=0)
        own_rows = residual.reshape(ctx_count, 2, half, cols)[:, group]
        sums = sums.reshape(ctx_count, half, cols) + own_rows.astype(jnp.float32)
        sums = sums.reshape(chip_count, 2, half, cols)
        kept = lax.dynamic_index_in_dim(sums, core_index, 1, keepdims=False)
        given = sibling(lax.dynamic_index_in_dim(sums, 1 - core_index, 1, keepdims=False))
        sums = jnp.concatenate(
            [jnp.where(core_index == 0, kept, given), jnp.where(core_index == 0, given, kept)], 2
        )
        scaled = (sums * gain).astype(jnp.bfloat16).reshape(chip_count * half, 2 * cols)
        plane = lax.all_gather(scaled, "z", axis=0)
        along, across = plane_step(plane, 1), plane_step(plane, 2)
        far_a = plane_step(along[: chip_count // 2], 2)
        far_b = plane_step(across[chip_count // 2 :], 1)
        hidden.append(sums)
        blocks.append((plane, along, across, far_a, far_b))

    weights = (expert_gate[0], expert_up[0], other_gate, other_up)
    outs = []
    for group in range(2):
        route_rows = route[:, :, group].reshape(exp_count, chip_count * half, 1)
        active = run_expert(
            spots, blocks[group], ffn_gain, weights, route_rows, half, 1 - group
        )
        outs.append(
            run_down(
                spots, active, expert_down[0], other_down, hidden[group], exp_count, 1 - group
            )
        )

    first = lax.psum_scatter(
        outs[0].reshape(chip_count, exp_count * half, model_width),
        "z",
        scatter_dimension=0,
        tiled=True,
    )
    first = lax.all_to_all(
        first.reshape(exp_count, half, model_width), "exp", split_axis=0, concat_axis=0, tiled=True
    )
    first = jnp.sum(first.astype(jnp.float32), axis=0).astype(jnp.bfloat16)

    second = lax.all_to_all(outs[1], "exp", split_axis=0, concat_axis=0, tiled=True)
    second = jnp.sum(second.astype(jnp.float32), axis=0).astype(jnp.bfloat16)
    second = lax.psum_scatter(second, "z", scatter_dimension=0, tiled=True)
    return jnp.concatenate([first, second.reshape(half, model_width)], 0)


def specs(ctx):
    in_specs = (
        P(ctx, "exp"),
        P(ctx, "exp"),
        P(ctx, "exp"),
        P(None, ctx, "exp"),
        P(None, None, "exp"),
        P("exp", ctx),
        P((*ctx, "exp"), None),
        P(),
        P((*ctx, "exp"), None),
        P((*ctx, "exp"), None),
        P("exp", None, ctx),
        P("exp", None, ctx),
        P("exp", ctx, None),
    )
    return in_specs, P((*ctx, "exp"), None)


def solution(mesh):
    ctx_count, exp_count = mesh.shape["ctx"], mesh.shape["exp"]

    def run(*args):
        head_count = args[4].shape[2] // exp_count
        share = args[0].shape[0] // (ctx_count * exp_count)
        body, axes, where = general, ("ctx",), mesh
        whole = head_count % ctx_count == 0 and share % 32 == 0 and ctx_count % 4 == 0
        if whole and exp_count.bit_length() == 3 and exp_count.bit_count() == 1:
            split = mesh.devices.reshape(ctx_count // 2, 2, exp_count)
            where = jax.sharding.Mesh(split, ("z", "core", "exp"))
            body, axes = by_heads, ("z", "core")
        in_specs, out_specs = specs(axes)
        return jax.shard_map(
            body, mesh=where, in_specs=in_specs, out_specs=out_specs, check_vma=False
        )(*args)

    return run
```

```python
import functools
import math

import jax
import jax.numpy as jnp
from jax import lax
from jax.experimental import pallas as pl
from jax.experimental.pallas import tpu as pltpu
from jax.sharding import PartitionSpec as P

WINDOW = 512


score_gain = 2.0
norm_eps = 1e-06


def passed_along(block, axis, distance):
    devices = range(lax.axis_size(axis))
    route = [(i - distance, i) for i in devices if i - distance in devices]
    return lax.ppermute(block, axis, route)


def head_norm(matrix, head_width):
    row_count = matrix.shape[0]
    shaped = matrix.reshape(row_count, -1, head_width).astype(jnp.float32)
    scaled = shaped * lax.rsqrt(jnp.mean(shaped * shaped, axis=2, keepdims=True) + norm_eps)
    return scaled.reshape(row_count, -1)


def compress(extended, position_weights, head_width):
    stride_len = position_weights.shape[0] // 2
    head_count = position_weights.shape[1]
    blocks = extended.reshape(-1, stride_len, head_count, head_width).astype(jnp.float32)
    first_half = jnp.einsum(
        "nshd,sh->nhd", blocks[:-1], position_weights[:stride_len], precision=lax.Precision.HIGHEST
    )
    second_half = jnp.einsum(
        "nshd,sh->nhd", blocks[1:], position_weights[stride_len:], precision=lax.Precision.HIGHEST
    )
    return (first_half + second_half).reshape(blocks.shape[0] - 1, head_count * head_width)


def window_attention(query_input, key_input, value_input, gate_logits, comp_weight):
    row_count = query_input.shape[0]
    head_count = comp_weight.shape[2]
    head_width = query_input.shape[1] // head_count
    block_len = comp_weight.shape[1]
    stride_len = block_len // 2
    exp_count = lax.axis_size("exp")
    ctx_index = lax.axis_index("ctx")
    scale = score_gain / math.sqrt(head_width)
    query_norm = head_norm(query_input, head_width).astype(jnp.bfloat16)
    key_norm = head_norm(key_input, head_width).astype(jnp.bfloat16)
    next_keys, next_values = passed_along(
        (key_input[:stride_len], value_input[:stride_len]), "ctx", -1
    )
    comp_keys = head_norm(
        compress(jnp.concatenate([key_input, next_keys], 0), comp_weight[0], head_width), head_width
    ).astype(jnp.bfloat16)
    comp_values = compress(
        jnp.concatenate([value_input, next_values], 0), comp_weight[1], head_width
    ).astype(jnp.bfloat16)
    query_pos = ctx_index * row_count + jnp.arange(row_count, dtype=jnp.int32)
    query_heads = query_norm.reshape(row_count, head_count, head_width)
    part_keys = lax.all_gather(comp_keys, "ctx", axis=0, tiled=True)
    part_values = lax.all_gather(comp_values, "ctx", axis=0, tiled=True)
    part_count = part_keys.shape[0]
    scores = jnp.einsum(
        "thd,nhd->htn",
        query_heads,
        part_keys.reshape(part_count, head_count, head_width),
        preferred_element_type=jnp.float32,
    )
    block_end = jnp.arange(part_count, dtype=jnp.int32) * stride_len + block_len - 1
    visible = block_end[None, :] <= query_pos[:, None]
    weights = jnp.where(visible[None], jnp.exp(scale * scores), 0.0)
    running_total = jnp.sum(weights, axis=2).T
    collected = jnp.einsum(
        "htn,nhd->thd",
        weights.astype(jnp.bfloat16),
        part_values.reshape(part_count, head_count, head_width),
        preferred_element_type=jnp.float32,
    )
    cmp_sum = collected.reshape(row_count, -1)
    no_block = (query_pos < block_len - 1).astype(jnp.float32)
    cmp_out = (
        cmp_sum.reshape(row_count, head_count, head_width)
        / (running_total + no_block[:, None])[:, :, None]
    )
    shift_count = max(1, WINDOW // row_count)
    earlier_keys = []
    earlier_values = []
    for distance in range(shift_count, 0, -1):
        moved_keys, moved_values = passed_along((key_norm, value_input), "ctx", distance)
        earlier_keys.append(moved_keys)
        earlier_values.append(moved_values)
    near_keys = jnp.concatenate(earlier_keys + [key_norm], 0)
    near_values = jnp.concatenate(earlier_values + [value_input], 0)
    key_pos = ctx_index * row_count - WINDOW + jnp.arange(near_keys.shape[0], dtype=jnp.int32)
    near_scores = jnp.einsum(
        "thd,shd->hts",
        query_heads,
        near_keys.reshape(-1, head_count, head_width),
        preferred_element_type=jnp.float32,
    )
    inside = (
        (key_pos[None, :] <= query_pos[:, None])
        & (key_pos[None, :] > query_pos[:, None] - WINDOW)
        & (key_pos[None, :] >= 0)
    )
    near_weights = jnp.where(inside[None], jnp.exp(scale * near_scores), 0.0)
    win_total = jnp.sum(near_weights, axis=2).T
    win_sum = jnp.einsum(
        "hts,shd->thd",
        near_weights.astype(jnp.bfloat16),
        near_values.reshape(-1, head_count, head_width),
        preferred_element_type=jnp.float32,
    )
    win_out = win_sum / win_total[:, :, None]
    branch_gates = jax.nn.sigmoid(gate_logits)
    attended = (
        (branch_gates[0][:, :, None] * cmp_out + branch_gates[1][:, :, None] * win_out)
        .reshape(row_count, -1)
        .astype(jnp.bfloat16)
    )
    return attended


def general(
    query_input,
    key_input,
    value_input,
    gate_logits,
    comp_weight,
    out_proj,
    residual_in,
    ffn_gain,
    expert_ids,
    route_gates,
    expert_gate,
    expert_up,
    expert_down,
):
    row_count = query_input.shape[0]
    ctx_count = lax.axis_size("ctx")
    exp_count = lax.axis_size("exp")
    ctx_index = lax.axis_index("ctx")
    exp_index = lax.axis_index("exp")
    share = row_count // exp_count
    seq_len = row_count * ctx_count
    cols = out_proj.shape[1]
    model_width = cols * ctx_count
    hidden_units = expert_gate.shape[2]
    own_tokens = ctx_count * share

    experts = jnp.arange(exp_count, dtype=jnp.int32)
    route_table = jnp.sum(
        jnp.where(expert_ids[:, :, None] == experts, route_gates[:, :, None], 0.0), axis=1
    )
    route_all = lax.all_gather(route_table, ("ctx", "exp"), axis=0, tiled=True)
    route_own = lax.dynamic_slice_in_dim(route_all, exp_index, 1, 1)
    residual = lax.all_to_all(residual_in, "ctx", split_axis=1, concat_axis=0, tiled=True)

    attention_args = (query_input, key_input, value_input, gate_logits, comp_weight)
    attended = window_attention(*attention_args)
    spread_rows = lax.all_gather(
        attended.reshape(1, exp_count, share, -1), "ctx", axis=0, tiled=True
    )
    partial = jnp.einsum(
        "cerh,hd->ecrd", spread_rows, out_proj, preferred_element_type=jnp.float32
    )
    pieces = lax.all_to_all(
        partial.astype(jnp.bfloat16).reshape(exp_count, own_tokens, cols),
        "exp",
        split_axis=0,
        concat_axis=0,
        tiled=True,
    )
    hidden_state = residual.reshape(own_tokens, cols).astype(jnp.float32) + jnp.sum(
        pieces.astype(jnp.float32), axis=0
    )
    gain = lax.dynamic_slice_in_dim(ffn_gain, ctx_index * cols, cols, 0)
    scaled = (hidden_state * gain).astype(jnp.bfloat16)
    squares = jnp.sum(hidden_state * hidden_state, axis=1)
    rows = lax.all_gather(scaled, ("ctx", "exp"), axis=0, tiled=True)
    rows = rows.reshape(ctx_count, seq_len, cols)
    squares = lax.all_gather(squares, ("ctx", "exp"), axis=0, tiled=True)
    mean_square = jnp.sum(squares.reshape(ctx_count, seq_len), axis=0) / model_width
    inverse = lax.rsqrt(mean_square + norm_eps)[:, None]

    gate_part = inverse * jnp.einsum(
        "ctk,ckf->tf",
        rows,
        expert_gate.reshape(ctx_count, cols, hidden_units),
        preferred_element_type=jnp.float32,
    )
    up_part = inverse * jnp.einsum(
        "ctk,ckf->tf",
        rows,
        expert_up.reshape(ctx_count, cols, hidden_units),
        preferred_element_type=jnp.float32,
    )
    activated = (jax.nn.silu(gate_part) * up_part).astype(jnp.bfloat16)
    activated = jnp.transpose(
        activated.reshape(exp_count, ctx_count, share, hidden_units), (1, 0, 2, 3)
    ).reshape(seq_len, hidden_units)
    outs = jnp.dot(activated, expert_down[0], preferred_element_type=jnp.float32)
    outs = (outs * route_own).astype(jnp.bfloat16)
    outs = outs.reshape(ctx_count, exp_count, share, model_width)
    place = (0, exp_index, 0, ctx_index * cols)
    mine = lax.dynamic_slice(outs, place, (ctx_count, 1, share, cols))
    mine = mine.astype(jnp.float32) + hidden_state.reshape(ctx_count, 1, share, cols)
    outs = lax.dynamic_update_slice(outs, mine.astype(jnp.bfloat16), place)
    return lax.psum_scatter(
        outs.reshape(seq_len, model_width), ("ctx", "exp"), scatter_dimension=0, tiled=True
    )


def high_low(values):
    high = lax.reduce_precision(values, 8, 7)
    return jnp.stack([high, values - high], 0).astype(jnp.bfloat16)


def unit_rows(block):
    return block * lax.rsqrt(jnp.mean(block * block, axis=1, keepdims=True) + norm_eps)


def attend_kernel(row_count, share, block_len, head_width, moved, taps, gates, out, keys, values):
    ctx_count = moved.shape[0]
    own = moved.shape[2] // head_width
    seq_len = row_count * ctx_count
    stride_len = block_len // 2
    part_count = seq_len // stride_len
    scale = score_gain / math.sqrt(head_width)

    def dot(left, right):
        return jnp.dot(left, right, preferred_element_type=jnp.float32)

    def dot_rows(left, right):
        return lax.dot_general(
            left, right, (((1,), (1,)), ((), ())), preferred_element_type=jnp.float32
        )

    def compressed(row, block):
        group = lax.broadcasted_iota(jnp.int32, (part_count, seq_len), 0)
        token_group = lax.broadcasted_iota(jnp.int32, (part_count, seq_len), 1) // stride_len
        band = jnp.where(token_group == group, taps[row : row + 1, :], 0.0)
        band = jnp.where(token_group == group + 1, taps[row + 1 : row + 2, :], band)
        high = band.astype(jnp.bfloat16)
        low = (band - high.astype(jnp.float32)).astype(jnp.bfloat16)
        return dot(high, block) + dot(low, block)

    for head in range(own):
        lanes = slice(head * head_width, (head + 1) * head_width)
        raw_keys = moved[:, row_count : 2 * row_count, lanes].reshape(seq_len, head_width)
        keys[...] = unit_rows(raw_keys.astype(jnp.float32)).astype(jnp.bfloat16)
        raw_values = moved[:, 2 * row_count : 3 * row_count, lanes].reshape(seq_len, head_width)
        values[...] = raw_values
        comp_keys = unit_rows(compressed(2 * head, raw_keys)).astype(jnp.bfloat16)
        comp_values = compressed(2 * (own + head), raw_values).astype(jnp.bfloat16)
        for block in range(ctx_count):
            query = moved[block, 0:row_count, lanes].astype(jnp.float32)
            query = unit_rows(query).astype(jnp.bfloat16)
            base = block * row_count
            rows = slice(base, base + row_count)
            spot = base + lax.broadcasted_iota(jnp.int32, (row_count, part_count), 0)
            ends = lax.broadcasted_iota(jnp.int32, (row_count, part_count), 1) * stride_len
            seen = ends + (block_len - 1) <= spot
            weight = jnp.where(seen, jnp.exp(scale * dot_rows(query, comp_keys)), 0.0)
            total = jnp.sum(weight, axis=1, keepdims=True)
            total = total + jnp.where(spot[:, :1] < block_len - 1, 1.0, 0.0)
            far = dot(weight.astype(jnp.bfloat16), comp_values) / total
            start = max(0, base - WINDOW)
            reach = base + row_count - start
            spot = base + lax.broadcasted_iota(jnp.int32, (row_count, reach), 0)
            key_spot = start + lax.broadcasted_iota(jnp.int32, (row_count, reach), 1)
            seen = (key_spot <= spot) & (key_spot > spot - WINDOW)
            score = dot_rows(query, keys[start : start + reach, :])
            weight = jnp.where(seen, jnp.exp(scale * score), 0.0)
            total = jnp.sum(weight, axis=1, keepdims=True)
            near = dot(weight.astype(jnp.bfloat16), values[start : start + reach, :]) / total
            mixed = (
                gates[rows, head : head + 1] * far
                + gates[rows, own + head : own + head + 1] * near
            ).astype(jnp.bfloat16)
            half = share // 2
            for part in range(row_count // share):
                for group in range(2):
                    target = (part * ctx_count + block) * half
                    base = part * share + group * half
                    out[group, target : target + half, lanes] = mixed[base : base + half]


def attend(moved, taps, gates, row_count, share, block_len, head_width):
    seq_len = moved.shape[0] * row_count
    width = moved.shape[2]
    return pl.pallas_call(
        functools.partial(attend_kernel, row_count, share, block_len, head_width),
        out_shape=jax.ShapeDtypeStruct((2, seq_len // 2, width), jnp.bfloat16),
        scratch_shapes=[
            pltpu.VMEM((seq_len, head_width), jnp.bfloat16),
            pltpu.VMEM((seq_len, head_width), jnp.bfloat16),
        ],
        compiler_params=pltpu.CompilerParams(vmem_limit_bytes=48 * 2**20),
        name="attend",
    )(moved, taps, gates)


def expert_kernel(exp_dim, spots, own, along, across, far_a, far_b, gain, gate_w, up_w, gate_v, up_v, route, out, total, squares):
    step = pl.program_id(0)

    @pl.when(step == 0)
    def _():
        total[...] = jnp.zeros_like(total)
        squares[...] = jnp.zeros_like(squares)

    far = jnp.where(step < pl.num_programs(0) // 2, far_a[0], far_b[0])
    block = jnp.concatenate([own[0], along[0], across[0], far], 0)
    for spot, weight in enumerate((gate_w, up_w, gate_v, up_v)):
        total[spot] += jnp.dot(block, weight[...], preferred_element_type=jnp.float32)
    lane = squares.shape[1]
    collected = squares[...]
    for part in range(block.shape[1] // lane):
        lanes = slice(part * lane, (part + 1) * lane)
        plain = block[:, lanes].astype(jnp.float32) * (1.0 / gain[0, :, lanes])
        collected = collected + plain * plain
    squares[...] = collected

    @pl.when(step == pl.num_programs(0) - 1)
    def _():
        model_width = pl.num_programs(0) * block.shape[1]
        mean_square = jnp.sum(squares[...], axis=1, keepdims=True) / model_width
        inverse = lax.rsqrt(mean_square + norm_eps)
        tokens = own.shape[1]
        for core in range(2):
            gate_part = total[2 * core] * inverse
            up_part = total[2 * core + 1] * inverse
            active = gate_part / (1.0 + jnp.exp(-gate_part)) * up_part
            for source in range(block.shape[0] // tokens):
                spot = pl.ds(jnp.bitwise_xor(spots[1], source), 1)
                piece = active[source * tokens : (source + 1) * tokens] * route[spot][0]
                piece = piece.astype(jnp.bfloat16)
                if exp_dim == 0:
                    out[core, spot] = piece.reshape((1,) + out.shape[2:])
                else:
                    out[core, :, spot] = piece.reshape(out.shape[1], 1, *out.shape[3:])


def run_expert(spots, blocks, gain, weights, route, half, exp_dim):
    chip_count, tokens, wide = blocks[0].shape
    cols = wide // 2
    middle = chip_count // 2
    steps = 2 * chip_count
    units = weights[0].shape[1]
    exp_count = route.shape[0]
    row_total = exp_count * tokens
    lane = math.gcd(128, cols)
    lead = (exp_count, tokens // half) if exp_dim == 0 else (tokens // half, exp_count)
    by_chip = pl.BlockSpec((1, tokens, cols), lambda i, _: (i // 2, 0, i % 2))
    by_cols = pl.BlockSpec((cols, units), lambda i, _: (i, 0))
    out = pl.pallas_call(
        functools.partial(expert_kernel, exp_dim),
        grid_spec=pltpu.PrefetchScalarGridSpec(
            num_scalar_prefetch=1,
            grid=(steps,),
            in_specs=[
                by_chip,
                by_chip,
                by_chip,
                pl.BlockSpec(
                    (1, tokens, cols), lambda i, _: (jnp.minimum(i // 2, middle - 1), 0, i % 2)
                ),
                pl.BlockSpec(
                    (1, tokens, cols), lambda i, _: (jnp.maximum(i // 2 - middle, 0), 0, i % 2)
                ),
                pl.BlockSpec((1, 1, cols), lambda i, _: (i, 0, 0)),
                by_cols,
                by_cols,
                by_cols,
                by_cols,
                pl.BlockSpec((exp_count, tokens, 1), lambda i, _: (0, 0, 0)),
            ],
            out_specs=pl.BlockSpec((2,) + lead + (half, units), lambda i, _: (0, 0, 0, 0, 0)),
            scratch_shapes=[
                pltpu.VMEM((4, row_total, units), jnp.float32),
                pltpu.VMEM((row_total, lane), jnp.float32),
            ],
        ),
        out_shape=jax.ShapeDtypeStruct((2,) + lead + (half, units), jnp.bfloat16),
        compiler_params=pltpu.CompilerParams(vmem_limit_bytes=40 * 2**20),
        cost_estimate=pl.CostEstimate(
            flops=8 * row_total * units * steps * cols,
            bytes_accessed=2 * steps * cols * (row_total + 4 * units),
            transcendentals=2 * row_total * units,
        ),
        name="expert",
    )(spots, *blocks, gain.reshape(steps, 1, cols), *weights, route)
    return out.reshape(2, row_total, units)


def down_kernel(exp_dim, spots, active, down_w, down_v, hidden, out):
    sums = jnp.dot(active[0], down_w[...], preferred_element_type=jnp.float32)
    sums += jnp.dot(active[1], down_v[...], preferred_element_type=jnp.float32)
    out[...] = sums.astype(out.dtype).reshape(out.shape)

    @pl.when(pl.program_id(0) == spots[0])
    def _():
        spot = pl.ds(spots[1], 1)
        place = (spot,) if exp_dim == 0 else (slice(None), spot)
        piece = out[place].astype(jnp.float32)
        out[place] = (piece + hidden[...].reshape(piece.shape)).astype(out.dtype)


def run_down(spots, active, down_w, down_v, hidden, exp_count, exp_dim):
    units, model_width = down_w.shape
    chip_count, half, wide = hidden.shape
    cols = wide
    lead = (exp_count, chip_count) if exp_dim == 0 else (chip_count, exp_count)
    by_cols = pl.BlockSpec((units, cols), lambda i, _: (0, i))
    rows = active.shape[1]
    return pl.pallas_call(
        functools.partial(down_kernel, exp_dim),
        grid_spec=pltpu.PrefetchScalarGridSpec(
            num_scalar_prefetch=1,
            grid=(model_width // cols,),
            in_specs=[
                pl.BlockSpec((2, rows, units), lambda i, _: (0, 0, 0)),
                by_cols,
                by_cols,
                pl.BlockSpec((chip_count, half, cols), lambda i, _: (0, 0, 0)),
            ],
            out_specs=pl.BlockSpec(lead + (half, cols), lambda i, _: (0, 0, 0, i)),
        ),
        out_shape=jax.ShapeDtypeStruct(lead + (half, model_width), jnp.bfloat16),
        compiler_params=pltpu.CompilerParams(vmem_limit_bytes=40 * 2**20),
        cost_estimate=pl.CostEstimate(
            flops=4 * rows * units * model_width,
            bytes_accessed=2 * model_width * (rows + 2 * units),
            transcendentals=0,
        ),
        name="down",
    )(spots, active, down_w, down_v, hidden)


def sibling(block):
    return lax.ppermute(block, "core", [(0, 1), (1, 0)])


def plane_step(block, step):
    count = lax.axis_size("exp")
    return lax.ppermute(block, "exp", [(i, i ^ step) for i in range(count)])


def by_heads(
    query_input,
    key_input,
    value_input,
    gate_logits,
    comp_weight,
    out_proj,
    residual_in,
    ffn_gain,
    expert_ids,
    route_gates,
    expert_gate,
    expert_up,
    expert_down,
):
    row_count = query_input.shape[0]
    head_count = comp_weight.shape[2]
    head_width = query_input.shape[1] // head_count
    block_len = comp_weight.shape[1]
    stride_len = block_len // 2
    ctx = ("z", "core")
    chip_count = lax.axis_size("z")
    ctx_count = chip_count * lax.axis_size("core")
    exp_count = lax.axis_size("exp")
    chip_index = lax.axis_index("z")
    core_index = lax.axis_index("core")
    ctx_index = 2 * chip_index + core_index
    exp_index = lax.axis_index("exp")
    own = head_count // ctx_count
    width = own * head_width
    share = row_count // exp_count
    half = share // 2
    seq_len = row_count * ctx_count
    cols = out_proj.shape[1]
    model_width = cols * ctx_count
    own_tokens = ctx_count * share

    other_gate = sibling(expert_gate[0])
    other_up = sibling(expert_up[0])
    other_down = sibling(expert_down[0])

    experts = jnp.arange(exp_count, dtype=jnp.int32)
    table = jnp.sum(
        jnp.where(expert_ids[:, :, None] == experts, route_gates[:, :, None], 0.0), axis=1
    )
    table = jnp.broadcast_to(high_low(table).reshape(1, -1), (ctx_count, 2 * share * exp_count))
    gates = high_low(jax.nn.sigmoid(gate_logits)).reshape(2, 2, row_count, ctx_count, own)
    gates = jnp.transpose(gates, (3, 0, 1, 2, 4)).reshape(ctx_count, -1)
    side = jnp.concatenate([gates, table], 1)
    side_rows = -(-side.shape[1] // width)
    residual_rows = -(-share * cols // width)
    side_rows += -(3 * row_count + residual_rows + side_rows) % 16
    side = jnp.pad(side, ((0, 0), (0, side_rows * width - side.shape[1])))
    residual = jnp.transpose(residual_in.reshape(share, ctx_count, cols), (1, 0, 2))
    residual = residual.reshape(ctx_count, share * cols)
    residual = jnp.pad(residual, ((0, 0), (0, residual_rows * width - share * cols)))
    heads = [
        jnp.transpose(block.reshape(row_count, ctx_count, width), (1, 0, 2))
        for block in (query_input, key_input, value_input)
    ]
    packed = jnp.concatenate(
        heads
        + [
            residual.reshape(ctx_count, residual_rows, width),
            side.reshape(ctx_count, side_rows, width),
        ],
        1,
    )
    moved = lax.all_to_all(packed, ctx, split_axis=0, concat_axis=0, tiled=True)
    residual = moved[:, 3 * row_count : 3 * row_count + residual_rows].reshape(ctx_count, -1)
    residual = residual[:, : share * cols].reshape(own_tokens, cols)
    side = moved[:, 3 * row_count + residual_rows :].reshape(ctx_count, -1).astype(jnp.float32)
    gate_size = 4 * row_count * own
    gates = side[:, :gate_size].reshape(ctx_count, 2, 2, row_count, own)
    gates = jnp.transpose(gates[:, 0] + gates[:, 1], (0, 2, 1, 3)).reshape(seq_len, 2 * own)
    table = side[:, gate_size : gate_size + 2 * share * exp_count]
    table = table.reshape(chip_count, 2, 2, share, exp_count)
    table = lax.dynamic_index_in_dim(table, core_index, 1, keepdims=False)

    taps = lax.dynamic_slice_in_dim(comp_weight, ctx_index * own, own, 2)
    taps = jnp.transpose(taps.reshape(2, 2, stride_len, own), (0, 3, 1, 2))
    taps = jnp.tile(taps.reshape(4 * own, stride_len), (1, seq_len // stride_len))
    attended = attend(moved, taps, gates, row_count, share, block_len, head_width)

    table = jnp.transpose(table, (3, 1, 0, 2)).reshape(exp_count, -1).astype(jnp.bfloat16)
    table_rows = -(-table.shape[1] // cols)
    table_rows += -table_rows % 16
    table = jnp.pad(table, ((0, 0), (0, table_rows * cols - table.shape[1])))
    table = table.reshape(exp_count, table_rows, cols)
    gain = lax.dynamic_slice_in_dim(ffn_gain, chip_index * 2 * cols, 2 * cols, 0)
    spots = jnp.stack([chip_index, exp_index]).astype(jnp.int32)
    group_tokens = ctx_count * half
    def project(spread_heads):
        pieces = jnp.einsum(
            "csk,ckd->sd",
            spread_heads,
            out_proj.reshape(ctx_count, width, cols),
            preferred_element_type=jnp.float32,
        ).astype(jnp.bfloat16)
        return pieces.reshape(exp_count, group_tokens, cols)

    def exchange(pieces):
        return lax.all_to_all(pieces, "exp", split_axis=0, concat_axis=0, tiled=True)

    def settle(pieces, group):
        sums = jnp.sum(pieces[:, :group_tokens].astype(jnp.float32), axis=0)
        own_rows = residual.reshape(ctx_count, 2, half, cols)[:, group]
        sums = sums.reshape(ctx_count, half, cols) + own_rows.astype(jnp.float32)
        sums = sums.reshape(chip_count, 2, half, cols)
        kept = lax.dynamic_index_in_dim(sums, core_index, 1, keepdims=False)
        given = sibling(lax.dynamic_index_in_dim(sums, 1 - core_index, 1, keepdims=False))
        sums = jnp.concatenate(
            [jnp.where(core_index == 0, kept, given), jnp.where(core_index == 0, given, kept)], 2
        )
        scaled = (sums * gain).astype(jnp.bfloat16).reshape(chip_count * half, 2 * cols)
        return sums, scaled

    middle = chip_count // 2
    spread_first = lax.all_gather(attended[0], ctx, axis=0)
    spread_first, later = lax.optimization_barrier((spread_first, attended[1]))
    spread_second = lax.all_gather(later, ctx, axis=0)
    pieces = exchange(jnp.concatenate([project(spread_first), table], 1))
    route = pieces[:, group_tokens:].reshape(exp_count, -1)[:, : 2 * chip_count * share]
    route = jnp.sum(
        route.reshape(exp_count, 2, chip_count, 2, half).astype(jnp.float32), axis=1
    )
    sums_first, scaled_first = settle(pieces, 0)
    pieces = project(spread_second)
    pieces, scaled_first = lax.optimization_barrier((pieces, scaled_first))
    sums_second, scaled_second = settle(exchange(pieces), 1)
    plane_first = lax.all_gather(scaled_first, "z", axis=0)
    along, across = plane_step(plane_first, 1), plane_step(plane_first, 2)
    plane_second = lax.all_gather(scaled_second, "z", axis=0)
    along, across, plane_second = lax.optimization_barrier((along, across, plane_second))
    far_a, far_b = plane_step(along[:middle], 2), plane_step(across[middle:], 1)
    far_a, far_b, plane_second = lax.optimization_barrier((far_a, far_b, plane_second))
    blocks = [(plane_first, along, across, far_a, far_b)]
    along, across = plane_step(plane_second, 1), plane_step(plane_second, 2)
    far_a, far_b = plane_step(along[:middle], 2), plane_step(across[middle:], 1)
    blocks.append((plane_second, along, across, far_a, far_b))
    hidden = [sums_first, sums_second]

    weights = (expert_gate[0], expert_up[0], other_gate, other_up)
    outs = []
    for group in range(2):
        route_rows = route[:, :, group].reshape(exp_count, chip_count * half, 1)
        active = run_expert(
            spots, blocks[group], ffn_gain, weights, route_rows, half, 1 - group
        )
        outs.append(
            run_down(
                spots, active, expert_down[0], other_down, hidden[group], exp_count, 1 - group
            )
        )

    first = lax.psum_scatter(
        outs[0].reshape(chip_count, exp_count * half, model_width),
        "z",
        scatter_dimension=0,
        tiled=True,
    )
    first = lax.all_to_all(
        first.reshape(exp_count, half, model_width), "exp", split_axis=0, concat_axis=0, tiled=True
    )
    first = jnp.sum(first.astype(jnp.float32), axis=0).astype(jnp.bfloat16)

    second = lax.all_to_all(outs[1], "exp", split_axis=0, concat_axis=0, tiled=True)
    second = jnp.sum(second.astype(jnp.float32), axis=0).astype(jnp.bfloat16)
    second = lax.psum_scatter(second, "z", scatter_dimension=0, tiled=True)
    return jnp.concatenate([first, second.reshape(half, model_width)], 0)


def specs(ctx):
    in_specs = (
        P(ctx, "exp"),
        P(ctx, "exp"),
        P(ctx, "exp"),
        P(None, ctx, "exp"),
        P(None, None, "exp"),
        P("exp", ctx),
        P((*ctx, "exp"), None),
        P(),
        P((*ctx, "exp"), None),
        P((*ctx, "exp"), None),
        P("exp", None, ctx),
        P("exp", None, ctx),
        P("exp", ctx, None),
    )
    return in_specs, P((*ctx, "exp"), None)


def solution(mesh):
    ctx_count, exp_count = mesh.shape["ctx"], mesh.shape["exp"]

    def run(*args):
        head_count = args[4].shape[2] // exp_count
        share = args[0].shape[0] // (ctx_count * exp_count)
        body, axes, where = general, ("ctx",), mesh
        whole = head_count % ctx_count == 0 and share % 32 == 0 and ctx_count % 4 == 0
        if whole and exp_count.bit_length() == 3 and exp_count.bit_count() == 1:
            split = mesh.devices.reshape(ctx_count // 2, 2, exp_count)
            where = jax.sharding.Mesh(split, ("z", "core", "exp"))
            body, axes = by_heads, ("z", "core")
        in_specs, out_specs = specs(axes)
        return jax.shard_map(
            body, mesh=where, in_specs=in_specs, out_specs=out_specs, check_vma=False
        )(*args)

    return run
```

```python
import functools
import math

import jax
import jax.numpy as jnp
from jax import lax
from jax.experimental import pallas as pl
from jax.experimental.pallas import tpu as pltpu
from jax.sharding import PartitionSpec as P

WINDOW = 512


score_gain = 2.0
norm_eps = 1e-06


def passed_along(block, axis, distance):
    devices = range(lax.axis_size(axis))
    route = [(i - distance, i) for i in devices if i - distance in devices]
    return lax.ppermute(block, axis, route)


def head_norm(matrix, head_width):
    row_count = matrix.shape[0]
    shaped = matrix.reshape(row_count, -1, head_width).astype(jnp.float32)
    scaled = shaped * lax.rsqrt(jnp.mean(shaped * shaped, axis=2, keepdims=True) + norm_eps)
    return scaled.reshape(row_count, -1)


def compress(extended, position_weights, head_width):
    stride_len = position_weights.shape[0] // 2
    head_count = position_weights.shape[1]
    blocks = extended.reshape(-1, stride_len, head_count, head_width).astype(jnp.float32)
    first_half = jnp.einsum(
        "nshd,sh->nhd", blocks[:-1], position_weights[:stride_len], precision=lax.Precision.HIGHEST
    )
    second_half = jnp.einsum(
        "nshd,sh->nhd", blocks[1:], position_weights[stride_len:], precision=lax.Precision.HIGHEST
    )
    return (first_half + second_half).reshape(blocks.shape[0] - 1, head_count * head_width)


def window_attention(query_input, key_input, value_input, gate_logits, comp_weight):
    row_count = query_input.shape[0]
    head_count = comp_weight.shape[2]
    head_width = query_input.shape[1] // head_count
    block_len = comp_weight.shape[1]
    stride_len = block_len // 2
    exp_count = lax.axis_size("exp")
    ctx_index = lax.axis_index("ctx")
    scale = score_gain / math.sqrt(head_width)
    query_norm = head_norm(query_input, head_width).astype(jnp.bfloat16)
    key_norm = head_norm(key_input, head_width).astype(jnp.bfloat16)
    next_keys, next_values = passed_along(
        (key_input[:stride_len], value_input[:stride_len]), "ctx", -1
    )
    comp_keys = head_norm(
        compress(jnp.concatenate([key_input, next_keys], 0), comp_weight[0], head_width), head_width
    ).astype(jnp.bfloat16)
    comp_values = compress(
        jnp.concatenate([value_input, next_values], 0), comp_weight[1], head_width
    ).astype(jnp.bfloat16)
    query_pos = ctx_index * row_count + jnp.arange(row_count, dtype=jnp.int32)
    query_heads = query_norm.reshape(row_count, head_count, head_width)
    part_keys = lax.all_gather(comp_keys, "ctx", axis=0, tiled=True)
    part_values = lax.all_gather(comp_values, "ctx", axis=0, tiled=True)
    part_count = part_keys.shape[0]
    scores = jnp.einsum(
        "thd,nhd->htn",
        query_heads,
        part_keys.reshape(part_count, head_count, head_width),
        preferred_element_type=jnp.float32,
    )
    block_end = jnp.arange(part_count, dtype=jnp.int32) * stride_len + block_len - 1
    visible = block_end[None, :] <= query_pos[:, None]
    weights = jnp.where(visible[None], jnp.exp(scale * scores), 0.0)
    running_total = jnp.sum(weights, axis=2).T
    collected = jnp.einsum(
        "htn,nhd->thd",
        weights.astype(jnp.bfloat16),
        part_values.reshape(part_count, head_count, head_width),
        preferred_element_type=jnp.float32,
    )
    cmp_sum = collected.reshape(row_count, -1)
    no_block = (query_pos < block_len - 1).astype(jnp.float32)
    cmp_out = (
        cmp_sum.reshape(row_count, head_count, head_width)
        / (running_total + no_block[:, None])[:, :, None]
    )
    shift_count = max(1, WINDOW // row_count)
    earlier_keys = []
    earlier_values = []
    for distance in range(shift_count, 0, -1):
        moved_keys, moved_values = passed_along((key_norm, value_input), "ctx", distance)
        earlier_keys.append(moved_keys)
        earlier_values.append(moved_values)
    near_keys = jnp.concatenate(earlier_keys + [key_norm], 0)
    near_values = jnp.concatenate(earlier_values + [value_input], 0)
    key_pos = ctx_index * row_count - WINDOW + jnp.arange(near_keys.shape[0], dtype=jnp.int32)
    near_scores = jnp.einsum(
        "thd,shd->hts",
        query_heads,
        near_keys.reshape(-1, head_count, head_width),
        preferred_element_type=jnp.float32,
    )
    inside = (
        (key_pos[None, :] <= query_pos[:, None])
        & (key_pos[None, :] > query_pos[:, None] - WINDOW)
        & (key_pos[None, :] >= 0)
    )
    near_weights = jnp.where(inside[None], jnp.exp(scale * near_scores), 0.0)
    win_total = jnp.sum(near_weights, axis=2).T
    win_sum = jnp.einsum(
        "hts,shd->thd",
        near_weights.astype(jnp.bfloat16),
        near_values.reshape(-1, head_count, head_width),
        preferred_element_type=jnp.float32,
    )
    win_out = win_sum / win_total[:, :, None]
    branch_gates = jax.nn.sigmoid(gate_logits)
    attended = (
        (branch_gates[0][:, :, None] * cmp_out + branch_gates[1][:, :, None] * win_out)
        .reshape(row_count, -1)
        .astype(jnp.bfloat16)
    )
    return attended


def general(
    query_input,
    key_input,
    value_input,
    gate_logits,
    comp_weight,
    out_proj,
    residual_in,
    ffn_gain,
    expert_ids,
    route_gates,
    expert_gate,
    expert_up,
    expert_down,
):
    row_count = query_input.shape[0]
    ctx_count = lax.axis_size("ctx")
    exp_count = lax.axis_size("exp")
    ctx_index = lax.axis_index("ctx")
    exp_index = lax.axis_index("exp")
    share = row_count // exp_count
    seq_len = row_count * ctx_count
    cols = out_proj.shape[1]
    model_width = cols * ctx_count
    hidden_units = expert_gate.shape[2]
    own_tokens = ctx_count * share

    experts = jnp.arange(exp_count, dtype=jnp.int32)
    route_table = jnp.sum(
        jnp.where(expert_ids[:, :, None] == experts, route_gates[:, :, None], 0.0), axis=1
    )
    route_all = lax.all_gather(route_table, ("ctx", "exp"), axis=0, tiled=True)
    route_own = lax.dynamic_slice_in_dim(route_all, exp_index, 1, 1)
    residual = lax.all_to_all(residual_in, "ctx", split_axis=1, concat_axis=0, tiled=True)

    attention_args = (query_input, key_input, value_input, gate_logits, comp_weight)
    attended = window_attention(*attention_args)
    spread_rows = lax.all_gather(
        attended.reshape(1, exp_count, share, -1), "ctx", axis=0, tiled=True
    )
    partial = jnp.einsum(
        "cerh,hd->ecrd", spread_rows, out_proj, preferred_element_type=jnp.float32
    )
    pieces = lax.all_to_all(
        partial.astype(jnp.bfloat16).reshape(exp_count, own_tokens, cols),
        "exp",
        split_axis=0,
        concat_axis=0,
        tiled=True,
    )
    hidden_state = residual.reshape(own_tokens, cols).astype(jnp.float32) + jnp.sum(
        pieces.astype(jnp.float32), axis=0
    )
    gain = lax.dynamic_slice_in_dim(ffn_gain, ctx_index * cols, cols, 0)
    scaled = (hidden_state * gain).astype(jnp.bfloat16)
    squares = jnp.sum(hidden_state * hidden_state, axis=1)
    rows = lax.all_gather(scaled, ("ctx", "exp"), axis=0, tiled=True)
    rows = rows.reshape(ctx_count, seq_len, cols)
    squares = lax.all_gather(squares, ("ctx", "exp"), axis=0, tiled=True)
    mean_square = jnp.sum(squares.reshape(ctx_count, seq_len), axis=0) / model_width
    inverse = lax.rsqrt(mean_square + norm_eps)[:, None]

    gate_part = inverse * jnp.einsum(
        "ctk,ckf->tf",
        rows,
        expert_gate.reshape(ctx_count, cols, hidden_units),
        preferred_element_type=jnp.float32,
    )
    up_part = inverse * jnp.einsum(
        "ctk,ckf->tf",
        rows,
        expert_up.reshape(ctx_count, cols, hidden_units),
        preferred_element_type=jnp.float32,
    )
    activated = (jax.nn.silu(gate_part) * up_part).astype(jnp.bfloat16)
    activated = jnp.transpose(
        activated.reshape(exp_count, ctx_count, share, hidden_units), (1, 0, 2, 3)
    ).reshape(seq_len, hidden_units)
    outs = jnp.dot(activated, expert_down[0], preferred_element_type=jnp.float32)
    outs = (outs * route_own).astype(jnp.bfloat16)
    outs = outs.reshape(ctx_count, exp_count, share, model_width)
    place = (0, exp_index, 0, ctx_index * cols)
    mine = lax.dynamic_slice(outs, place, (ctx_count, 1, share, cols))
    mine = mine.astype(jnp.float32) + hidden_state.reshape(ctx_count, 1, share, cols)
    outs = lax.dynamic_update_slice(outs, mine.astype(jnp.bfloat16), place)
    return lax.psum_scatter(
        outs.reshape(seq_len, model_width), ("ctx", "exp"), scatter_dimension=0, tiled=True
    )


def high_low(values):
    high = lax.reduce_precision(values, 8, 7)
    return jnp.stack([high, values - high], 0).astype(jnp.bfloat16)


def unit_rows(block):
    return block * lax.rsqrt(jnp.mean(block * block, axis=1, keepdims=True) + norm_eps)


def attend_kernel(row_count, share, block_len, head_width, moved, taps, gates, out, keys, values):
    ctx_count = moved.shape[0]
    own = moved.shape[2] // head_width
    seq_len = row_count * ctx_count
    stride_len = block_len // 2
    part_count = seq_len // stride_len
    scale = score_gain / math.sqrt(head_width)

    def dot(left, right):
        return jnp.dot(left, right, preferred_element_type=jnp.float32)

    def dot_rows(left, right):
        return lax.dot_general(
            left, right, (((1,), (1,)), ((), ())), preferred_element_type=jnp.float32
        )

    def compressed(row, block):
        group = lax.broadcasted_iota(jnp.int32, (part_count, seq_len), 0)
        token_group = lax.broadcasted_iota(jnp.int32, (part_count, seq_len), 1) // stride_len
        band = jnp.where(token_group == group, taps[row : row + 1, :], 0.0)
        band = jnp.where(token_group == group + 1, taps[row + 1 : row + 2, :], band)
        high = band.astype(jnp.bfloat16)
        low = (band - high.astype(jnp.float32)).astype(jnp.bfloat16)
        return dot(high, block) + dot(low, block)

    for head in range(own):
        lanes = slice(head * head_width, (head + 1) * head_width)
        raw_keys = moved[:, row_count : 2 * row_count, lanes].reshape(seq_len, head_width)
        keys[...] = unit_rows(raw_keys.astype(jnp.float32)).astype(jnp.bfloat16)
        raw_values = moved[:, 2 * row_count : 3 * row_count, lanes].reshape(seq_len, head_width)
        values[...] = raw_values
        comp_keys = unit_rows(compressed(2 * head, raw_keys)).astype(jnp.bfloat16)
        comp_values = compressed(2 * (own + head), raw_values).astype(jnp.bfloat16)
        for block in range(ctx_count):
            query = moved[block, 0:row_count, lanes].astype(jnp.float32)
            query = unit_rows(query).astype(jnp.bfloat16)
            base = block * row_count
            rows = slice(base, base + row_count)
            spot = base + lax.broadcasted_iota(jnp.int32, (row_count, part_count), 0)
            ends = lax.broadcasted_iota(jnp.int32, (row_count, part_count), 1) * stride_len
            seen = ends + (block_len - 1) <= spot
            weight = jnp.where(seen, jnp.exp(scale * dot_rows(query, comp_keys)), 0.0)
            total = jnp.sum(weight, axis=1, keepdims=True)
            total = total + jnp.where(spot[:, :1] < block_len - 1, 1.0, 0.0)
            far = dot(weight.astype(jnp.bfloat16), comp_values) / total
            start = max(0, base - WINDOW)
            reach = base + row_count - start
            spot = base + lax.broadcasted_iota(jnp.int32, (row_count, reach), 0)
            key_spot = start + lax.broadcasted_iota(jnp.int32, (row_count, reach), 1)
            seen = (key_spot <= spot) & (key_spot > spot - WINDOW)
            score = dot_rows(query, keys[start : start + reach, :])
            weight = jnp.where(seen, jnp.exp(scale * score), 0.0)
            total = jnp.sum(weight, axis=1, keepdims=True)
            near = dot(weight.astype(jnp.bfloat16), values[start : start + reach, :]) / total
            mixed = (
                gates[rows, head : head + 1] * far
                + gates[rows, own + head : own + head + 1] * near
            ).astype(jnp.bfloat16)
            half = share // 2
            for part in range(row_count // share):
                for group in range(2):
                    target = (part * ctx_count + block) * half
                    base = part * share + group * half
                    out[group, target : target + half, lanes] = mixed[base : base + half]


def attend(moved, taps, gates, row_count, share, block_len, head_width):
    seq_len = moved.shape[0] * row_count
    width = moved.shape[2]
    return pl.pallas_call(
        functools.partial(attend_kernel, row_count, share, block_len, head_width),
        out_shape=jax.ShapeDtypeStruct((2, seq_len // 2, width), jnp.bfloat16),
        scratch_shapes=[
            pltpu.VMEM((seq_len, head_width), jnp.bfloat16),
            pltpu.VMEM((seq_len, head_width), jnp.bfloat16),
        ],
        compiler_params=pltpu.CompilerParams(vmem_limit_bytes=48 * 2**20),
        name="attend",
    )(moved, taps, gates)


def expert_kernel(exp_dim, spots, own, along, across, far_a, far_b, gain, gate_w, up_w, gate_v, up_v, route, out, total, squares):
    step = pl.program_id(0)

    @pl.when(step == 0)
    def _():
        total[...] = jnp.zeros_like(total)
        squares[...] = jnp.zeros_like(squares)

    far = jnp.where(step < pl.num_programs(0) // 2, far_a[0], far_b[0])
    block = jnp.concatenate([own[0], along[0], across[0], far], 0)
    for spot, weight in enumerate((gate_w, up_w, gate_v, up_v)):
        total[spot] += jnp.dot(block, weight[...], preferred_element_type=jnp.float32)
    lane = squares.shape[1]
    collected = squares[...]
    for part in range(block.shape[1] // lane):
        lanes = slice(part * lane, (part + 1) * lane)
        plain = block[:, lanes].astype(jnp.float32) * (1.0 / gain[0, :, lanes])
        collected = collected + plain * plain
    squares[...] = collected

    @pl.when(step == pl.num_programs(0) - 1)
    def _():
        model_width = pl.num_programs(0) * block.shape[1]
        mean_square = jnp.sum(squares[...], axis=1, keepdims=True) / model_width
        inverse = lax.rsqrt(mean_square + norm_eps)
        tokens = own.shape[1]
        for core in range(2):
            gate_part = total[2 * core] * inverse
            up_part = total[2 * core + 1] * inverse
            active = gate_part / (1.0 + jnp.exp(-gate_part)) * up_part
            for source in range(block.shape[0] // tokens):
                spot = pl.ds(jnp.bitwise_xor(spots[1], source), 1)
                piece = active[source * tokens : (source + 1) * tokens] * route[spot][0]
                piece = piece.astype(jnp.bfloat16)
                if exp_dim == 0:
                    out[core, spot] = piece.reshape((1,) + out.shape[2:])
                else:
                    out[core, :, spot] = piece.reshape(out.shape[1], 1, *out.shape[3:])


def run_expert(spots, blocks, gain, weights, route, half, exp_dim):
    chip_count, tokens, wide = blocks[0].shape
    cols = wide // 2
    middle = chip_count // 2
    steps = 2 * chip_count
    units = weights[0].shape[1]
    exp_count = route.shape[0]
    row_total = exp_count * tokens
    lane = math.gcd(128, cols)
    lead = (exp_count, tokens // half) if exp_dim == 0 else (tokens // half, exp_count)
    by_chip = pl.BlockSpec((1, tokens, cols), lambda i, _: (i // 2, 0, i % 2))
    by_cols = pl.BlockSpec((cols, units), lambda i, _: (i, 0))
    out = pl.pallas_call(
        functools.partial(expert_kernel, exp_dim),
        grid_spec=pltpu.PrefetchScalarGridSpec(
            num_scalar_prefetch=1,
            grid=(steps,),
            in_specs=[
                by_chip,
                by_chip,
                by_chip,
                pl.BlockSpec(
                    (1, tokens, cols), lambda i, _: (jnp.minimum(i // 2, middle - 1), 0, i % 2)
                ),
                pl.BlockSpec(
                    (1, tokens, cols), lambda i, _: (jnp.maximum(i // 2 - middle, 0), 0, i % 2)
                ),
                pl.BlockSpec((1, 1, cols), lambda i, _: (i, 0, 0)),
                by_cols,
                by_cols,
                by_cols,
                by_cols,
                pl.BlockSpec((exp_count, tokens, 1), lambda i, _: (0, 0, 0)),
            ],
            out_specs=pl.BlockSpec((2,) + lead + (half, units), lambda i, _: (0, 0, 0, 0, 0)),
            scratch_shapes=[
                pltpu.VMEM((4, row_total, units), jnp.float32),
                pltpu.VMEM((row_total, lane), jnp.float32),
            ],
        ),
        out_shape=jax.ShapeDtypeStruct((2,) + lead + (half, units), jnp.bfloat16),
        compiler_params=pltpu.CompilerParams(vmem_limit_bytes=56 * 2**20),
        cost_estimate=pl.CostEstimate(
            flops=8 * row_total * units * steps * cols,
            bytes_accessed=2 * steps * cols * (row_total + 4 * units),
            transcendentals=2 * row_total * units,
        ),
        name="expert",
    )(spots, *blocks, gain.reshape(steps, 1, cols), *weights, route)
    return out.reshape(2, row_total, units)


def down_kernel(exp_dim, spots, active, down_w, down_v, hidden, out):
    sums = jnp.dot(active[0], down_w[...], preferred_element_type=jnp.float32)
    sums += jnp.dot(active[1], down_v[...], preferred_element_type=jnp.float32)
    out[...] = sums.astype(out.dtype).reshape(out.shape)

    @pl.when(pl.program_id(0) == spots[0])
    def _():
        spot = pl.ds(spots[1], 1)
        place = (spot,) if exp_dim == 0 else (slice(None), spot)
        piece = out[place].astype(jnp.float32)
        out[place] = (piece + hidden[...].reshape(piece.shape)).astype(out.dtype)


def run_down(spots, active, down_w, down_v, hidden, exp_count, exp_dim):
    units, model_width = down_w.shape
    chip_count, half, wide = hidden.shape
    cols = wide
    lead = (exp_count, chip_count) if exp_dim == 0 else (chip_count, exp_count)
    by_cols = pl.BlockSpec((units, cols), lambda i, _: (0, i))
    rows = active.shape[1]
    return pl.pallas_call(
        functools.partial(down_kernel, exp_dim),
        grid_spec=pltpu.PrefetchScalarGridSpec(
            num_scalar_prefetch=1,
            grid=(model_width // cols,),
            in_specs=[
                pl.BlockSpec((2, rows, units), lambda i, _: (0, 0, 0)),
                by_cols,
                by_cols,
                pl.BlockSpec((chip_count, half, cols), lambda i, _: (0, 0, 0)),
            ],
            out_specs=pl.BlockSpec(lead + (half, cols), lambda i, _: (0, 0, 0, i)),
        ),
        out_shape=jax.ShapeDtypeStruct(lead + (half, model_width), jnp.bfloat16),
        compiler_params=pltpu.CompilerParams(vmem_limit_bytes=56 * 2**20),
        cost_estimate=pl.CostEstimate(
            flops=4 * rows * units * model_width,
            bytes_accessed=2 * model_width * (rows + 2 * units),
            transcendentals=0,
        ),
        name="down",
    )(spots, active, down_w, down_v, hidden)


def sibling(block):
    return lax.ppermute(block, "core", [(0, 1), (1, 0)])


def plane_step(block, step):
    count = lax.axis_size("exp")
    return lax.ppermute(block, "exp", [(i, i ^ step) for i in range(count)])


def by_heads(
    query_input,
    key_input,
    value_input,
    gate_logits,
    comp_weight,
    out_proj,
    residual_in,
    ffn_gain,
    expert_ids,
    route_gates,
    expert_gate,
    expert_up,
    expert_down,
):
    row_count = query_input.shape[0]
    head_count = comp_weight.shape[2]
    head_width = query_input.shape[1] // head_count
    block_len = comp_weight.shape[1]
    stride_len = block_len // 2
    ctx = ("z", "core")
    chip_count = lax.axis_size("z")
    ctx_count = chip_count * lax.axis_size("core")
    exp_count = lax.axis_size("exp")
    chip_index = lax.axis_index("z")
    core_index = lax.axis_index("core")
    ctx_index = 2 * chip_index + core_index
    exp_index = lax.axis_index("exp")
    own = head_count // ctx_count
    width = own * head_width
    share = row_count // exp_count
    half = share // 2
    seq_len = row_count * ctx_count
    cols = out_proj.shape[1]
    model_width = cols * ctx_count
    own_tokens = ctx_count * share

    other_gate = sibling(expert_gate[0])
    other_up = sibling(expert_up[0])
    other_down = sibling(expert_down[0])

    experts = jnp.arange(exp_count, dtype=jnp.int32)
    table = jnp.sum(
        jnp.where(expert_ids[:, :, None] == experts, route_gates[:, :, None], 0.0), axis=1
    )
    table = jnp.broadcast_to(high_low(table).reshape(1, -1), (ctx_count, 2 * share * exp_count))
    gates = high_low(jax.nn.sigmoid(gate_logits)).reshape(2, 2, row_count, ctx_count, own)
    gates = jnp.transpose(gates, (3, 0, 1, 2, 4)).reshape(ctx_count, -1)
    side = jnp.concatenate([gates, table], 1)
    side_rows = -(-side.shape[1] // width)
    residual_rows = -(-share * cols // width)
    side_rows += -(3 * row_count + residual_rows + side_rows) % 16
    side = jnp.pad(side, ((0, 0), (0, side_rows * width - side.shape[1])))
    residual = jnp.transpose(residual_in.reshape(share, ctx_count, cols), (1, 0, 2))
    residual = residual.reshape(ctx_count, share * cols)
    residual = jnp.pad(residual, ((0, 0), (0, residual_rows * width - share * cols)))
    heads = [
        jnp.transpose(block.reshape(row_count, ctx_count, width), (1, 0, 2))
        for block in (query_input, key_input, value_input)
    ]
    packed = jnp.concatenate(
        heads
        + [
            residual.reshape(ctx_count, residual_rows, width),
            side.reshape(ctx_count, side_rows, width),
        ],
        1,
    )
    moved = lax.all_to_all(packed, ctx, split_axis=0, concat_axis=0, tiled=True)
    residual = moved[:, 3 * row_count : 3 * row_count + residual_rows].reshape(ctx_count, -1)
    residual = residual[:, : share * cols].reshape(own_tokens, cols)
    side = moved[:, 3 * row_count + residual_rows :].reshape(ctx_count, -1).astype(jnp.float32)
    gate_size = 4 * row_count * own
    gates = side[:, :gate_size].reshape(ctx_count, 2, 2, row_count, own)
    gates = jnp.transpose(gates[:, 0] + gates[:, 1], (0, 2, 1, 3)).reshape(seq_len, 2 * own)
    table = side[:, gate_size : gate_size + 2 * share * exp_count]
    table = table.reshape(chip_count, 2, 2, share, exp_count)
    table = lax.dynamic_index_in_dim(table, core_index, 1, keepdims=False)

    taps = lax.dynamic_slice_in_dim(comp_weight, ctx_index * own, own, 2)
    taps = jnp.transpose(taps.reshape(2, 2, stride_len, own), (0, 3, 1, 2))
    taps = jnp.tile(taps.reshape(4 * own, stride_len), (1, seq_len // stride_len))
    attended = attend(moved, taps, gates, row_count, share, block_len, head_width)

    table = jnp.transpose(table, (3, 1, 0, 2)).reshape(exp_count, -1).astype(jnp.bfloat16)
    table_rows = -(-table.shape[1] // cols)
    table_rows += -table_rows % 16
    table = jnp.pad(table, ((0, 0), (0, table_rows * cols - table.shape[1])))
    table = table.reshape(exp_count, table_rows, cols)
    gain = lax.dynamic_slice_in_dim(ffn_gain, chip_index * 2 * cols, 2 * cols, 0)
    spots = jnp.stack([chip_index, exp_index]).astype(jnp.int32)
    group_tokens = ctx_count * half
    def project(spread_heads):
        pieces = jnp.einsum(
            "csk,ckd->sd",
            spread_heads,
            out_proj.reshape(ctx_count, width, cols),
            preferred_element_type=jnp.float32,
        ).astype(jnp.bfloat16)
        return pieces.reshape(exp_count, group_tokens, cols)

    def exchange(pieces):
        return lax.all_to_all(pieces, "exp", split_axis=0, concat_axis=0, tiled=True)

    def settle(pieces, group):
        sums = jnp.sum(pieces[:, :group_tokens].astype(jnp.float32), axis=0)
        own_rows = residual.reshape(ctx_count, 2, half, cols)[:, group]
        sums = sums.reshape(ctx_count, half, cols) + own_rows.astype(jnp.float32)
        sums = sums.reshape(chip_count, 2, half, cols)
        kept = lax.dynamic_index_in_dim(sums, core_index, 1, keepdims=False)
        given = sibling(lax.dynamic_index_in_dim(sums, 1 - core_index, 1, keepdims=False))
        sums = jnp.concatenate(
            [jnp.where(core_index == 0, kept, given), jnp.where(core_index == 0, given, kept)], 2
        )
        scaled = (sums * gain).astype(jnp.bfloat16).reshape(chip_count * half, 2 * cols)
        return sums, scaled

    middle = chip_count // 2
    spread_first = lax.all_gather(attended[0], ctx, axis=0)
    spread_first, later = lax.optimization_barrier((spread_first, attended[1]))
    spread_second = lax.all_gather(later, ctx, axis=0)
    pieces = exchange(jnp.concatenate([project(spread_first), table], 1))
    route = pieces[:, group_tokens:].reshape(exp_count, -1)[:, : 2 * chip_count * share]
    route = jnp.sum(
        route.reshape(exp_count, 2, chip_count, 2, half).astype(jnp.float32), axis=1
    )
    sums_first, scaled_first = settle(pieces, 0)
    pieces = project(spread_second)
    pieces, scaled_first = lax.optimization_barrier((pieces, scaled_first))
    plane_first = lax.all_gather(scaled_first, "z", axis=0)
    pieces, plane_first = lax.optimization_barrier((exchange(pieces), plane_first))
    sums_second, scaled_second = settle(pieces, 1)
    along, across = plane_step(plane_first, 1), plane_step(plane_first, 2)
    plane_second = lax.all_gather(scaled_second, "z", axis=0)
    along, across, plane_second = lax.optimization_barrier((along, across, plane_second))
    far_a, far_b = plane_step(along[:middle], 2), plane_step(across[middle:], 1)
    far_a, far_b, plane_second = lax.optimization_barrier((far_a, far_b, plane_second))
    weights = (expert_gate[0], expert_up[0], other_gate, other_up)

    def run_group(blocks, sums, group):
        route_rows = route[:, :, group].reshape(exp_count, chip_count * half, 1)
        active = run_expert(spots, blocks, ffn_gain, weights, route_rows, half, 1 - group)
        return run_down(spots, active, expert_down[0], other_down, sums, exp_count, 1 - group)

    first = run_group((plane_first, along, across, far_a, far_b), sums_first, 0)
    along, across = plane_step(plane_second, 1), plane_step(plane_second, 2)
    first, along, across = lax.optimization_barrier((first, along, across))
    far_a, far_b = plane_step(along[:middle], 2), plane_step(across[middle:], 1)
    second = run_group((plane_second, along, across, far_a, far_b), sums_second, 1)

    first = lax.psum_scatter(
        first.reshape(chip_count, exp_count * half, model_width),
        "z",
        scatter_dimension=0,
        tiled=True,
    )
    first = lax.all_to_all(
        first.reshape(exp_count, half, model_width), "exp", split_axis=0, concat_axis=0, tiled=True
    )
    first = jnp.sum(first.astype(jnp.float32), axis=0).astype(jnp.bfloat16)

    second = lax.all_to_all(second, "exp", split_axis=0, concat_axis=0, tiled=True)
    second = jnp.sum(second.astype(jnp.float32), axis=0).astype(jnp.bfloat16)
    second = lax.psum_scatter(second, "z", scatter_dimension=0, tiled=True)
    return jnp.concatenate([first, second.reshape(half, model_width)], 0)


def specs(ctx):
    in_specs = (
        P(ctx, "exp"),
        P(ctx, "exp"),
        P(ctx, "exp"),
        P(None, ctx, "exp"),
        P(None, None, "exp"),
        P("exp", ctx),
        P((*ctx, "exp"), None),
        P(),
        P((*ctx, "exp"), None),
        P((*ctx, "exp"), None),
        P("exp", None, ctx),
        P("exp", None, ctx),
        P("exp", ctx, None),
    )
    return in_specs, P((*ctx, "exp"), None)


def solution(mesh):
    ctx_count, exp_count = mesh.shape["ctx"], mesh.shape["exp"]

    def run(*args):
        head_count = args[4].shape[2] // exp_count
        share = args[0].shape[0] // (ctx_count * exp_count)
        body, axes, where = general, ("ctx",), mesh
        whole = head_count % ctx_count == 0 and share % 32 == 0 and ctx_count % 4 == 0
        if whole and exp_count.bit_length() == 3 and exp_count.bit_count() == 1:
            split = mesh.devices.reshape(ctx_count // 2, 2, exp_count)
            where = jax.sharding.Mesh(split, ("z", "core", "exp"))
            body, axes = by_heads, ("z", "core")
        in_specs, out_specs = specs(axes)
        return jax.shard_map(
            body, mesh=where, in_specs=in_specs, out_specs=out_specs, check_vma=False
        )(*args)

    return run
```

```python
import functools
import math

import jax
import jax.numpy as jnp
from jax import lax
from jax.experimental import pallas as pl
from jax.experimental.pallas import tpu as pltpu
from jax.sharding import PartitionSpec as P

WINDOW = 512


score_gain = 2.0
norm_eps = 1e-06


def passed_along(block, axis, distance):
    devices = range(lax.axis_size(axis))
    route = [(i - distance, i) for i in devices if i - distance in devices]
    return lax.ppermute(block, axis, route)


def head_norm(matrix, head_width):
    row_count = matrix.shape[0]
    shaped = matrix.reshape(row_count, -1, head_width).astype(jnp.float32)
    scaled = shaped * lax.rsqrt(jnp.mean(shaped * shaped, axis=2, keepdims=True) + norm_eps)
    return scaled.reshape(row_count, -1)


def compress(extended, position_weights, head_width):
    stride_len = position_weights.shape[0] // 2
    head_count = position_weights.shape[1]
    blocks = extended.reshape(-1, stride_len, head_count, head_width).astype(jnp.float32)
    first_half = jnp.einsum(
        "nshd,sh->nhd", blocks[:-1], position_weights[:stride_len], precision=lax.Precision.HIGHEST
    )
    second_half = jnp.einsum(
        "nshd,sh->nhd", blocks[1:], position_weights[stride_len:], precision=lax.Precision.HIGHEST
    )
    return (first_half + second_half).reshape(blocks.shape[0] - 1, head_count * head_width)


def window_attention(query_input, key_input, value_input, gate_logits, comp_weight):
    row_count = query_input.shape[0]
    head_count = comp_weight.shape[2]
    head_width = query_input.shape[1] // head_count
    block_len = comp_weight.shape[1]
    stride_len = block_len // 2
    exp_count = lax.axis_size("exp")
    ctx_index = lax.axis_index("ctx")
    scale = score_gain / math.sqrt(head_width)
    query_norm = head_norm(query_input, head_width).astype(jnp.bfloat16)
    key_norm = head_norm(key_input, head_width).astype(jnp.bfloat16)
    next_keys, next_values = passed_along(
        (key_input[:stride_len], value_input[:stride_len]), "ctx", -1
    )
    comp_keys = head_norm(
        compress(jnp.concatenate([key_input, next_keys], 0), comp_weight[0], head_width), head_width
    ).astype(jnp.bfloat16)
    comp_values = compress(
        jnp.concatenate([value_input, next_values], 0), comp_weight[1], head_width
    ).astype(jnp.bfloat16)
    query_pos = ctx_index * row_count + jnp.arange(row_count, dtype=jnp.int32)
    query_heads = query_norm.reshape(row_count, head_count, head_width)
    part_keys = lax.all_gather(comp_keys, "ctx", axis=0, tiled=True)
    part_values = lax.all_gather(comp_values, "ctx", axis=0, tiled=True)
    part_count = part_keys.shape[0]
    scores = jnp.einsum(
        "thd,nhd->htn",
        query_heads,
        part_keys.reshape(part_count, head_count, head_width),
        preferred_element_type=jnp.float32,
    )
    block_end = jnp.arange(part_count, dtype=jnp.int32) * stride_len + block_len - 1
    visible = block_end[None, :] <= query_pos[:, None]
    weights = jnp.where(visible[None], jnp.exp(scale * scores), 0.0)
    running_total = jnp.sum(weights, axis=2).T
    collected = jnp.einsum(
        "htn,nhd->thd",
        weights.astype(jnp.bfloat16),
        part_values.reshape(part_count, head_count, head_width),
        preferred_element_type=jnp.float32,
    )
    cmp_sum = collected.reshape(row_count, -1)
    no_block = (query_pos < block_len - 1).astype(jnp.float32)
    cmp_out = (
        cmp_sum.reshape(row_count, head_count, head_width)
        / (running_total + no_block[:, None])[:, :, None]
    )
    shift_count = max(1, WINDOW // row_count)
    earlier_keys = []
    earlier_values = []
    for distance in range(shift_count, 0, -1):
        moved_keys, moved_values = passed_along((key_norm, value_input), "ctx", distance)
        earlier_keys.append(moved_keys)
        earlier_values.append(moved_values)
    near_keys = jnp.concatenate(earlier_keys + [key_norm], 0)
    near_values = jnp.concatenate(earlier_values + [value_input], 0)
    key_pos = ctx_index * row_count - WINDOW + jnp.arange(near_keys.shape[0], dtype=jnp.int32)
    near_scores = jnp.einsum(
        "thd,shd->hts",
        query_heads,
        near_keys.reshape(-1, head_count, head_width),
        preferred_element_type=jnp.float32,
    )
    inside = (
        (key_pos[None, :] <= query_pos[:, None])
        & (key_pos[None, :] > query_pos[:, None] - WINDOW)
        & (key_pos[None, :] >= 0)
    )
    near_weights = jnp.where(inside[None], jnp.exp(scale * near_scores), 0.0)
    win_total = jnp.sum(near_weights, axis=2).T
    win_sum = jnp.einsum(
        "hts,shd->thd",
        near_weights.astype(jnp.bfloat16),
        near_values.reshape(-1, head_count, head_width),
        preferred_element_type=jnp.float32,
    )
    win_out = win_sum / win_total[:, :, None]
    branch_gates = jax.nn.sigmoid(gate_logits)
    attended = (
        (branch_gates[0][:, :, None] * cmp_out + branch_gates[1][:, :, None] * win_out)
        .reshape(row_count, -1)
        .astype(jnp.bfloat16)
    )
    return attended


def general(
    query_input,
    key_input,
    value_input,
    gate_logits,
    comp_weight,
    out_proj,
    residual_in,
    ffn_gain,
    expert_ids,
    route_gates,
    expert_gate,
    expert_up,
    expert_down,
):
    row_count = query_input.shape[0]
    ctx_count = lax.axis_size("ctx")
    exp_count = lax.axis_size("exp")
    ctx_index = lax.axis_index("ctx")
    exp_index = lax.axis_index("exp")
    share = row_count // exp_count
    seq_len = row_count * ctx_count
    cols = out_proj.shape[1]
    model_width = cols * ctx_count
    hidden_units = expert_gate.shape[2]
    own_tokens = ctx_count * share

    experts = jnp.arange(exp_count, dtype=jnp.int32)
    route_table = jnp.sum(
        jnp.where(expert_ids[:, :, None] == experts, route_gates[:, :, None], 0.0), axis=1
    )
    route_all = lax.all_gather(route_table, ("ctx", "exp"), axis=0, tiled=True)
    route_own = lax.dynamic_slice_in_dim(route_all, exp_index, 1, 1)
    residual = lax.all_to_all(residual_in, "ctx", split_axis=1, concat_axis=0, tiled=True)

    attention_args = (query_input, key_input, value_input, gate_logits, comp_weight)
    attended = window_attention(*attention_args)
    spread_rows = lax.all_gather(
        attended.reshape(1, exp_count, share, -1), "ctx", axis=0, tiled=True
    )
    partial = jnp.einsum(
        "cerh,hd->ecrd", spread_rows, out_proj, preferred_element_type=jnp.float32
    )
    pieces = lax.all_to_all(
        partial.astype(jnp.bfloat16).reshape(exp_count, own_tokens, cols),
        "exp",
        split_axis=0,
        concat_axis=0,
        tiled=True,
    )
    hidden_state = residual.reshape(own_tokens, cols).astype(jnp.float32) + jnp.sum(
        pieces.astype(jnp.float32), axis=0
    )
    gain = lax.dynamic_slice_in_dim(ffn_gain, ctx_index * cols, cols, 0)
    scaled = (hidden_state * gain).astype(jnp.bfloat16)
    squares = jnp.sum(hidden_state * hidden_state, axis=1)
    rows = lax.all_gather(scaled, ("ctx", "exp"), axis=0, tiled=True)
    rows = rows.reshape(ctx_count, seq_len, cols)
    squares = lax.all_gather(squares, ("ctx", "exp"), axis=0, tiled=True)
    mean_square = jnp.sum(squares.reshape(ctx_count, seq_len), axis=0) / model_width
    inverse = lax.rsqrt(mean_square + norm_eps)[:, None]

    gate_part = inverse * jnp.einsum(
        "ctk,ckf->tf",
        rows,
        expert_gate.reshape(ctx_count, cols, hidden_units),
        preferred_element_type=jnp.float32,
    )
    up_part = inverse * jnp.einsum(
        "ctk,ckf->tf",
        rows,
        expert_up.reshape(ctx_count, cols, hidden_units),
        preferred_element_type=jnp.float32,
    )
    activated = (jax.nn.silu(gate_part) * up_part).astype(jnp.bfloat16)
    activated = jnp.transpose(
        activated.reshape(exp_count, ctx_count, share, hidden_units), (1, 0, 2, 3)
    ).reshape(seq_len, hidden_units)
    outs = jnp.dot(activated, expert_down[0], preferred_element_type=jnp.float32)
    outs = (outs * route_own).astype(jnp.bfloat16)
    outs = outs.reshape(ctx_count, exp_count, share, model_width)
    place = (0, exp_index, 0, ctx_index * cols)
    mine = lax.dynamic_slice(outs, place, (ctx_count, 1, share, cols))
    mine = mine.astype(jnp.float32) + hidden_state.reshape(ctx_count, 1, share, cols)
    outs = lax.dynamic_update_slice(outs, mine.astype(jnp.bfloat16), place)
    return lax.psum_scatter(
        outs.reshape(seq_len, model_width), ("ctx", "exp"), scatter_dimension=0, tiled=True
    )


def high_low(values):
    high = lax.reduce_precision(values, 8, 7)
    return jnp.stack([high, values - high], 0).astype(jnp.bfloat16)


def unit_rows(block):
    return block * lax.rsqrt(jnp.mean(block * block, axis=1, keepdims=True) + norm_eps)


def attend_kernel(row_count, share, block_len, head_width, moved, taps, gates, out_a, out_b, keys, values):
    ctx_count = moved.shape[0]
    own = moved.shape[2] // head_width
    seq_len = row_count * ctx_count
    stride_len = block_len // 2
    part_count = seq_len // stride_len
    scale = score_gain / math.sqrt(head_width)

    def dot(left, right):
        return jnp.dot(left, right, preferred_element_type=jnp.float32)

    def dot_rows(left, right):
        return lax.dot_general(
            left, right, (((1,), (1,)), ((), ())), preferred_element_type=jnp.float32
        )

    def compressed(row, block):
        group = lax.broadcasted_iota(jnp.int32, (part_count, seq_len), 0)
        token_group = lax.broadcasted_iota(jnp.int32, (part_count, seq_len), 1) // stride_len
        band = jnp.where(token_group == group, taps[row : row + 1, :], 0.0)
        band = jnp.where(token_group == group + 1, taps[row + 1 : row + 2, :], band)
        high = band.astype(jnp.bfloat16)
        low = (band - high.astype(jnp.float32)).astype(jnp.bfloat16)
        return dot(high, block) + dot(low, block)

    for head in range(own):
        lanes = slice(head * head_width, (head + 1) * head_width)
        raw_keys = moved[:, row_count : 2 * row_count, lanes].reshape(seq_len, head_width)
        keys[...] = unit_rows(raw_keys.astype(jnp.float32)).astype(jnp.bfloat16)
        raw_values = moved[:, 2 * row_count : 3 * row_count, lanes].reshape(seq_len, head_width)
        values[...] = raw_values
        comp_keys = unit_rows(compressed(2 * head, raw_keys)).astype(jnp.bfloat16)
        comp_values = compressed(2 * (own + head), raw_values).astype(jnp.bfloat16)
        for block in range(ctx_count):
            query = moved[block, 0:row_count, lanes].astype(jnp.float32)
            query = unit_rows(query).astype(jnp.bfloat16)
            base = block * row_count
            rows = slice(base, base + row_count)
            spot = base + lax.broadcasted_iota(jnp.int32, (row_count, part_count), 0)
            ends = lax.broadcasted_iota(jnp.int32, (row_count, part_count), 1) * stride_len
            seen = ends + (block_len - 1) <= spot
            weight = jnp.where(seen, jnp.exp(scale * dot_rows(query, comp_keys)), 0.0)
            total = jnp.sum(weight, axis=1, keepdims=True)
            total = total + jnp.where(spot[:, :1] < block_len - 1, 1.0, 0.0)
            far = dot(weight.astype(jnp.bfloat16), comp_values) / total
            start = max(0, base - WINDOW)
            reach = base + row_count - start
            spot = base + lax.broadcasted_iota(jnp.int32, (row_count, reach), 0)
            key_spot = start + lax.broadcasted_iota(jnp.int32, (row_count, reach), 1)
            seen = (key_spot <= spot) & (key_spot > spot - WINDOW)
            score = dot_rows(query, keys[start : start + reach, :])
            weight = jnp.where(seen, jnp.exp(scale * score), 0.0)
            total = jnp.sum(weight, axis=1, keepdims=True)
            near = dot(weight.astype(jnp.bfloat16), values[start : start + reach, :]) / total
            mixed = (
                gates[rows, head : head + 1] * far
                + gates[rows, own + head : own + head + 1] * near
            ).astype(jnp.bfloat16)
            half = share // 2
            for part in range(row_count // share):
                for group in range(2):
                    target = (part * ctx_count + block) * half
                    base = part * share + group * half
                    (out_a, out_b)[group][target : target + half, lanes] = mixed[base : base + half]


def attend(moved, taps, gates, row_count, share, block_len, head_width):
    seq_len = moved.shape[0] * row_count
    width = moved.shape[2]
    return pl.pallas_call(
        functools.partial(attend_kernel, row_count, share, block_len, head_width),
        out_shape=[jax.ShapeDtypeStruct((seq_len // 2, width), jnp.bfloat16)] * 2,
        scratch_shapes=[
            pltpu.VMEM((seq_len, head_width), jnp.bfloat16),
            pltpu.VMEM((seq_len, head_width), jnp.bfloat16),
        ],
        compiler_params=pltpu.CompilerParams(vmem_limit_bytes=48 * 2**20),
        name="attend",
    )(moved, taps, gates)


def project_kernel(spots, left_a, left_b, proj_a, proj_b, table, out, total):
    step = pl.program_id(0)
    sums = jnp.dot(left_a[0], proj_a[0], preferred_element_type=jnp.float32)
    sums += jnp.dot(left_b[0], proj_b[0], preferred_element_type=jnp.float32)

    @pl.when(step == 0)
    def _():
        total[...] = sums

    @pl.when(step > 0)
    def _():
        total[...] += sums

    @pl.when(step == pl.num_programs(0) - 1)
    def _():
        exp_count = out.shape[0]
        tokens = total.shape[0] // exp_count
        for spot in range(exp_count):
            rows = total[spot * tokens : (spot + 1) * tokens]
            out[spot, :tokens] = rows.astype(jnp.bfloat16)
            if out.shape[1] > tokens:
                out[spot, tokens:] = table[spot]


def run_project(spots, left_a, left_b, paired, proj, table, exp_count, extra):
    tokens, width = left_a.shape[1:]
    cols = proj.shape[2]
    steps = proj.shape[0] // 2
    rows = tokens // exp_count + (table.shape[1] if extra else 0)
    if paired:
        maps = [lambda i, s: (2 * i, 0, 0), lambda i, s: (2 * i + 1, 0, 0)] * 2
    else:
        maps = [lambda i, s: (i, 0, 0)] * 2
        maps += [lambda i, s: (2 * i + s[0], 0, 0), lambda i, s: (2 * i + 1 - s[0], 0, 0)]
    return pl.pallas_call(
        project_kernel,
        grid_spec=pltpu.PrefetchScalarGridSpec(
            num_scalar_prefetch=1,
            grid=(steps,),
            in_specs=[
                pl.BlockSpec((1, tokens, width), maps[0]),
                pl.BlockSpec((1, tokens, width), maps[1]),
                pl.BlockSpec((1, width, cols), maps[2]),
                pl.BlockSpec((1, width, cols), maps[3]),
                pl.BlockSpec(table.shape, lambda i, s: (0, 0, 0)),
            ],
            out_specs=pl.BlockSpec((exp_count, rows, cols), lambda i, s: (0, 0, 0)),
            scratch_shapes=[pltpu.VMEM((tokens, cols), jnp.float32)],
        ),
        out_shape=jax.ShapeDtypeStruct((exp_count, rows, cols), jnp.bfloat16),
        compiler_params=pltpu.CompilerParams(vmem_limit_bytes=40 * 2**20),
        cost_estimate=pl.CostEstimate(
            flops=4 * tokens * width * cols * steps,
            bytes_accessed=4 * steps * width * (tokens + cols) + 2 * exp_count * rows * cols,
            transcendentals=0,
        ),
        name="project",
    )(spots, left_a, left_b, proj, proj, table)


def expert_kernel(exp_dim, spots, own, along, across, far_a, far_b, gain, gate_w, up_w, gate_v, up_v, route, out, total, squares):
    step = pl.program_id(0)

    @pl.when(step == 0)
    def _():
        total[...] = jnp.zeros_like(total)
        squares[...] = jnp.zeros_like(squares)

    far = jnp.where(step < pl.num_programs(0) // 2, far_a[0], far_b[0])
    block = jnp.concatenate([own[0], along[0], across[0], far], 0)
    for spot, weight in enumerate((gate_w, up_w, gate_v, up_v)):
        total[spot] += jnp.dot(block, weight[...], preferred_element_type=jnp.float32)
    lane = squares.shape[1]
    collected = squares[...]
    for part in range(block.shape[1] // lane):
        lanes = slice(part * lane, (part + 1) * lane)
        plain = block[:, lanes].astype(jnp.float32) * (1.0 / gain[0, :, lanes])
        collected = collected + plain * plain
    squares[...] = collected

    @pl.when(step == pl.num_programs(0) - 1)
    def _():
        model_width = pl.num_programs(0) * block.shape[1]
        mean_square = jnp.sum(squares[...], axis=1, keepdims=True) / model_width
        inverse = lax.rsqrt(mean_square + norm_eps)
        tokens = own.shape[1]
        for core in range(2):
            gate_part = total[2 * core] * inverse
            up_part = total[2 * core + 1] * inverse
            active = gate_part / (1.0 + jnp.exp(-gate_part)) * up_part
            for source in range(block.shape[0] // tokens):
                spot = pl.ds(jnp.bitwise_xor(spots[1], source), 1)
                piece = active[source * tokens : (source + 1) * tokens] * route[spot][0]
                piece = piece.astype(jnp.bfloat16)
                if exp_dim == 0:
                    out[core, source] = piece.reshape(out.shape[2:])
                else:
                    out[core, :, spot] = piece.reshape(out.shape[1], 1, *out.shape[3:])


def run_expert(spots, blocks, gain, weights, route, half, exp_dim):
    chip_count, tokens, wide = blocks[0].shape
    cols = wide
    middle = chip_count // 2
    steps = chip_count
    units = weights[0].shape[1]
    exp_count = route.shape[0]
    row_total = exp_count * tokens
    lane = math.gcd(128, cols)
    lead = (exp_count, tokens // half) if exp_dim == 0 else (tokens // half, exp_count)
    by_chip = pl.BlockSpec((1, tokens, cols), lambda i, _: (i, 0, 0))
    by_cols = pl.BlockSpec((cols, units), lambda i, _: (i, 0))
    out = pl.pallas_call(
        functools.partial(expert_kernel, exp_dim),
        grid_spec=pltpu.PrefetchScalarGridSpec(
            num_scalar_prefetch=1,
            grid=(steps,),
            in_specs=[
                by_chip,
                by_chip,
                by_chip,
                pl.BlockSpec(
                    (1, tokens, cols), lambda i, _: (jnp.minimum(i, middle - 1), 0, 0)
                ),
                pl.BlockSpec(
                    (1, tokens, cols), lambda i, _: (jnp.maximum(i - middle, 0), 0, 0)
                ),
                pl.BlockSpec((1, 1, cols), lambda i, _: (i, 0, 0)),
                by_cols,
                by_cols,
                by_cols,
                by_cols,
                pl.BlockSpec((exp_count, tokens, 1), lambda i, _: (0, 0, 0)),
            ],
            out_specs=pl.BlockSpec((2,) + lead + (half, units), lambda i, _: (0, 0, 0, 0, 0)),
            scratch_shapes=[
                pltpu.VMEM((4, row_total, units), jnp.float32),
                pltpu.VMEM((row_total, lane), jnp.float32),
            ],
        ),
        out_shape=jax.ShapeDtypeStruct((2,) + lead + (half, units), jnp.bfloat16),
        compiler_params=pltpu.CompilerParams(vmem_limit_bytes=56 * 2**20),
        cost_estimate=pl.CostEstimate(
            flops=8 * row_total * units * steps * cols,
            bytes_accessed=2 * steps * cols * (row_total + 4 * units),
            transcendentals=2 * row_total * units,
        ),
        name="expert",
    )(spots, *blocks, gain.reshape(steps, 1, cols), *weights, route)
    return out.reshape(2, row_total, units)


def down_kernel(start, spots, active, down_w, down_v, hidden, *outs):
    sums = jnp.dot(active[0], down_w[...], preferred_element_type=jnp.float32)
    sums += jnp.dot(active[1], down_v[...], preferred_element_type=jnp.float32)
    sums = sums.astype(jnp.bfloat16)
    kept = outs[0]
    if len(outs) == 1:
        kept[...] = sums.reshape(kept.shape)
    else:
        tokens = sums.shape[0] // len(outs)
        for source, out in enumerate(outs):
            out[...] = sums[source * tokens : (source + 1) * tokens].reshape(out.shape)

    @pl.when(pl.program_id(0) + start == spots[0])
    def _():
        place = (slice(None), pl.ds(spots[1], 1)) if len(outs) == 1 else ...
        piece = kept[place].astype(jnp.float32)
        kept[place] = (piece + hidden[...].reshape(piece.shape)).astype(kept.dtype)


def run_down(spots, active, down_w, down_v, hidden, exp_count, start, stop):
    units = down_w.shape[0]
    chip_count, half, cols = hidden.shape
    rows = active.shape[1]
    whole = stop - start == chip_count
    lead = (chip_count, exp_count) if whole else (chip_count,)
    zeros = (0,) * len(lead + (half,))
    by_cols = pl.BlockSpec((units, cols), lambda i, _: (0, i + start))
    count = 1 if whole else exp_count
    shape = lead + (half, (stop - start) * cols)
    return pl.pallas_call(
        functools.partial(down_kernel, start),
        grid_spec=pltpu.PrefetchScalarGridSpec(
            num_scalar_prefetch=1,
            grid=(stop - start,),
            in_specs=[
                pl.BlockSpec((2, rows, units), lambda i, _: (0, 0, 0)),
                by_cols,
                by_cols,
                pl.BlockSpec((chip_count, half, cols), lambda i, _: (0, 0, 0)),
            ],
            out_specs=[pl.BlockSpec(lead + (half, cols), lambda i, _: (*zeros, i))] * count,
        ),
        out_shape=[jax.ShapeDtypeStruct(shape, jnp.bfloat16)] * count,
        compiler_params=pltpu.CompilerParams(vmem_limit_bytes=56 * 2**20),
        cost_estimate=pl.CostEstimate(
            flops=4 * rows * units * cols * (stop - start),
            bytes_accessed=2 * cols * (stop - start) * (rows + 2 * units),
            transcendentals=0,
        ),
        name="down",
    )(spots, active, down_w, down_v, hidden)


def sibling(block):
    return lax.ppermute(block, "core", [(0, 1), (1, 0)])


def plane_step(block, step):
    count = lax.axis_size("exp")
    return lax.ppermute(block, "exp", [(i, i ^ step) for i in range(count)])


def by_heads(
    query_input,
    key_input,
    value_input,
    gate_logits,
    comp_weight,
    out_proj,
    residual_in,
    ffn_gain,
    expert_ids,
    route_gates,
    expert_gate,
    expert_up,
    expert_down,
):
    row_count = query_input.shape[0]
    head_count = comp_weight.shape[2]
    head_width = query_input.shape[1] // head_count
    block_len = comp_weight.shape[1]
    stride_len = block_len // 2
    ctx = ("z", "core")
    chip_count = lax.axis_size("z")
    ctx_count = chip_count * lax.axis_size("core")
    exp_count = lax.axis_size("exp")
    chip_index = lax.axis_index("z")
    core_index = lax.axis_index("core")
    ctx_index = 2 * chip_index + core_index
    exp_index = lax.axis_index("exp")
    own = head_count // ctx_count
    width = own * head_width
    share = row_count // exp_count
    half = share // 2
    seq_len = row_count * ctx_count
    cols = out_proj.shape[1]
    model_width = cols * ctx_count
    own_tokens = ctx_count * share

    other_gate = sibling(expert_gate[0])
    other_up = sibling(expert_up[0])
    other_down = sibling(expert_down[0])

    experts = jnp.arange(exp_count, dtype=jnp.int32)
    table = jnp.sum(
        jnp.where(expert_ids[:, :, None] == experts, route_gates[:, :, None], 0.0), axis=1
    )
    table = jnp.broadcast_to(high_low(table).reshape(1, -1), (ctx_count, 2 * share * exp_count))
    gates = high_low(jax.nn.sigmoid(gate_logits)).reshape(2, 2, row_count, ctx_count, own)
    gates = jnp.transpose(gates, (3, 0, 1, 2, 4)).reshape(ctx_count, -1)
    side = jnp.concatenate([gates, table], 1)
    side_rows = -(-side.shape[1] // width)
    residual_rows = -(-share * cols // width)
    side_rows += -(3 * row_count + residual_rows + side_rows) % 16
    side = jnp.pad(side, ((0, 0), (0, side_rows * width - side.shape[1])))
    residual = jnp.transpose(residual_in.reshape(share, ctx_count, cols), (1, 0, 2))
    residual = residual.reshape(ctx_count, share * cols)
    residual = jnp.pad(residual, ((0, 0), (0, residual_rows * width - share * cols)))
    heads = [
        jnp.transpose(block.reshape(row_count, ctx_count, width), (1, 0, 2))
        for block in (query_input, key_input, value_input)
    ]
    packed = jnp.concatenate(
        heads
        + [
            residual.reshape(ctx_count, residual_rows, width),
            side.reshape(ctx_count, side_rows, width),
        ],
        1,
    )
    moved = lax.all_to_all(packed, ctx, split_axis=0, concat_axis=0, tiled=True)
    residual = moved[:, 3 * row_count : 3 * row_count + residual_rows].reshape(ctx_count, -1)
    residual = residual[:, : share * cols].reshape(own_tokens, cols)
    side = moved[:, 3 * row_count + residual_rows :].reshape(ctx_count, -1).astype(jnp.float32)
    gate_size = 4 * row_count * own
    gates = side[:, :gate_size].reshape(ctx_count, 2, 2, row_count, own)
    gates = jnp.transpose(gates[:, 0] + gates[:, 1], (0, 2, 1, 3)).reshape(seq_len, 2 * own)
    table = side[:, gate_size : gate_size + 2 * share * exp_count]
    table = table.reshape(chip_count, 2, 2, share, exp_count)
    table = lax.dynamic_index_in_dim(table, core_index, 1, keepdims=False)

    taps = lax.dynamic_slice_in_dim(comp_weight, ctx_index * own, own, 2)
    taps = jnp.transpose(taps.reshape(2, 2, stride_len, own), (0, 3, 1, 2))
    taps = jnp.tile(taps.reshape(4 * own, stride_len), (1, seq_len // stride_len))
    attended = attend(moved, taps, gates, row_count, share, block_len, head_width)

    table = jnp.transpose(table, (3, 1, 0, 2)).reshape(exp_count, -1).astype(jnp.bfloat16)
    table_rows = -(-table.shape[1] // cols)
    table_rows += -table_rows % 16
    table = jnp.pad(table, ((0, 0), (0, table_rows * cols - table.shape[1])))
    table = table.reshape(exp_count, table_rows, cols)
    gain = lax.dynamic_slice_in_dim(ffn_gain, chip_index * 2 * cols, 2 * cols, 0)
    spots = jnp.stack([chip_index, exp_index]).astype(jnp.int32)
    group_tokens = ctx_count * half
    def exchange(pieces):
        return lax.all_to_all(pieces, "exp", split_axis=0, concat_axis=0, tiled=True)

    def settle(pieces, group):
        sums = jnp.sum(pieces[:, :group_tokens].astype(jnp.float32), axis=0)
        own_rows = residual.reshape(ctx_count, 2, half, cols)[:, group]
        sums = sums.reshape(ctx_count, half, cols) + own_rows.astype(jnp.float32)
        sums = sums.reshape(chip_count, 2, half, cols)
        kept = lax.dynamic_index_in_dim(sums, core_index, 1, keepdims=False)
        given = sibling(lax.dynamic_index_in_dim(sums, 1 - core_index, 1, keepdims=False))
        sums = jnp.concatenate(
            [jnp.where(core_index == 0, kept, given), jnp.where(core_index == 0, given, kept)], 2
        )
        scaled = (sums * gain).astype(jnp.bfloat16).reshape(chip_count * half, 2 * cols)
        return sums, scaled

    middle = chip_count // 2
    proj = out_proj.reshape(ctx_count, width, cols)
    core_spot = core_index.astype(jnp.int32).reshape(1)
    spread_first = lax.all_gather(attended[0], "z", axis=0)
    spread_other = sibling(spread_first)
    spread_first, later = lax.optimization_barrier((spread_first, attended[1]))
    spread_second = lax.all_gather(later, ctx, axis=0)
    pieces = exchange(
        run_project(core_spot, spread_first, spread_other, False, proj, table, exp_count, True)
    )
    route = pieces[:, group_tokens:].reshape(exp_count, -1)[:, : 2 * chip_count * share]
    route = jnp.sum(
        route.reshape(exp_count, 2, chip_count, 2, half).astype(jnp.float32), axis=1
    )
    sums_first, scaled_first = settle(pieces, 0)
    pieces = run_project(
        core_spot, spread_second, spread_second, True, proj, table, exp_count, False
    )
    pieces, scaled_first = lax.optimization_barrier((pieces, scaled_first))
    plane_first = lax.all_gather(scaled_first, "z", axis=0)
    pieces, plane_first = lax.optimization_barrier((exchange(pieces), plane_first))
    sums_second, scaled_second = settle(pieces, 1)
    along, across = plane_step(plane_first, 1), plane_step(plane_first, 2)
    plane_second = lax.all_gather(scaled_second, "z", axis=0)
    along, across, plane_second = lax.optimization_barrier((along, across, plane_second))
    far_a, far_b = plane_step(along[:middle], 2), plane_step(across[middle:], 1)
    far_a, far_b, plane_second = lax.optimization_barrier((far_a, far_b, plane_second))
    weights = (expert_gate[0], expert_up[0], other_gate, other_up)

    def run_active(blocks, group):
        route_rows = route[:, :, group].reshape(exp_count, chip_count * half, 1)
        return run_expert(spots, blocks, ffn_gain, weights, route_rows, half, 1 - group)

    def run_outs(active, sums, start, stop):
        return run_down(
            spots, active, expert_down[0], other_down, sums, exp_count, start, stop
        )

    active = run_active((plane_first, along, across, far_a, far_b), 0)
    (first,) = run_outs(active, sums_first, 0, chip_count)
    along, across = plane_step(plane_second, 1), plane_step(plane_second, 2)
    first, along, across = lax.optimization_barrier((first, along, across))
    far_a, far_b = plane_step(along[:middle], 2), plane_step(across[middle:], 1)

    first = lax.psum_scatter(
        first.reshape(chip_count, exp_count * half, model_width),
        "z",
        scatter_dimension=0,
        tiled=True,
    )
    active = run_active((plane_second, along, across, far_a, far_b), 1)

    sides = []
    for start, stop in ((0, middle), (middle, chip_count)):
        own, *given = run_outs(active, sums_second, start, stop)
        total = own.astype(jnp.float32)
        for step, block in enumerate(given, 1):
            total = total + plane_step(block, step).astype(jnp.float32)
        sides.append(total.astype(jnp.bfloat16))
    second = jnp.concatenate(sides, 2)
    second, first = lax.optimization_barrier((second, first))
    second = lax.psum_scatter(second, "z", scatter_dimension=0, tiled=True)
    first = lax.all_to_all(
        first.reshape(exp_count, half, model_width), "exp", split_axis=0, concat_axis=0, tiled=True
    )
    first = jnp.sum(first.astype(jnp.float32), axis=0).astype(jnp.bfloat16)
    return jnp.concatenate([first, second.reshape(half, model_width)], 0)


def specs(ctx):
    in_specs = (
        P(ctx, "exp"),
        P(ctx, "exp"),
        P(ctx, "exp"),
        P(None, ctx, "exp"),
        P(None, None, "exp"),
        P("exp", ctx),
        P((*ctx, "exp"), None),
        P(),
        P((*ctx, "exp"), None),
        P((*ctx, "exp"), None),
        P("exp", None, ctx),
        P("exp", None, ctx),
        P("exp", ctx, None),
    )
    return in_specs, P((*ctx, "exp"), None)


def solution(mesh):
    ctx_count, exp_count = mesh.shape["ctx"], mesh.shape["exp"]

    def run(*args):
        head_count = args[4].shape[2] // exp_count
        share = args[0].shape[0] // (ctx_count * exp_count)
        body, axes, where = general, ("ctx",), mesh
        whole = head_count % ctx_count == 0 and share % 32 == 0 and ctx_count % 4 == 0
        if whole and exp_count.bit_length() == 3 and exp_count.bit_count() == 1:
            split = mesh.devices.reshape(ctx_count // 2, 2, exp_count)
            where = jax.sharding.Mesh(split, ("z", "core", "exp"))
            body, axes = by_heads, ("z", "core")
        in_specs, out_specs = specs(axes)
        return jax.shard_map(
            body, mesh=where, in_specs=in_specs, out_specs=out_specs, check_vma=False
        )(*args)

    return run
```

```python
import functools
import math

import jax
import jax.numpy as jnp
from jax import lax
from jax.experimental import pallas as pl
from jax.experimental.pallas import tpu as pltpu
from jax.sharding import PartitionSpec as P

WINDOW = 512


score_gain = 2.0
norm_eps = 1e-06


def passed_along(block, axis, distance):
    devices = range(lax.axis_size(axis))
    route = [(i - distance, i) for i in devices if i - distance in devices]
    return lax.ppermute(block, axis, route)


def head_norm(matrix, head_width):
    row_count = matrix.shape[0]
    shaped = matrix.reshape(row_count, -1, head_width).astype(jnp.float32)
    scaled = shaped * lax.rsqrt(jnp.mean(shaped * shaped, axis=2, keepdims=True) + norm_eps)
    return scaled.reshape(row_count, -1)


def compress(extended, position_weights, head_width):
    stride_len = position_weights.shape[0] // 2
    head_count = position_weights.shape[1]
    blocks = extended.reshape(-1, stride_len, head_count, head_width).astype(jnp.float32)
    first_half = jnp.einsum(
        "nshd,sh->nhd", blocks[:-1], position_weights[:stride_len], precision=lax.Precision.HIGHEST
    )
    second_half = jnp.einsum(
        "nshd,sh->nhd", blocks[1:], position_weights[stride_len:], precision=lax.Precision.HIGHEST
    )
    return (first_half + second_half).reshape(blocks.shape[0] - 1, head_count * head_width)


def window_attention(query_input, key_input, value_input, gate_logits, comp_weight):
    row_count = query_input.shape[0]
    head_count = comp_weight.shape[2]
    head_width = query_input.shape[1] // head_count
    block_len = comp_weight.shape[1]
    stride_len = block_len // 2
    exp_count = lax.axis_size("exp")
    ctx_index = lax.axis_index("ctx")
    scale = score_gain / math.sqrt(head_width)
    query_norm = head_norm(query_input, head_width).astype(jnp.bfloat16)
    key_norm = head_norm(key_input, head_width).astype(jnp.bfloat16)
    next_keys, next_values = passed_along(
        (key_input[:stride_len], value_input[:stride_len]), "ctx", -1
    )
    comp_keys = head_norm(
        compress(jnp.concatenate([key_input, next_keys], 0), comp_weight[0], head_width), head_width
    ).astype(jnp.bfloat16)
    comp_values = compress(
        jnp.concatenate([value_input, next_values], 0), comp_weight[1], head_width
    ).astype(jnp.bfloat16)
    query_pos = ctx_index * row_count + jnp.arange(row_count, dtype=jnp.int32)
    query_heads = query_norm.reshape(row_count, head_count, head_width)
    part_keys = lax.all_gather(comp_keys, "ctx", axis=0, tiled=True)
    part_values = lax.all_gather(comp_values, "ctx", axis=0, tiled=True)
    part_count = part_keys.shape[0]
    scores = jnp.einsum(
        "thd,nhd->htn",
        query_heads,
        part_keys.reshape(part_count, head_count, head_width),
        preferred_element_type=jnp.float32,
    )
    block_end = jnp.arange(part_count, dtype=jnp.int32) * stride_len + block_len - 1
    visible = block_end[None, :] <= query_pos[:, None]
    weights = jnp.where(visible[None], jnp.exp(scale * scores), 0.0)
    running_total = jnp.sum(weights, axis=2).T
    collected = jnp.einsum(
        "htn,nhd->thd",
        weights.astype(jnp.bfloat16),
        part_values.reshape(part_count, head_count, head_width),
        preferred_element_type=jnp.float32,
    )
    cmp_sum = collected.reshape(row_count, -1)
    no_block = (query_pos < block_len - 1).astype(jnp.float32)
    cmp_out = (
        cmp_sum.reshape(row_count, head_count, head_width)
        / (running_total + no_block[:, None])[:, :, None]
    )
    shift_count = max(1, WINDOW // row_count)
    earlier_keys = []
    earlier_values = []
    for distance in range(shift_count, 0, -1):
        moved_keys, moved_values = passed_along((key_norm, value_input), "ctx", distance)
        earlier_keys.append(moved_keys)
        earlier_values.append(moved_values)
    near_keys = jnp.concatenate(earlier_keys + [key_norm], 0)
    near_values = jnp.concatenate(earlier_values + [value_input], 0)
    key_pos = ctx_index * row_count - WINDOW + jnp.arange(near_keys.shape[0], dtype=jnp.int32)
    near_scores = jnp.einsum(
        "thd,shd->hts",
        query_heads,
        near_keys.reshape(-1, head_count, head_width),
        preferred_element_type=jnp.float32,
    )
    inside = (
        (key_pos[None, :] <= query_pos[:, None])
        & (key_pos[None, :] > query_pos[:, None] - WINDOW)
        & (key_pos[None, :] >= 0)
    )
    near_weights = jnp.where(inside[None], jnp.exp(scale * near_scores), 0.0)
    win_total = jnp.sum(near_weights, axis=2).T
    win_sum = jnp.einsum(
        "hts,shd->thd",
        near_weights.astype(jnp.bfloat16),
        near_values.reshape(-1, head_count, head_width),
        preferred_element_type=jnp.float32,
    )
    win_out = win_sum / win_total[:, :, None]
    branch_gates = jax.nn.sigmoid(gate_logits)
    attended = (
        (branch_gates[0][:, :, None] * cmp_out + branch_gates[1][:, :, None] * win_out)
        .reshape(row_count, -1)
        .astype(jnp.bfloat16)
    )
    return attended


def general(
    query_input,
    key_input,
    value_input,
    gate_logits,
    comp_weight,
    out_proj,
    residual_in,
    ffn_gain,
    expert_ids,
    route_gates,
    expert_gate,
    expert_up,
    expert_down,
):
    row_count = query_input.shape[0]
    ctx_count = lax.axis_size("ctx")
    exp_count = lax.axis_size("exp")
    ctx_index = lax.axis_index("ctx")
    exp_index = lax.axis_index("exp")
    share = row_count // exp_count
    seq_len = row_count * ctx_count
    cols = out_proj.shape[1]
    model_width = cols * ctx_count
    hidden_units = expert_gate.shape[2]
    own_tokens = ctx_count * share

    experts = jnp.arange(exp_count, dtype=jnp.int32)
    route_table = jnp.sum(
        jnp.where(expert_ids[:, :, None] == experts, route_gates[:, :, None], 0.0), axis=1
    )
    route_all = lax.all_gather(route_table, ("ctx", "exp"), axis=0, tiled=True)
    route_own = lax.dynamic_slice_in_dim(route_all, exp_index, 1, 1)
    residual = lax.all_to_all(residual_in, "ctx", split_axis=1, concat_axis=0, tiled=True)

    attention_args = (query_input, key_input, value_input, gate_logits, comp_weight)
    attended = window_attention(*attention_args)
    spread_rows = lax.all_gather(
        attended.reshape(1, exp_count, share, -1), "ctx", axis=0, tiled=True
    )
    partial = jnp.einsum(
        "cerh,hd->ecrd", spread_rows, out_proj, preferred_element_type=jnp.float32
    )
    pieces = lax.all_to_all(
        partial.astype(jnp.bfloat16).reshape(exp_count, own_tokens, cols),
        "exp",
        split_axis=0,
        concat_axis=0,
        tiled=True,
    )
    hidden_state = residual.reshape(own_tokens, cols).astype(jnp.float32) + jnp.sum(
        pieces.astype(jnp.float32), axis=0
    )
    gain = lax.dynamic_slice_in_dim(ffn_gain, ctx_index * cols, cols, 0)
    scaled = (hidden_state * gain).astype(jnp.bfloat16)
    squares = jnp.sum(hidden_state * hidden_state, axis=1)
    rows = lax.all_gather(scaled, ("ctx", "exp"), axis=0, tiled=True)
    rows = rows.reshape(ctx_count, seq_len, cols)
    squares = lax.all_gather(squares, ("ctx", "exp"), axis=0, tiled=True)
    mean_square = jnp.sum(squares.reshape(ctx_count, seq_len), axis=0) / model_width
    inverse = lax.rsqrt(mean_square + norm_eps)[:, None]

    gate_part = inverse * jnp.einsum(
        "ctk,ckf->tf",
        rows,
        expert_gate.reshape(ctx_count, cols, hidden_units),
        preferred_element_type=jnp.float32,
    )
    up_part = inverse * jnp.einsum(
        "ctk,ckf->tf",
        rows,
        expert_up.reshape(ctx_count, cols, hidden_units),
        preferred_element_type=jnp.float32,
    )
    activated = (jax.nn.silu(gate_part) * up_part).astype(jnp.bfloat16)
    activated = jnp.transpose(
        activated.reshape(exp_count, ctx_count, share, hidden_units), (1, 0, 2, 3)
    ).reshape(seq_len, hidden_units)
    outs = jnp.dot(activated, expert_down[0], preferred_element_type=jnp.float32)
    outs = (outs * route_own).astype(jnp.bfloat16)
    outs = outs.reshape(ctx_count, exp_count, share, model_width)
    place = (0, exp_index, 0, ctx_index * cols)
    mine = lax.dynamic_slice(outs, place, (ctx_count, 1, share, cols))
    mine = mine.astype(jnp.float32) + hidden_state.reshape(ctx_count, 1, share, cols)
    outs = lax.dynamic_update_slice(outs, mine.astype(jnp.bfloat16), place)
    return lax.psum_scatter(
        outs.reshape(seq_len, model_width), ("ctx", "exp"), scatter_dimension=0, tiled=True
    )


def high_low(values):
    high = lax.reduce_precision(values, 8, 7)
    return jnp.stack([high, values - high], 0).astype(jnp.bfloat16)


def unit_rows(block):
    return block * lax.rsqrt(jnp.mean(block * block, axis=1, keepdims=True) + norm_eps)


def attend_kernel(row_count, share, block_len, head_width, moved, taps, gates, out_a, out_b, keys, values):
    ctx_count = moved.shape[0]
    own = moved.shape[2] // head_width
    seq_len = row_count * ctx_count
    stride_len = block_len // 2
    part_count = seq_len // stride_len
    scale = score_gain / math.sqrt(head_width)

    def dot(left, right):
        return jnp.dot(left, right, preferred_element_type=jnp.float32)

    def dot_rows(left, right):
        return lax.dot_general(
            left, right, (((1,), (1,)), ((), ())), preferred_element_type=jnp.float32
        )

    def compressed(row, block):
        group = lax.broadcasted_iota(jnp.int32, (part_count, seq_len), 0)
        token_group = lax.broadcasted_iota(jnp.int32, (part_count, seq_len), 1) // stride_len
        band = jnp.where(token_group == group, taps[row : row + 1, :], 0.0)
        band = jnp.where(token_group == group + 1, taps[row + 1 : row + 2, :], band)
        high = band.astype(jnp.bfloat16)
        low = (band - high.astype(jnp.float32)).astype(jnp.bfloat16)
        return dot(high, block) + dot(low, block)

    for head in range(own):
        lanes = slice(head * head_width, (head + 1) * head_width)
        raw_keys = moved[:, row_count : 2 * row_count, lanes].reshape(seq_len, head_width)
        keys[...] = unit_rows(raw_keys.astype(jnp.float32)).astype(jnp.bfloat16)
        raw_values = moved[:, 2 * row_count : 3 * row_count, lanes].reshape(seq_len, head_width)
        values[...] = raw_values
        comp_keys = unit_rows(compressed(2 * head, raw_keys)).astype(jnp.bfloat16)
        comp_values = compressed(2 * (own + head), raw_values).astype(jnp.bfloat16)
        for block in range(ctx_count):
            query = moved[block, 0:row_count, lanes].astype(jnp.float32)
            query = unit_rows(query).astype(jnp.bfloat16)
            base = block * row_count
            rows = slice(base, base + row_count)
            spot = base + lax.broadcasted_iota(jnp.int32, (row_count, part_count), 0)
            ends = lax.broadcasted_iota(jnp.int32, (row_count, part_count), 1) * stride_len
            seen = ends + (block_len - 1) <= spot
            weight = jnp.where(seen, jnp.exp(scale * dot_rows(query, comp_keys)), 0.0)
            total = jnp.sum(weight, axis=1, keepdims=True)
            total = total + jnp.where(spot[:, :1] < block_len - 1, 1.0, 0.0)
            far = dot(weight.astype(jnp.bfloat16), comp_values) / total
            start = max(0, base - WINDOW)
            reach = base + row_count - start
            spot = base + lax.broadcasted_iota(jnp.int32, (row_count, reach), 0)
            key_spot = start + lax.broadcasted_iota(jnp.int32, (row_count, reach), 1)
            seen = (key_spot <= spot) & (key_spot > spot - WINDOW)
            score = dot_rows(query, keys[start : start + reach, :])
            weight = jnp.where(seen, jnp.exp(scale * score), 0.0)
            total = jnp.sum(weight, axis=1, keepdims=True)
            near = dot(weight.astype(jnp.bfloat16), values[start : start + reach, :]) / total
            mixed = (
                gates[rows, head : head + 1] * far
                + gates[rows, own + head : own + head + 1] * near
            ).astype(jnp.bfloat16)
            half = share // 2
            for part in range(row_count // share):
                for group in range(2):
                    target = (part * ctx_count + block) * half
                    base = part * share + group * half
                    (out_a, out_b)[group][target : target + half, lanes] = mixed[base : base + half]


def attend(moved, taps, gates, row_count, share, block_len, head_width):
    seq_len = moved.shape[0] * row_count
    width = moved.shape[2]
    return pl.pallas_call(
        functools.partial(attend_kernel, row_count, share, block_len, head_width),
        out_shape=[jax.ShapeDtypeStruct((seq_len // 2, width), jnp.bfloat16)] * 2,
        scratch_shapes=[
            pltpu.VMEM((seq_len, head_width), jnp.bfloat16),
            pltpu.VMEM((seq_len, head_width), jnp.bfloat16),
        ],
        compiler_params=pltpu.CompilerParams(vmem_limit_bytes=48 * 2**20),
        name="attend",
    )(moved, taps, gates)


def project_kernel(spots, left_a, left_b, proj_a, proj_b, table, out, total):
    step = pl.program_id(0)
    sums = jnp.dot(left_a[0], proj_a[0], preferred_element_type=jnp.float32)
    sums += jnp.dot(left_b[0], proj_b[0], preferred_element_type=jnp.float32)

    @pl.when(step == 0)
    def _():
        total[...] = sums

    @pl.when(step > 0)
    def _():
        total[...] += sums

    @pl.when(step == pl.num_programs(0) - 1)
    def _():
        exp_count = out.shape[0]
        tokens = total.shape[0] // exp_count
        for spot in range(exp_count):
            rows = total[spot * tokens : (spot + 1) * tokens]
            out[spot, :tokens] = rows.astype(jnp.bfloat16)
            if out.shape[1] > tokens:
                out[spot, tokens:] = table[spot]


def run_project(spots, left_a, left_b, paired, proj, table, exp_count, extra):
    tokens, width = left_a.shape[1:]
    cols = proj.shape[2]
    steps = proj.shape[0] // 2
    rows = tokens // exp_count + (table.shape[1] if extra else 0)
    if paired:
        maps = [lambda i, s: (2 * i, 0, 0), lambda i, s: (2 * i + 1, 0, 0)] * 2
    else:
        maps = [lambda i, s: (i, 0, 0)] * 2
        maps += [lambda i, s: (2 * i + s[0], 0, 0), lambda i, s: (2 * i + 1 - s[0], 0, 0)]
    return pl.pallas_call(
        project_kernel,
        grid_spec=pltpu.PrefetchScalarGridSpec(
            num_scalar_prefetch=1,
            grid=(steps,),
            in_specs=[
                pl.BlockSpec((1, tokens, width), maps[0]),
                pl.BlockSpec((1, tokens, width), maps[1]),
                pl.BlockSpec((1, width, cols), maps[2]),
                pl.BlockSpec((1, width, cols), maps[3]),
                pl.BlockSpec(table.shape, lambda i, s: (0, 0, 0)),
            ],
            out_specs=pl.BlockSpec((exp_count, rows, cols), lambda i, s: (0, 0, 0)),
            scratch_shapes=[pltpu.VMEM((tokens, cols), jnp.float32)],
        ),
        out_shape=jax.ShapeDtypeStruct((exp_count, rows, cols), jnp.bfloat16),
        compiler_params=pltpu.CompilerParams(vmem_limit_bytes=56 * 2**20),
        cost_estimate=pl.CostEstimate(
            flops=4 * tokens * width * cols * steps,
            bytes_accessed=4 * steps * width * (tokens + cols) + 2 * exp_count * rows * cols,
            transcendentals=0,
        ),
        name="project",
    )(spots, left_a, left_b, proj, proj, table)


def expert_kernel(exp_dim, spots, own, along, across, far_a, far_b, gain, gate_w, up_w, gate_v, up_v, route, out, total, squares):
    step = pl.program_id(0)

    @pl.when(step == 0)
    def _():
        total[...] = jnp.zeros_like(total)
        squares[...] = jnp.zeros_like(squares)

    far = jnp.where(step < pl.num_programs(0) // 2, far_a[0], far_b[0])
    block = jnp.concatenate([own[0], along[0], across[0], far], 0)
    for spot, weight in enumerate((gate_w, up_w, gate_v, up_v)):
        total[spot] += jnp.dot(block, weight[...], preferred_element_type=jnp.float32)
    lane = squares.shape[1]
    collected = squares[...]
    for part in range(block.shape[1] // lane):
        lanes = slice(part * lane, (part + 1) * lane)
        plain = block[:, lanes].astype(jnp.float32) * (1.0 / gain[0, :, lanes])
        collected = collected + plain * plain
    squares[...] = collected

    @pl.when(step == pl.num_programs(0) - 1)
    def _():
        model_width = pl.num_programs(0) * block.shape[1]
        mean_square = jnp.sum(squares[...], axis=1, keepdims=True) / model_width
        inverse = lax.rsqrt(mean_square + norm_eps)
        tokens = own.shape[1]
        for core in range(2):
            gate_part = total[2 * core] * inverse
            up_part = total[2 * core + 1] * inverse
            active = gate_part / (1.0 + jnp.exp(-gate_part)) * up_part
            for source in range(block.shape[0] // tokens):
                spot = pl.ds(jnp.bitwise_xor(spots[1], source), 1)
                piece = active[source * tokens : (source + 1) * tokens] * route[spot][0]
                piece = piece.astype(jnp.bfloat16)
                if exp_dim == 0:
                    out[core, source] = piece.reshape(out.shape[2:])
                else:
                    out[core, :, spot] = piece.reshape(out.shape[1], 1, *out.shape[3:])


def run_expert(spots, blocks, gain, weights, route, half, exp_dim):
    chip_count, tokens, wide = blocks[0].shape
    cols = wide
    middle = chip_count // 2
    steps = chip_count
    units = weights[0].shape[1]
    exp_count = route.shape[0]
    row_total = exp_count * tokens
    lane = math.gcd(128, cols)
    lead = (exp_count, tokens // half) if exp_dim == 0 else (tokens // half, exp_count)
    by_chip = pl.BlockSpec((1, tokens, cols), lambda i, _: (i, 0, 0))
    by_cols = pl.BlockSpec((cols, units), lambda i, _: (i, 0))
    out = pl.pallas_call(
        functools.partial(expert_kernel, exp_dim),
        grid_spec=pltpu.PrefetchScalarGridSpec(
            num_scalar_prefetch=1,
            grid=(steps,),
            in_specs=[
                by_chip,
                by_chip,
                by_chip,
                pl.BlockSpec(
                    (1, tokens, cols), lambda i, _: (jnp.minimum(i, middle - 1), 0, 0)
                ),
                pl.BlockSpec(
                    (1, tokens, cols), lambda i, _: (jnp.maximum(i - middle, 0), 0, 0)
                ),
                pl.BlockSpec((1, 1, cols), lambda i, _: (i, 0, 0)),
                by_cols,
                by_cols,
                by_cols,
                by_cols,
                pl.BlockSpec((exp_count, tokens, 1), lambda i, _: (0, 0, 0)),
            ],
            out_specs=pl.BlockSpec((2,) + lead + (half, units), lambda i, _: (0, 0, 0, 0, 0)),
            scratch_shapes=[
                pltpu.VMEM((4, row_total, units), jnp.float32),
                pltpu.VMEM((row_total, lane), jnp.float32),
            ],
        ),
        out_shape=jax.ShapeDtypeStruct((2,) + lead + (half, units), jnp.bfloat16),
        compiler_params=pltpu.CompilerParams(vmem_limit_bytes=56 * 2**20),
        cost_estimate=pl.CostEstimate(
            flops=8 * row_total * units * steps * cols,
            bytes_accessed=2 * steps * cols * (row_total + 4 * units),
            transcendentals=2 * row_total * units,
        ),
        name="expert",
    )(spots, *blocks, gain.reshape(steps, 1, cols), *weights, route)
    return out.reshape(2, row_total, units)


def down_kernel(start, spots, active, down_w, down_v, hidden, *outs):
    sums = jnp.dot(active[0], down_w[...], preferred_element_type=jnp.float32)
    sums += jnp.dot(active[1], down_v[...], preferred_element_type=jnp.float32)
    sums = sums.astype(jnp.bfloat16)
    kept = outs[0]
    if len(outs) == 1:
        kept[...] = sums.reshape(kept.shape)
    else:
        tokens = sums.shape[0] // len(outs)
        for source, out in enumerate(outs):
            out[...] = sums[source * tokens : (source + 1) * tokens].reshape(out.shape)

    @pl.when(pl.program_id(0) + start == spots[0])
    def _():
        place = (slice(None), pl.ds(spots[1], 1)) if len(outs) == 1 else ...
        piece = kept[place].astype(jnp.float32)
        kept[place] = (piece + hidden[...].reshape(piece.shape)).astype(kept.dtype)


def run_down(spots, active, down_w, down_v, hidden, exp_count, start, stop):
    units = down_w.shape[0]
    chip_count, half, cols = hidden.shape
    rows = active.shape[1]
    whole = stop - start == chip_count
    lead = (chip_count, exp_count) if whole else (chip_count,)
    zeros = (0,) * len(lead + (half,))
    by_cols = pl.BlockSpec((units, cols), lambda i, _: (0, i + start))
    count = 1 if whole else exp_count
    shape = lead + (half, (stop - start) * cols)
    return pl.pallas_call(
        functools.partial(down_kernel, start),
        grid_spec=pltpu.PrefetchScalarGridSpec(
            num_scalar_prefetch=1,
            grid=(stop - start,),
            in_specs=[
                pl.BlockSpec((2, rows, units), lambda i, _: (0, 0, 0)),
                by_cols,
                by_cols,
                pl.BlockSpec((chip_count, half, cols), lambda i, _: (0, 0, 0)),
            ],
            out_specs=[pl.BlockSpec(lead + (half, cols), lambda i, _: (*zeros, i))] * count,
        ),
        out_shape=[jax.ShapeDtypeStruct(shape, jnp.bfloat16)] * count,
        compiler_params=pltpu.CompilerParams(vmem_limit_bytes=56 * 2**20),
        cost_estimate=pl.CostEstimate(
            flops=4 * rows * units * cols * (stop - start),
            bytes_accessed=2 * cols * (stop - start) * (rows + 2 * units),
            transcendentals=0,
        ),
        name="down",
    )(spots, active, down_w, down_v, hidden)


def sibling(block):
    return lax.ppermute(block, "core", [(0, 1), (1, 0)])


def plane_step(block, step):
    count = lax.axis_size("exp")
    return lax.ppermute(block, "exp", [(i, i ^ step) for i in range(count)])


def by_heads(
    query_input,
    key_input,
    value_input,
    gate_logits,
    comp_weight,
    out_proj,
    residual_in,
    ffn_gain,
    expert_ids,
    route_gates,
    expert_gate,
    expert_up,
    expert_down,
):
    row_count = query_input.shape[0]
    head_count = comp_weight.shape[2]
    head_width = query_input.shape[1] // head_count
    block_len = comp_weight.shape[1]
    stride_len = block_len // 2
    ctx = ("z", "core")
    chip_count = lax.axis_size("z")
    ctx_count = chip_count * lax.axis_size("core")
    exp_count = lax.axis_size("exp")
    chip_index = lax.axis_index("z")
    core_index = lax.axis_index("core")
    ctx_index = 2 * chip_index + core_index
    exp_index = lax.axis_index("exp")
    own = head_count // ctx_count
    width = own * head_width
    share = row_count // exp_count
    half = share // 2
    seq_len = row_count * ctx_count
    cols = out_proj.shape[1]
    model_width = cols * ctx_count
    own_tokens = ctx_count * share

    other_gate = sibling(expert_gate[0])
    other_up = sibling(expert_up[0])
    other_down = sibling(expert_down[0])

    experts = jnp.arange(exp_count, dtype=jnp.int32)
    table = jnp.sum(
        jnp.where(expert_ids[:, :, None] == experts, route_gates[:, :, None], 0.0), axis=1
    )
    table = jnp.broadcast_to(high_low(table).reshape(1, -1), (ctx_count, 2 * share * exp_count))
    gates = high_low(jax.nn.sigmoid(gate_logits)).reshape(2, 2, row_count, ctx_count, own)
    gates = jnp.transpose(gates, (3, 0, 1, 2, 4)).reshape(ctx_count, -1)
    side = jnp.concatenate([gates, table], 1)
    side_rows = -(-side.shape[1] // width)
    residual_rows = -(-share * cols // width)
    side_rows += -(3 * row_count + residual_rows + side_rows) % 16
    side = jnp.pad(side, ((0, 0), (0, side_rows * width - side.shape[1])))
    residual = jnp.transpose(residual_in.reshape(share, ctx_count, cols), (1, 0, 2))
    residual = residual.reshape(ctx_count, share * cols)
    residual = jnp.pad(residual, ((0, 0), (0, residual_rows * width - share * cols)))
    heads = [
        jnp.transpose(block.reshape(row_count, ctx_count, width), (1, 0, 2))
        for block in (query_input, key_input, value_input)
    ]
    packed = jnp.concatenate(
        heads
        + [
            residual.reshape(ctx_count, residual_rows, width),
            side.reshape(ctx_count, side_rows, width),
        ],
        1,
    )
    moved = lax.all_to_all(packed, ctx, split_axis=0, concat_axis=0, tiled=True)
    residual = moved[:, 3 * row_count : 3 * row_count + residual_rows].reshape(ctx_count, -1)
    residual = residual[:, : share * cols].reshape(own_tokens, cols)
    side = moved[:, 3 * row_count + residual_rows :].reshape(ctx_count, -1).astype(jnp.float32)
    gate_size = 4 * row_count * own
    gates = side[:, :gate_size].reshape(ctx_count, 2, 2, row_count, own)
    gates = jnp.transpose(gates[:, 0] + gates[:, 1], (0, 2, 1, 3)).reshape(seq_len, 2 * own)
    table = side[:, gate_size : gate_size + 2 * share * exp_count]
    table = table.reshape(chip_count, 2, 2, share, exp_count)
    table = lax.dynamic_index_in_dim(table, core_index, 1, keepdims=False)

    taps = lax.dynamic_slice_in_dim(comp_weight, ctx_index * own, own, 2)
    taps = jnp.transpose(taps.reshape(2, 2, stride_len, own), (0, 3, 1, 2))
    taps = jnp.tile(taps.reshape(4 * own, stride_len), (1, seq_len // stride_len))
    attended = attend(moved, taps, gates, row_count, share, block_len, head_width)

    table = jnp.transpose(table, (3, 1, 0, 2)).reshape(exp_count, -1).astype(jnp.bfloat16)
    table_rows = -(-table.shape[1] // cols)
    table_rows += -table_rows % 16
    table = jnp.pad(table, ((0, 0), (0, table_rows * cols - table.shape[1])))
    table = table.reshape(exp_count, table_rows, cols)
    gain = lax.dynamic_slice_in_dim(ffn_gain, chip_index * 2 * cols, 2 * cols, 0)
    spots = jnp.stack([chip_index, exp_index]).astype(jnp.int32)
    group_tokens = ctx_count * half
    def exchange(pieces):
        return lax.all_to_all(pieces, "exp", split_axis=0, concat_axis=0, tiled=True)

    def settle(pieces, group):
        sums = jnp.sum(pieces[:, :group_tokens].astype(jnp.float32), axis=0)
        own_rows = residual.reshape(ctx_count, 2, half, cols)[:, group]
        sums = sums.reshape(ctx_count, half, cols) + own_rows.astype(jnp.float32)
        sums = sums.reshape(chip_count, 2, half, cols)
        kept = lax.dynamic_index_in_dim(sums, core_index, 1, keepdims=False)
        given = sibling(lax.dynamic_index_in_dim(sums, 1 - core_index, 1, keepdims=False))
        sums = jnp.concatenate(
            [jnp.where(core_index == 0, kept, given), jnp.where(core_index == 0, given, kept)], 2
        )
        scaled = (sums * gain).astype(jnp.bfloat16).reshape(chip_count * half, 2 * cols)
        return sums, scaled

    middle = chip_count // 2
    proj = out_proj.reshape(ctx_count, width, cols)
    core_spot = core_index.astype(jnp.int32).reshape(1)
    spread_first = lax.all_gather(attended[0], "z", axis=0)
    spread_first, other_gate, other_up, other_down = lax.optimization_barrier(
        (spread_first, other_gate, other_up, other_down)
    )
    spread_other = sibling(spread_first)
    spread_first, later = lax.optimization_barrier((spread_first, attended[1]))
    spread_second = lax.all_gather(later, ctx, axis=0)
    pieces = exchange(
        run_project(core_spot, spread_first, spread_other, False, proj, table, exp_count, True)
    )
    route = pieces[:, group_tokens:].reshape(exp_count, -1)[:, : 2 * chip_count * share]
    route = jnp.sum(
        route.reshape(exp_count, 2, chip_count, 2, half).astype(jnp.float32), axis=1
    )
    sums_first, scaled_first = settle(pieces, 0)
    pieces = run_project(
        core_spot, spread_second, spread_second, True, proj, table, exp_count, False
    )
    pieces, sums_first = lax.optimization_barrier((pieces, sums_first))
    wide = 1 << (2 * cols - 1).bit_length()
    padded = jnp.pad(scaled_first, ((0, 0), (0, wide - 2 * cols)))
    plane_first = lax.all_gather(padded, "z", axis=0)[:, :, : 2 * cols]
    pieces, plane_first = lax.optimization_barrier((exchange(pieces), plane_first))
    sums_second, scaled_second = settle(pieces, 1)
    along, across = plane_step(plane_first, 1), plane_step(plane_first, 2)
    plane_second = lax.all_gather(scaled_second, "z", axis=0)
    along, across, plane_second = lax.optimization_barrier((along, across, plane_second))
    far_a, far_b = plane_step(along[:middle], 2), plane_step(across[middle:], 1)
    far_a, far_b, plane_second = lax.optimization_barrier((far_a, far_b, plane_second))
    weights = (expert_gate[0], expert_up[0], other_gate, other_up)

    def run_active(blocks, group):
        route_rows = route[:, :, group].reshape(exp_count, chip_count * half, 1)
        return run_expert(spots, blocks, ffn_gain, weights, route_rows, half, 1 - group)

    def run_outs(active, sums, start, stop):
        return run_down(
            spots, active, expert_down[0], other_down, sums, exp_count, start, stop
        )

    active = run_active((plane_first, along, across, far_a, far_b), 0)
    (first,) = run_outs(active, sums_first, 0, chip_count)
    along, across = plane_step(plane_second, 1), plane_step(plane_second, 2)
    first, along, across = lax.optimization_barrier((first, along, across))
    far_a, far_b = plane_step(along[:middle], 2), plane_step(across[middle:], 1)

    first = lax.psum_scatter(
        first.reshape(chip_count, exp_count * half, model_width),
        "z",
        scatter_dimension=0,
        tiled=True,
    )
    active = run_active((plane_second, along, across, far_a, far_b), 1)

    sides = []
    for start, stop in ((0, middle), (middle, chip_count)):
        own, *given = run_outs(active, sums_second, start, stop)
        total = own.astype(jnp.float32)
        for step, block in enumerate(given, 1):
            total = total + plane_step(block, step).astype(jnp.float32)
        sides.append(total.astype(jnp.bfloat16))
    second = jnp.concatenate(sides, 2)
    second, first = lax.optimization_barrier((second, first))
    second = lax.psum_scatter(second, "z", scatter_dimension=0, tiled=True)
    first = lax.all_to_all(
        first.reshape(exp_count, half, model_width), "exp", split_axis=0, concat_axis=0, tiled=True
    )
    first = jnp.sum(first.astype(jnp.float32), axis=0).astype(jnp.bfloat16)
    return jnp.concatenate([first, second.reshape(half, model_width)], 0)


def specs(ctx):
    in_specs = (
        P(ctx, "exp"),
        P(ctx, "exp"),
        P(ctx, "exp"),
        P(None, ctx, "exp"),
        P(None, None, "exp"),
        P("exp", ctx),
        P((*ctx, "exp"), None),
        P(),
        P((*ctx, "exp"), None),
        P((*ctx, "exp"), None),
        P("exp", None, ctx),
        P("exp", None, ctx),
        P("exp", ctx, None),
    )
    return in_specs, P((*ctx, "exp"), None)


def solution(mesh):
    ctx_count, exp_count = mesh.shape["ctx"], mesh.shape["exp"]

    def run(*args):
        head_count = args[4].shape[2] // exp_count
        share = args[0].shape[0] // (ctx_count * exp_count)
        body, axes, where = general, ("ctx",), mesh
        whole = head_count % ctx_count == 0 and share % 32 == 0 and ctx_count % 4 == 0
        if whole and exp_count.bit_length() == 3 and exp_count.bit_count() == 1:
            split = mesh.devices.reshape(ctx_count // 2, 2, exp_count)
            where = jax.sharding.Mesh(split, ("z", "core", "exp"))
            body, axes = by_heads, ("z", "core")
        in_specs, out_specs = specs(axes)
        return jax.shard_map(
            body, mesh=where, in_specs=in_specs, out_specs=out_specs, check_vma=False
        )(*args)

    return run
```

```python
import functools
import math

import jax
import jax.numpy as jnp
from jax import lax
from jax.experimental import pallas as pl
from jax.experimental.pallas import tpu as pltpu
from jax.sharding import PartitionSpec as P

WINDOW = 512


score_gain = 2.0
norm_eps = 1e-06


def passed_along(block, axis, distance):
    devices = range(lax.axis_size(axis))
    route = [(i - distance, i) for i in devices if i - distance in devices]
    return lax.ppermute(block, axis, route)


def head_norm(matrix, head_width):
    row_count = matrix.shape[0]
    shaped = matrix.reshape(row_count, -1, head_width).astype(jnp.float32)
    scaled = shaped * lax.rsqrt(jnp.mean(shaped * shaped, axis=2, keepdims=True) + norm_eps)
    return scaled.reshape(row_count, -1)


def compress(extended, position_weights, head_width):
    stride_len = position_weights.shape[0] // 2
    head_count = position_weights.shape[1]
    blocks = extended.reshape(-1, stride_len, head_count, head_width).astype(jnp.float32)
    first_half = jnp.einsum(
        "nshd,sh->nhd", blocks[:-1], position_weights[:stride_len], precision=lax.Precision.HIGHEST
    )
    second_half = jnp.einsum(
        "nshd,sh->nhd", blocks[1:], position_weights[stride_len:], precision=lax.Precision.HIGHEST
    )
    return (first_half + second_half).reshape(blocks.shape[0] - 1, head_count * head_width)


def window_attention(query_input, key_input, value_input, gate_logits, comp_weight):
    row_count = query_input.shape[0]
    head_count = comp_weight.shape[2]
    head_width = query_input.shape[1] // head_count
    block_len = comp_weight.shape[1]
    stride_len = block_len // 2
    exp_count = lax.axis_size("exp")
    ctx_index = lax.axis_index("ctx")
    scale = score_gain / math.sqrt(head_width)
    query_norm = head_norm(query_input, head_width).astype(jnp.bfloat16)
    key_norm = head_norm(key_input, head_width).astype(jnp.bfloat16)
    next_keys, next_values = passed_along(
        (key_input[:stride_len], value_input[:stride_len]), "ctx", -1
    )
    comp_keys = head_norm(
        compress(jnp.concatenate([key_input, next_keys], 0), comp_weight[0], head_width), head_width
    ).astype(jnp.bfloat16)
    comp_values = compress(
        jnp.concatenate([value_input, next_values], 0), comp_weight[1], head_width
    ).astype(jnp.bfloat16)
    query_pos = ctx_index * row_count + jnp.arange(row_count, dtype=jnp.int32)
    query_heads = query_norm.reshape(row_count, head_count, head_width)
    part_keys = lax.all_gather(comp_keys, "ctx", axis=0, tiled=True)
    part_values = lax.all_gather(comp_values, "ctx", axis=0, tiled=True)
    part_count = part_keys.shape[0]
    scores = jnp.einsum(
        "thd,nhd->htn",
        query_heads,
        part_keys.reshape(part_count, head_count, head_width),
        preferred_element_type=jnp.float32,
    )
    block_end = jnp.arange(part_count, dtype=jnp.int32) * stride_len + block_len - 1
    visible = block_end[None, :] <= query_pos[:, None]
    weights = jnp.where(visible[None], jnp.exp(scale * scores), 0.0)
    running_total = jnp.sum(weights, axis=2).T
    collected = jnp.einsum(
        "htn,nhd->thd",
        weights.astype(jnp.bfloat16),
        part_values.reshape(part_count, head_count, head_width),
        preferred_element_type=jnp.float32,
    )
    cmp_sum = collected.reshape(row_count, -1)
    no_block = (query_pos < block_len - 1).astype(jnp.float32)
    cmp_out = (
        cmp_sum.reshape(row_count, head_count, head_width)
        / (running_total + no_block[:, None])[:, :, None]
    )
    shift_count = max(1, WINDOW // row_count)
    earlier_keys = []
    earlier_values = []
    for distance in range(shift_count, 0, -1):
        moved_keys, moved_values = passed_along((key_norm, value_input), "ctx", distance)
        earlier_keys.append(moved_keys)
        earlier_values.append(moved_values)
    near_keys = jnp.concatenate(earlier_keys + [key_norm], 0)
    near_values = jnp.concatenate(earlier_values + [value_input], 0)
    key_pos = ctx_index * row_count - WINDOW + jnp.arange(near_keys.shape[0], dtype=jnp.int32)
    near_scores = jnp.einsum(
        "thd,shd->hts",
        query_heads,
        near_keys.reshape(-1, head_count, head_width),
        preferred_element_type=jnp.float32,
    )
    inside = (
        (key_pos[None, :] <= query_pos[:, None])
        & (key_pos[None, :] > query_pos[:, None] - WINDOW)
        & (key_pos[None, :] >= 0)
    )
    near_weights = jnp.where(inside[None], jnp.exp(scale * near_scores), 0.0)
    win_total = jnp.sum(near_weights, axis=2).T
    win_sum = jnp.einsum(
        "hts,shd->thd",
        near_weights.astype(jnp.bfloat16),
        near_values.reshape(-1, head_count, head_width),
        preferred_element_type=jnp.float32,
    )
    win_out = win_sum / win_total[:, :, None]
    branch_gates = jax.nn.sigmoid(gate_logits)
    attended = (
        (branch_gates[0][:, :, None] * cmp_out + branch_gates[1][:, :, None] * win_out)
        .reshape(row_count, -1)
        .astype(jnp.bfloat16)
    )
    return attended


def general(
    query_input,
    key_input,
    value_input,
    gate_logits,
    comp_weight,
    out_proj,
    residual_in,
    ffn_gain,
    expert_ids,
    route_gates,
    expert_gate,
    expert_up,
    expert_down,
):
    row_count = query_input.shape[0]
    ctx_count = lax.axis_size("ctx")
    exp_count = lax.axis_size("exp")
    ctx_index = lax.axis_index("ctx")
    exp_index = lax.axis_index("exp")
    share = row_count // exp_count
    seq_len = row_count * ctx_count
    cols = out_proj.shape[1]
    model_width = cols * ctx_count
    hidden_units = expert_gate.shape[2]
    own_tokens = ctx_count * share

    experts = jnp.arange(exp_count, dtype=jnp.int32)
    route_table = jnp.sum(
        jnp.where(expert_ids[:, :, None] == experts, route_gates[:, :, None], 0.0), axis=1
    )
    route_all = lax.all_gather(route_table, ("ctx", "exp"), axis=0, tiled=True)
    route_own = lax.dynamic_slice_in_dim(route_all, exp_index, 1, 1)
    residual = lax.all_to_all(residual_in, "ctx", split_axis=1, concat_axis=0, tiled=True)

    attention_args = (query_input, key_input, value_input, gate_logits, comp_weight)
    attended = window_attention(*attention_args)
    spread_rows = lax.all_gather(
        attended.reshape(1, exp_count, share, -1), "ctx", axis=0, tiled=True
    )
    partial = jnp.einsum(
        "cerh,hd->ecrd", spread_rows, out_proj, preferred_element_type=jnp.float32
    )
    pieces = lax.all_to_all(
        partial.astype(jnp.bfloat16).reshape(exp_count, own_tokens, cols),
        "exp",
        split_axis=0,
        concat_axis=0,
        tiled=True,
    )
    hidden_state = residual.reshape(own_tokens, cols).astype(jnp.float32) + jnp.sum(
        pieces.astype(jnp.float32), axis=0
    )
    gain = lax.dynamic_slice_in_dim(ffn_gain, ctx_index * cols, cols, 0)
    scaled = (hidden_state * gain).astype(jnp.bfloat16)
    squares = jnp.sum(hidden_state * hidden_state, axis=1)
    rows = lax.all_gather(scaled, ("ctx", "exp"), axis=0, tiled=True)
    rows = rows.reshape(ctx_count, seq_len, cols)
    squares = lax.all_gather(squares, ("ctx", "exp"), axis=0, tiled=True)
    mean_square = jnp.sum(squares.reshape(ctx_count, seq_len), axis=0) / model_width
    inverse = lax.rsqrt(mean_square + norm_eps)[:, None]

    gate_part = inverse * jnp.einsum(
        "ctk,ckf->tf",
        rows,
        expert_gate.reshape(ctx_count, cols, hidden_units),
        preferred_element_type=jnp.float32,
    )
    up_part = inverse * jnp.einsum(
        "ctk,ckf->tf",
        rows,
        expert_up.reshape(ctx_count, cols, hidden_units),
        preferred_element_type=jnp.float32,
    )
    activated = (jax.nn.silu(gate_part) * up_part).astype(jnp.bfloat16)
    activated = jnp.transpose(
        activated.reshape(exp_count, ctx_count, share, hidden_units), (1, 0, 2, 3)
    ).reshape(seq_len, hidden_units)
    outs = jnp.dot(activated, expert_down[0], preferred_element_type=jnp.float32)
    outs = (outs * route_own).astype(jnp.bfloat16)
    outs = outs.reshape(ctx_count, exp_count, share, model_width)
    place = (0, exp_index, 0, ctx_index * cols)
    mine = lax.dynamic_slice(outs, place, (ctx_count, 1, share, cols))
    mine = mine.astype(jnp.float32) + hidden_state.reshape(ctx_count, 1, share, cols)
    outs = lax.dynamic_update_slice(outs, mine.astype(jnp.bfloat16), place)
    return lax.psum_scatter(
        outs.reshape(seq_len, model_width), ("ctx", "exp"), scatter_dimension=0, tiled=True
    )


def high_low(values):
    high = lax.reduce_precision(values, 8, 7)
    return jnp.stack([high, values - high], 0).astype(jnp.bfloat16)


def unit_rows(block):
    return block * lax.rsqrt(jnp.mean(block * block, axis=1, keepdims=True) + norm_eps)


def side_spots(count, own, row_count, share, head_width):
    spots = []
    for piece in range(count):
        first = 3 * row_count + piece // own * share
        lane = piece % own * head_width
        spots.append((slice(first, first + share), slice(lane, lane + head_width)))
    return spots


def pack_kernel(query, key, value, residual, side, out):
    row_count, width = query.shape
    share, head_width = side.shape[1:]
    for spot, block in enumerate((query, key, value)):
        out[0, spot * row_count : (spot + 1) * row_count, :] = block[...]
    count = residual.shape[1] // head_width
    spots = side_spots(count + 1, width // head_width, row_count, share, head_width)
    for piece, (rows, lanes) in enumerate(spots[:-1]):
        out[0, rows, lanes] = residual[:, piece * head_width : (piece + 1) * head_width]
    rows, lanes = spots[-1]
    out[0, rows, lanes] = side[0]


def pack(query, key, value, residual, side, width):
    ctx_count, share, head_width = side.shape
    row_count = query.shape[0]
    cols = residual.shape[1] // ctx_count
    rows = 3 * row_count + (cols // head_width + 1) * head_width // width * share
    heads = pl.BlockSpec((row_count, width), lambda i: (0, i))
    return pl.pallas_call(
        pack_kernel,
        grid=(ctx_count,),
        in_specs=[
            heads,
            heads,
            heads,
            pl.BlockSpec((share, cols), lambda i: (0, i)),
            pl.BlockSpec((1, share, head_width), lambda i: (i, 0, 0)),
        ],
        out_specs=pl.BlockSpec((1, rows, width), lambda i: (i, 0, 0)),
        out_shape=jax.ShapeDtypeStruct((ctx_count, rows, width), jnp.bfloat16),
        compiler_params=pltpu.CompilerParams(vmem_limit_bytes=32 * 2**20),
        name="pack",
    )(query, key, value, residual, side)


def attend_kernel(row_count, share, block_len, head_width, moved, taps, gates, out_a, out_b, keys, values):
    ctx_count = moved.shape[0]
    own = moved.shape[2] // head_width
    seq_len = row_count * ctx_count
    stride_len = block_len // 2
    part_count = seq_len // stride_len
    scale = score_gain / math.sqrt(head_width)

    def dot(left, right):
        return jnp.dot(left, right, preferred_element_type=jnp.float32)

    def dot_rows(left, right):
        return lax.dot_general(
            left, right, (((1,), (1,)), ((), ())), preferred_element_type=jnp.float32
        )

    def compressed(row, block):
        group = lax.broadcasted_iota(jnp.int32, (part_count, seq_len), 0)
        token_group = lax.broadcasted_iota(jnp.int32, (part_count, seq_len), 1) // stride_len
        band = jnp.where(token_group == group, taps[row : row + 1, :], 0.0)
        band = jnp.where(token_group == group + 1, taps[row + 1 : row + 2, :], band)
        high = band.astype(jnp.bfloat16)
        low = (band - high.astype(jnp.float32)).astype(jnp.bfloat16)
        return dot(high, block) + dot(low, block)

    for head in range(own):
        lanes = slice(head * head_width, (head + 1) * head_width)
        raw_keys = moved[:, row_count : 2 * row_count, lanes].reshape(seq_len, head_width)
        keys[...] = unit_rows(raw_keys.astype(jnp.float32)).astype(jnp.bfloat16)
        raw_values = moved[:, 2 * row_count : 3 * row_count, lanes].reshape(seq_len, head_width)
        values[...] = raw_values
        comp_keys = unit_rows(compressed(2 * head, raw_keys)).astype(jnp.bfloat16)
        comp_values = compressed(2 * (own + head), raw_values).astype(jnp.bfloat16)
        for block in range(ctx_count):
            query = moved[block, 0:row_count, lanes].astype(jnp.float32)
            query = unit_rows(query).astype(jnp.bfloat16)
            base = block * row_count
            rows = slice(base, base + row_count)
            spot = base + lax.broadcasted_iota(jnp.int32, (row_count, part_count), 0)
            ends = lax.broadcasted_iota(jnp.int32, (row_count, part_count), 1) * stride_len
            seen = ends + (block_len - 1) <= spot
            weight = jnp.where(seen, jnp.exp(scale * dot_rows(query, comp_keys)), 0.0)
            total = jnp.sum(weight, axis=1, keepdims=True)
            total = total + jnp.where(spot[:, :1] < block_len - 1, 1.0, 0.0)
            far = dot(weight.astype(jnp.bfloat16), comp_values) / total
            start = max(0, base - WINDOW)
            reach = base + row_count - start
            score = dot_rows(query, keys[start : start + reach, :])
            weight = jnp.exp(scale * score)
            edges = []
            for first in range(0, reach, row_count):
                piece = weight[:, first : first + row_count]
                offset = base - start - first
                ahead = lax.broadcasted_iota(jnp.int32, (row_count, row_count), 1)
                ahead = ahead - lax.broadcasted_iota(jnp.int32, (row_count, row_count), 0)
                if offset < row_count:
                    piece = jnp.where(ahead <= offset, piece, 0.0)
                if offset + row_count > WINDOW:
                    piece = jnp.where(ahead > offset - WINDOW, piece, 0.0)
                edges.append(piece)
            weight = jnp.concatenate(edges, 1)
            total = jnp.sum(weight, axis=1, keepdims=True)
            near = dot(weight.astype(jnp.bfloat16), values[start : start + reach, :]) / total
            mixed = (
                gates[rows, head : head + 1] * far
                + gates[rows, own + head : own + head + 1] * near
            ).astype(jnp.bfloat16)
            half = share // 2
            for part in range(row_count // share):
                for group in range(2):
                    target = (part * ctx_count + block) * half
                    base = part * share + group * half
                    (out_a, out_b)[group][target : target + half, lanes] = mixed[base : base + half]


def attend(moved, taps, gates, row_count, share, block_len, head_width):
    seq_len = moved.shape[0] * row_count
    width = moved.shape[2]
    return pl.pallas_call(
        functools.partial(attend_kernel, row_count, share, block_len, head_width),
        out_shape=[jax.ShapeDtypeStruct((seq_len // 2, width), jnp.bfloat16)] * 2,
        scratch_shapes=[
            pltpu.VMEM((seq_len, head_width), jnp.bfloat16),
            pltpu.VMEM((seq_len, head_width), jnp.bfloat16),
        ],
        compiler_params=pltpu.CompilerParams(vmem_limit_bytes=48 * 2**20),
        name="attend",
    )(moved, taps, gates)


def project_kernel(paired, spots, left_a, left_b, proj, table, out, total):
    step = pl.program_id(0)
    first = jnp.logical_or(paired, spots[0] == 0)
    parts = []
    for chip in range(left_a.shape[0]):
        if paired:
            parts += [left_a[chip, 0], left_a[chip, 1]]
        else:
            parts.append(jnp.where(first, left_a[chip, 0], left_b[chip, 0]))
            parts.append(jnp.where(first, left_b[chip, 0], left_a[chip, 0]))
    sums = jnp.dot(jnp.concatenate(parts, 1), proj[...], preferred_element_type=jnp.float32)

    @pl.when(step == 0)
    def _():
        total[...] = sums

    @pl.when(step == pl.num_programs(0) - 1)
    def _():
        exp_count = out.shape[0]
        tokens = total.shape[0] // exp_count
        for spot in range(exp_count):
            rows = slice(spot * tokens, (spot + 1) * tokens)
            out[spot, :tokens] = (total[rows] + sums[rows]).astype(jnp.bfloat16)
            if out.shape[1] > tokens:
                out[spot, tokens:] = table[spot]


def run_project(spots, left_a, left_b, paired, proj, table, exp_count, extra):
    depth, cols = proj.shape
    tokens, width = left_a.shape[1:]
    cores = 2 if paired else 1
    chips = depth // (2 * width)
    left_a = left_a.reshape(chips, cores, tokens, width)
    left_b = left_b.reshape(chips, cores, tokens, width)
    left = pl.BlockSpec((chips // 2, cores, tokens, width), lambda i, _: (i, 0, 0, 0))
    unused = pl.BlockSpec((1, 1, tokens, width), lambda i, _: (0, 0, 0, 0))
    rows = tokens // exp_count + (table.shape[1] if extra else 0)
    return pl.pallas_call(
        functools.partial(project_kernel, paired),
        grid_spec=pltpu.PrefetchScalarGridSpec(
            num_scalar_prefetch=1,
            grid=(2,),
            in_specs=[
                left,
                unused if paired else left,
                pl.BlockSpec((depth // 2, cols), lambda i, _: (i, 0)),
                pl.BlockSpec(table.shape, lambda i, _: (0, 0, 0)),
            ],
            out_specs=pl.BlockSpec((exp_count, rows, cols), lambda i, _: (0, 0, 0)),
            scratch_shapes=[pltpu.VMEM((tokens, cols), jnp.float32)],
        ),
        out_shape=jax.ShapeDtypeStruct((exp_count, rows, cols), jnp.bfloat16),
        compiler_params=pltpu.CompilerParams(vmem_limit_bytes=56 * 2**20),
        cost_estimate=pl.CostEstimate(
            flops=2 * tokens * depth * cols,
            bytes_accessed=2 * depth * (tokens + cols) + 2 * exp_count * rows * cols,
            transcendentals=0,
        ),
        name="project",
    )(spots, left_a, left_b, proj, table)


def expert_kernel(exp_dim, spots, own, along, across, far_a, far_b, gain, gate_w, up_w, gate_v, up_v, route, out, total, squares):
    step = pl.program_id(0)

    @pl.when(step == 0)
    def _():
        total[...] = jnp.zeros_like(total)
        squares[...] = jnp.zeros_like(squares)

    far = jnp.where(step < pl.num_programs(0) // 2, far_a[0], far_b[0])
    block = jnp.concatenate([own[0], along[0], across[0], far], 0)
    for spot, weight in enumerate((gate_w, up_w, gate_v, up_v)):
        total[spot] += jnp.dot(block, weight[...], preferred_element_type=jnp.float32)
    lane = squares.shape[1]
    collected = squares[...]
    for part in range(block.shape[1] // lane):
        lanes = slice(part * lane, (part + 1) * lane)
        plain = block[:, lanes].astype(jnp.float32) * (1.0 / gain[0, :, lanes])
        collected = collected + plain * plain
    squares[...] = collected

    @pl.when(step == pl.num_programs(0) - 1)
    def _():
        model_width = pl.num_programs(0) * block.shape[1]
        mean_square = jnp.sum(squares[...], axis=1, keepdims=True) / model_width
        inverse = lax.rsqrt(mean_square + norm_eps)
        tokens = own.shape[1]
        for core in range(2):
            gate_part = total[2 * core] * inverse
            up_part = total[2 * core + 1] * inverse
            active = gate_part / (1.0 + jnp.exp(-gate_part)) * up_part
            for source in range(block.shape[0] // tokens):
                spot = pl.ds(jnp.bitwise_xor(spots[1], source), 1)
                piece = active[source * tokens : (source + 1) * tokens] * route[spot][0]
                piece = piece.astype(jnp.bfloat16)
                if exp_dim == 0:
                    out[core, source] = piece.reshape(out.shape[2:])
                else:
                    out[core, :, spot] = piece.reshape(out.shape[1], 1, *out.shape[3:])


def run_expert(spots, blocks, gain, weights, route, half, exp_dim):
    chip_count, tokens, wide = blocks[0].shape
    cols = wide
    middle = chip_count // 2
    steps = chip_count
    units = weights[0].shape[1]
    exp_count = route.shape[0]
    row_total = exp_count * tokens
    lane = math.gcd(128, cols)
    lead = (exp_count, tokens // half) if exp_dim == 0 else (tokens // half, exp_count)
    by_chip = pl.BlockSpec((1, tokens, cols), lambda i, _: (i, 0, 0))
    by_cols = pl.BlockSpec((cols, units), lambda i, _: (i, 0))
    out = pl.pallas_call(
        functools.partial(expert_kernel, exp_dim),
        grid_spec=pltpu.PrefetchScalarGridSpec(
            num_scalar_prefetch=1,
            grid=(steps,),
            in_specs=[
                by_chip,
                by_chip,
                by_chip,
                pl.BlockSpec(
                    (1, tokens, cols), lambda i, _: (jnp.minimum(i, middle - 1), 0, 0)
                ),
                pl.BlockSpec(
                    (1, tokens, cols), lambda i, _: (jnp.maximum(i - middle, 0), 0, 0)
                ),
                pl.BlockSpec((1, 1, cols), lambda i, _: (i, 0, 0)),
                by_cols,
                by_cols,
                by_cols,
                by_cols,
                pl.BlockSpec((exp_count, tokens, 1), lambda i, _: (0, 0, 0)),
            ],
            out_specs=pl.BlockSpec((2,) + lead + (half, units), lambda i, _: (0, 0, 0, 0, 0)),
            scratch_shapes=[
                pltpu.VMEM((4, row_total, units), jnp.float32),
                pltpu.VMEM((row_total, lane), jnp.float32),
            ],
        ),
        out_shape=jax.ShapeDtypeStruct((2,) + lead + (half, units), jnp.bfloat16),
        compiler_params=pltpu.CompilerParams(vmem_limit_bytes=56 * 2**20),
        cost_estimate=pl.CostEstimate(
            flops=8 * row_total * units * steps * cols,
            bytes_accessed=2 * steps * cols * (row_total + 4 * units),
            transcendentals=2 * row_total * units,
        ),
        name="expert",
    )(spots, *blocks, gain.reshape(steps, 1, cols), *weights, route)
    return out.reshape(2, row_total, units)


def down_kernel(start, spots, active, down_w, down_v, hidden, *outs):
    left = jnp.concatenate([active[0], active[1]], 1)
    right = jnp.concatenate([down_w[...], down_v[...]], 0)
    sums = jnp.dot(left, right, preferred_element_type=jnp.float32).astype(jnp.bfloat16)
    kept = outs[0]
    if len(outs) == 1:
        kept[...] = sums.reshape(kept.shape)
    else:
        tokens = sums.shape[0] // len(outs)
        for source, out in enumerate(outs):
            out[...] = sums[source * tokens : (source + 1) * tokens].reshape(out.shape)

    @pl.when(pl.program_id(0) + start == spots[0])
    def _():
        place = (slice(None), pl.ds(spots[1], 1)) if len(outs) == 1 else ...
        piece = kept[place].astype(jnp.float32)
        kept[place] = (piece + hidden[...].reshape(piece.shape)).astype(kept.dtype)


def run_down(spots, active, down_w, down_v, hidden, exp_count, start, stop):
    units = down_w.shape[0]
    chip_count, half, cols = hidden.shape
    rows = active.shape[1]
    whole = stop - start == chip_count
    lead = (chip_count, exp_count) if whole else (chip_count,)
    zeros = (0,) * len(lead + (half,))
    by_cols = pl.BlockSpec((units, cols), lambda i, _: (0, i + start))
    count = 1 if whole else exp_count
    shape = lead + (half, (stop - start) * cols)
    return pl.pallas_call(
        functools.partial(down_kernel, start),
        grid_spec=pltpu.PrefetchScalarGridSpec(
            num_scalar_prefetch=1,
            grid=(stop - start,),
            in_specs=[
                pl.BlockSpec((2, rows, units), lambda i, _: (0, 0, 0)),
                by_cols,
                by_cols,
                pl.BlockSpec((chip_count, half, cols), lambda i, _: (0, 0, 0)),
            ],
            out_specs=[pl.BlockSpec(lead + (half, cols), lambda i, _: (*zeros, i))] * count,
        ),
        out_shape=[jax.ShapeDtypeStruct(shape, jnp.bfloat16)] * count,
        compiler_params=pltpu.CompilerParams(vmem_limit_bytes=56 * 2**20),
        cost_estimate=pl.CostEstimate(
            flops=4 * rows * units * cols * (stop - start),
            bytes_accessed=2 * cols * (stop - start) * (rows + 2 * units),
            transcendentals=0,
        ),
        name="down",
    )(spots, active, down_w, down_v, hidden)


def sibling(block):
    return lax.ppermute(block, "core", [(0, 1), (1, 0)])


def plane_step(block, step):
    count = lax.axis_size("exp")
    return lax.ppermute(block, "exp", [(i, i ^ step) for i in range(count)])


def by_heads(
    query_input,
    key_input,
    value_input,
    gate_logits,
    comp_weight,
    out_proj,
    residual_in,
    ffn_gain,
    expert_ids,
    route_gates,
    expert_gate,
    expert_up,
    expert_down,
):
    row_count = query_input.shape[0]
    head_count = comp_weight.shape[2]
    head_width = query_input.shape[1] // head_count
    block_len = comp_weight.shape[1]
    stride_len = block_len // 2
    ctx = ("z", "core")
    chip_count = lax.axis_size("z")
    ctx_count = chip_count * lax.axis_size("core")
    exp_count = lax.axis_size("exp")
    chip_index = lax.axis_index("z")
    core_index = lax.axis_index("core")
    ctx_index = 2 * chip_index + core_index
    exp_index = lax.axis_index("exp")
    own = head_count // ctx_count
    width = own * head_width
    share = row_count // exp_count
    half = share // 2
    seq_len = row_count * ctx_count
    cols = out_proj.shape[1]
    model_width = cols * ctx_count
    own_tokens = ctx_count * share

    other_gate = sibling(expert_gate[0])
    other_up = sibling(expert_up[0])
    other_down = sibling(expert_down[0])

    experts = jnp.arange(exp_count, dtype=jnp.int32)
    table = jnp.sum(
        jnp.where(expert_ids[:, :, None] == experts, route_gates[:, :, None], 0.0), axis=1
    )
    table = jnp.broadcast_to(high_low(table).reshape(1, -1), (ctx_count, 2 * share * exp_count))
    gates = high_low(jax.nn.sigmoid(gate_logits)).reshape(2, 2, row_count, ctx_count, own)
    gates = jnp.transpose(gates, (3, 0, 1, 2, 4)).reshape(ctx_count, -1)
    side = jnp.concatenate([gates, table], 1)
    side = jnp.pad(side, ((0, 0), (0, share * head_width - side.shape[1])))
    side = side.reshape(ctx_count, share, head_width)
    packed = pack(query_input, key_input, value_input, residual_in, side, width)
    moved = lax.all_to_all(packed, ctx, split_axis=0, concat_axis=0, tiled=True)
    spots = side_spots(cols // head_width + 1, own, row_count, share, head_width)
    parts = [moved[:, rows, lanes] for rows, lanes in spots]
    residual = jnp.concatenate(parts[:-1], 2).reshape(own_tokens, cols)
    side = parts[-1].reshape(ctx_count, -1).astype(jnp.float32)
    gate_size = 4 * row_count * own
    gates = side[:, :gate_size].reshape(ctx_count, 2, 2, row_count, own)
    gates = jnp.transpose(gates[:, 0] + gates[:, 1], (0, 2, 1, 3)).reshape(seq_len, 2 * own)
    table = side[:, gate_size : gate_size + 2 * share * exp_count]
    table = table.reshape(chip_count, 2, 2, share, exp_count)
    table = lax.dynamic_index_in_dim(table, core_index, 1, keepdims=False)

    taps = lax.dynamic_slice_in_dim(comp_weight, ctx_index * own, own, 2)
    taps = jnp.transpose(taps.reshape(2, 2, stride_len, own), (0, 3, 1, 2))
    taps = jnp.tile(taps.reshape(4 * own, stride_len), (1, seq_len // stride_len))
    attended = attend(moved, taps, gates, row_count, share, block_len, head_width)

    table = jnp.transpose(table, (3, 1, 0, 2)).reshape(exp_count, -1).astype(jnp.bfloat16)
    table_rows = -(-table.shape[1] // cols)
    table_rows += -table_rows % 16
    table = jnp.pad(table, ((0, 0), (0, table_rows * cols - table.shape[1])))
    table = table.reshape(exp_count, table_rows, cols)
    gain = lax.dynamic_slice_in_dim(ffn_gain, chip_index * 2 * cols, 2 * cols, 0)
    spots = jnp.stack([chip_index, exp_index]).astype(jnp.int32)
    group_tokens = ctx_count * half
    def exchange(pieces):
        return lax.all_to_all(pieces, "exp", split_axis=0, concat_axis=0, tiled=True)

    def settle(pieces, group):
        sums = jnp.sum(pieces[:, :group_tokens].astype(jnp.float32), axis=0)
        own_rows = residual.reshape(ctx_count, 2, half, cols)[:, group]
        sums = sums.reshape(ctx_count, half, cols) + own_rows.astype(jnp.float32)
        sums = sums.reshape(chip_count, 2, half, cols)
        kept = lax.dynamic_index_in_dim(sums, core_index, 1, keepdims=False)
        given = sibling(lax.dynamic_index_in_dim(sums, 1 - core_index, 1, keepdims=False))
        sums = jnp.concatenate(
            [jnp.where(core_index == 0, kept, given), jnp.where(core_index == 0, given, kept)], 2
        )
        scaled = (sums * gain).astype(jnp.bfloat16).reshape(chip_count * half, 2 * cols)
        return sums, scaled

    middle = chip_count // 2
    core_spot = core_index.astype(jnp.int32).reshape(1)
    spread_first = lax.all_gather(attended[0], "z", axis=0)
    spread_first, other_gate, other_up, other_down = lax.optimization_barrier(
        (spread_first, other_gate, other_up, other_down)
    )
    spread_other = sibling(spread_first)
    spread_first, later = lax.optimization_barrier((spread_first, attended[1]))
    spread_second = lax.all_gather(later, ctx, axis=0)
    pieces = exchange(
        run_project(
            core_spot, spread_first, spread_other, False, out_proj, table, exp_count, True
        )
    )
    route = pieces[:, group_tokens:].reshape(exp_count, -1)[:, : 2 * chip_count * share]
    route = jnp.sum(
        route.reshape(exp_count, 2, chip_count, 2, half).astype(jnp.float32), axis=1
    )
    sums_first, scaled_first = settle(pieces, 0)
    pieces = run_project(
        core_spot, spread_second, spread_second, True, out_proj, table, exp_count, False
    )
    pieces, sums_first = lax.optimization_barrier((pieces, sums_first))
    wide = 1 << (2 * cols - 1).bit_length()
    padded = jnp.pad(scaled_first, ((0, 0), (0, wide - 2 * cols)))
    plane_first = lax.all_gather(padded, "z", axis=0)[:, :, : 2 * cols]
    pieces, plane_first = lax.optimization_barrier((exchange(pieces), plane_first))
    sums_second, scaled_second = settle(pieces, 1)
    along, across = plane_step(plane_first, 1), plane_step(plane_first, 2)
    plane_second = lax.all_gather(scaled_second, "z", axis=0)
    along, across, plane_second = lax.optimization_barrier((along, across, plane_second))
    far_a, far_b = plane_step(along[:middle], 2), plane_step(across[middle:], 1)
    far_a, far_b, plane_second = lax.optimization_barrier((far_a, far_b, plane_second))
    weights = (expert_gate[0], expert_up[0], other_gate, other_up)

    def run_active(blocks, group):
        route_rows = route[:, :, group].reshape(exp_count, chip_count * half, 1)
        return run_expert(spots, blocks, ffn_gain, weights, route_rows, half, 1 - group)

    def run_outs(active, sums, start, stop):
        return run_down(
            spots, active, expert_down[0], other_down, sums, exp_count, start, stop
        )

    active = run_active((plane_first, along, across, far_a, far_b), 0)
    (first,) = run_outs(active, sums_first, 0, chip_count)
    along, across = plane_step(plane_second, 1), plane_step(plane_second, 2)
    first, along, across = lax.optimization_barrier((first, along, across))
    far_a, far_b = plane_step(along[:middle], 2), plane_step(across[middle:], 1)

    first = lax.psum_scatter(
        first.reshape(chip_count, exp_count * half, model_width),
        "z",
        scatter_dimension=0,
        tiled=True,
    )
    active = run_active((plane_second, along, across, far_a, far_b), 1)

    sides = []
    for start, stop in ((0, middle), (middle, chip_count)):
        own, *given = run_outs(active, sums_second, start, stop)
        total = own.astype(jnp.float32)
        for step, block in enumerate(given, 1):
            total = total + plane_step(block, step).astype(jnp.float32)
        sides.append(total.astype(jnp.bfloat16))
    second = jnp.concatenate(sides, 2)
    second, first = lax.optimization_barrier((second, first))
    second = lax.psum_scatter(second, "z", scatter_dimension=0, tiled=True)
    first = lax.all_to_all(
        first.reshape(exp_count, half, model_width), "exp", split_axis=0, concat_axis=0, tiled=True
    )
    first = jnp.sum(first.astype(jnp.float32), axis=0).astype(jnp.bfloat16)
    return jnp.concatenate([first, second.reshape(half, model_width)], 0)


def specs(ctx):
    in_specs = (
        P(ctx, "exp"),
        P(ctx, "exp"),
        P(ctx, "exp"),
        P(None, ctx, "exp"),
        P(None, None, "exp"),
        P("exp", ctx),
        P((*ctx, "exp"), None),
        P(),
        P((*ctx, "exp"), None),
        P((*ctx, "exp"), None),
        P("exp", None, ctx),
        P("exp", None, ctx),
        P("exp", ctx, None),
    )
    return in_specs, P((*ctx, "exp"), None)


def solution(mesh):
    ctx_count, exp_count = mesh.shape["ctx"], mesh.shape["exp"]

    def run(*args):
        head_count = args[4].shape[2] // exp_count
        share = args[0].shape[0] // (ctx_count * exp_count)
        body, axes, where = general, ("ctx",), mesh
        own = head_count // ctx_count
        head_width = args[0].shape[1] // args[4].shape[2]
        pieces = args[5].shape[1] // (ctx_count * head_width) + 1
        fits = head_count % ctx_count == 0 and share % 32 == 0 and ctx_count % 8 == 0
        fits = fits and exp_count.bit_length() == 3 and exp_count.bit_count() == 1
        fits = fits and args[5].shape[1] % (ctx_count * head_width) == 0
        if fits and pieces % own == 0:
            split = mesh.devices.reshape(ctx_count // 2, 2, exp_count)
            where = jax.sharding.Mesh(split, ("z", "core", "exp"))
            body, axes = by_heads, ("z", "core")
        in_specs, out_specs = specs(axes)
        return jax.shard_map(
            body, mesh=where, in_specs=in_specs, out_specs=out_specs, check_vma=False
        )(*args)

    return run
```

```python
import functools
import math

import jax
import jax.numpy as jnp
from jax import lax
from jax.experimental import pallas as pl
from jax.experimental.pallas import tpu as pltpu
from jax.sharding import PartitionSpec as P

WINDOW = 512


score_gain = 2.0
norm_eps = 1e-06


def passed_along(block, axis, distance):
    devices = range(lax.axis_size(axis))
    route = [(i - distance, i) for i in devices if i - distance in devices]
    return lax.ppermute(block, axis, route)


def head_norm(matrix, head_width):
    row_count = matrix.shape[0]
    shaped = matrix.reshape(row_count, -1, head_width).astype(jnp.float32)
    scaled = shaped * lax.rsqrt(jnp.mean(shaped * shaped, axis=2, keepdims=True) + norm_eps)
    return scaled.reshape(row_count, -1)


def compress(extended, position_weights, head_width):
    stride_len = position_weights.shape[0] // 2
    head_count = position_weights.shape[1]
    blocks = extended.reshape(-1, stride_len, head_count, head_width).astype(jnp.float32)
    first_half = jnp.einsum(
        "nshd,sh->nhd", blocks[:-1], position_weights[:stride_len], precision=lax.Precision.HIGHEST
    )
    second_half = jnp.einsum(
        "nshd,sh->nhd", blocks[1:], position_weights[stride_len:], precision=lax.Precision.HIGHEST
    )
    return (first_half + second_half).reshape(blocks.shape[0] - 1, head_count * head_width)


def window_attention(query_input, key_input, value_input, gate_logits, comp_weight):
    row_count = query_input.shape[0]
    head_count = comp_weight.shape[2]
    head_width = query_input.shape[1] // head_count
    block_len = comp_weight.shape[1]
    stride_len = block_len // 2
    exp_count = lax.axis_size("exp")
    ctx_index = lax.axis_index("ctx")
    scale = score_gain / math.sqrt(head_width)
    query_norm = head_norm(query_input, head_width).astype(jnp.bfloat16)
    key_norm = head_norm(key_input, head_width).astype(jnp.bfloat16)
    next_keys, next_values = passed_along(
        (key_input[:stride_len], value_input[:stride_len]), "ctx", -1
    )
    comp_keys = head_norm(
        compress(jnp.concatenate([key_input, next_keys], 0), comp_weight[0], head_width), head_width
    ).astype(jnp.bfloat16)
    comp_values = compress(
        jnp.concatenate([value_input, next_values], 0), comp_weight[1], head_width
    ).astype(jnp.bfloat16)
    query_pos = ctx_index * row_count + jnp.arange(row_count, dtype=jnp.int32)
    query_heads = query_norm.reshape(row_count, head_count, head_width)
    part_keys = lax.all_gather(comp_keys, "ctx", axis=0, tiled=True)
    part_values = lax.all_gather(comp_values, "ctx", axis=0, tiled=True)
    part_count = part_keys.shape[0]
    scores = jnp.einsum(
        "thd,nhd->htn",
        query_heads,
        part_keys.reshape(part_count, head_count, head_width),
        preferred_element_type=jnp.float32,
    )
    block_end = jnp.arange(part_count, dtype=jnp.int32) * stride_len + block_len - 1
    visible = block_end[None, :] <= query_pos[:, None]
    weights = jnp.where(visible[None], jnp.exp(scale * scores), 0.0)
    running_total = jnp.sum(weights, axis=2).T
    collected = jnp.einsum(
        "htn,nhd->thd",
        weights.astype(jnp.bfloat16),
        part_values.reshape(part_count, head_count, head_width),
        preferred_element_type=jnp.float32,
    )
    cmp_sum = collected.reshape(row_count, -1)
    no_block = (query_pos < block_len - 1).astype(jnp.float32)
    cmp_out = (
        cmp_sum.reshape(row_count, head_count, head_width)
        / (running_total + no_block[:, None])[:, :, None]
    )
    shift_count = max(1, WINDOW // row_count)
    earlier_keys = []
    earlier_values = []
    for distance in range(shift_count, 0, -1):
        moved_keys, moved_values = passed_along((key_norm, value_input), "ctx", distance)
        earlier_keys.append(moved_keys)
        earlier_values.append(moved_values)
    near_keys = jnp.concatenate(earlier_keys + [key_norm], 0)
    near_values = jnp.concatenate(earlier_values + [value_input], 0)
    key_pos = ctx_index * row_count - WINDOW + jnp.arange(near_keys.shape[0], dtype=jnp.int32)
    near_scores = jnp.einsum(
        "thd,shd->hts",
        query_heads,
        near_keys.reshape(-1, head_count, head_width),
        preferred_element_type=jnp.float32,
    )
    inside = (
        (key_pos[None, :] <= query_pos[:, None])
        & (key_pos[None, :] > query_pos[:, None] - WINDOW)
        & (key_pos[None, :] >= 0)
    )
    near_weights = jnp.where(inside[None], jnp.exp(scale * near_scores), 0.0)
    win_total = jnp.sum(near_weights, axis=2).T
    win_sum = jnp.einsum(
        "hts,shd->thd",
        near_weights.astype(jnp.bfloat16),
        near_values.reshape(-1, head_count, head_width),
        preferred_element_type=jnp.float32,
    )
    win_out = win_sum / win_total[:, :, None]
    branch_gates = jax.nn.sigmoid(gate_logits)
    attended = (
        (branch_gates[0][:, :, None] * cmp_out + branch_gates[1][:, :, None] * win_out)
        .reshape(row_count, -1)
        .astype(jnp.bfloat16)
    )
    return attended


def general(
    query_input,
    key_input,
    value_input,
    gate_logits,
    comp_weight,
    out_proj,
    residual_in,
    ffn_gain,
    expert_ids,
    route_gates,
    expert_gate,
    expert_up,
    expert_down,
):
    row_count = query_input.shape[0]
    ctx_count = lax.axis_size("ctx")
    exp_count = lax.axis_size("exp")
    ctx_index = lax.axis_index("ctx")
    exp_index = lax.axis_index("exp")
    share = row_count // exp_count
    seq_len = row_count * ctx_count
    cols = out_proj.shape[1]
    model_width = cols * ctx_count
    hidden_units = expert_gate.shape[2]
    own_tokens = ctx_count * share

    experts = jnp.arange(exp_count, dtype=jnp.int32)
    route_table = jnp.sum(
        jnp.where(expert_ids[:, :, None] == experts, route_gates[:, :, None], 0.0), axis=1
    )
    route_all = lax.all_gather(route_table, ("ctx", "exp"), axis=0, tiled=True)
    route_own = lax.dynamic_slice_in_dim(route_all, exp_index, 1, 1)
    residual = lax.all_to_all(residual_in, "ctx", split_axis=1, concat_axis=0, tiled=True)

    attention_args = (query_input, key_input, value_input, gate_logits, comp_weight)
    attended = window_attention(*attention_args)
    spread_rows = lax.all_gather(
        attended.reshape(1, exp_count, share, -1), "ctx", axis=0, tiled=True
    )
    partial = jnp.einsum(
        "cerh,hd->ecrd", spread_rows, out_proj, preferred_element_type=jnp.float32
    )
    pieces = lax.all_to_all(
        partial.astype(jnp.bfloat16).reshape(exp_count, own_tokens, cols),
        "exp",
        split_axis=0,
        concat_axis=0,
        tiled=True,
    )
    hidden_state = residual.reshape(own_tokens, cols).astype(jnp.float32) + jnp.sum(
        pieces.astype(jnp.float32), axis=0
    )
    gain = lax.dynamic_slice_in_dim(ffn_gain, ctx_index * cols, cols, 0)
    scaled = (hidden_state * gain).astype(jnp.bfloat16)
    squares = jnp.sum(hidden_state * hidden_state, axis=1)
    rows = lax.all_gather(scaled, ("ctx", "exp"), axis=0, tiled=True)
    rows = rows.reshape(ctx_count, seq_len, cols)
    squares = lax.all_gather(squares, ("ctx", "exp"), axis=0, tiled=True)
    mean_square = jnp.sum(squares.reshape(ctx_count, seq_len), axis=0) / model_width
    inverse = lax.rsqrt(mean_square + norm_eps)[:, None]

    gate_part = inverse * jnp.einsum(
        "ctk,ckf->tf",
        rows,
        expert_gate.reshape(ctx_count, cols, hidden_units),
        preferred_element_type=jnp.float32,
    )
    up_part = inverse * jnp.einsum(
        "ctk,ckf->tf",
        rows,
        expert_up.reshape(ctx_count, cols, hidden_units),
        preferred_element_type=jnp.float32,
    )
    activated = (jax.nn.silu(gate_part) * up_part).astype(jnp.bfloat16)
    activated = jnp.transpose(
        activated.reshape(exp_count, ctx_count, share, hidden_units), (1, 0, 2, 3)
    ).reshape(seq_len, hidden_units)
    outs = jnp.dot(activated, expert_down[0], preferred_element_type=jnp.float32)
    outs = (outs * route_own).astype(jnp.bfloat16)
    outs = outs.reshape(ctx_count, exp_count, share, model_width)
    place = (0, exp_index, 0, ctx_index * cols)
    mine = lax.dynamic_slice(outs, place, (ctx_count, 1, share, cols))
    mine = mine.astype(jnp.float32) + hidden_state.reshape(ctx_count, 1, share, cols)
    outs = lax.dynamic_update_slice(outs, mine.astype(jnp.bfloat16), place)
    return lax.psum_scatter(
        outs.reshape(seq_len, model_width), ("ctx", "exp"), scatter_dimension=0, tiled=True
    )


def high_low(values):
    high = lax.reduce_precision(values, 8, 7)
    return jnp.stack([high, values - high], 0).astype(jnp.bfloat16)


def unit_rows(block):
    return block * lax.rsqrt(jnp.mean(block * block, axis=1, keepdims=True) + norm_eps)


def side_spots(count, own, row_count, share, head_width):
    spots = []
    for piece in range(count):
        first = 3 * row_count + piece // own * share
        lane = piece % own * head_width
        spots.append((slice(first, first + share), slice(lane, lane + head_width)))
    return spots


def pack_kernel(query, key, value, residual, side, out):
    row_count, width = query.shape
    share, head_width = side.shape[1:]
    for spot, block in enumerate((query, key, value)):
        out[0, spot * row_count : (spot + 1) * row_count, :] = block[...]
    count = residual.shape[1] // head_width
    spots = side_spots(count + 1, width // head_width, row_count, share, head_width)
    for piece, (rows, lanes) in enumerate(spots[:-1]):
        out[0, rows, lanes] = residual[:, piece * head_width : (piece + 1) * head_width]
    rows, lanes = spots[-1]
    out[0, rows, lanes] = side[0]


def pack(query, key, value, residual, side, width):
    ctx_count, share, head_width = side.shape
    row_count = query.shape[0]
    cols = residual.shape[1] // ctx_count
    rows = 3 * row_count + (cols // head_width + 1) * head_width // width * share
    heads = pl.BlockSpec((row_count, width), lambda i: (0, i))
    return pl.pallas_call(
        pack_kernel,
        grid=(ctx_count,),
        in_specs=[
            heads,
            heads,
            heads,
            pl.BlockSpec((share, cols), lambda i: (0, i)),
            pl.BlockSpec((1, share, head_width), lambda i: (i, 0, 0)),
        ],
        out_specs=pl.BlockSpec((1, rows, width), lambda i: (i, 0, 0)),
        out_shape=jax.ShapeDtypeStruct((ctx_count, rows, width), jnp.bfloat16),
        compiler_params=pltpu.CompilerParams(vmem_limit_bytes=16 * 2**20),
        name="pack",
    )(query, key, value, residual, side)


def attend_kernel(row_count, share, block_len, head_width, moved, taps, gates, out_a, out_b, keys, values):
    ctx_count = moved.shape[0]
    own = moved.shape[2] // head_width
    seq_len = row_count * ctx_count
    stride_len = block_len // 2
    part_count = seq_len // stride_len
    scale = score_gain / math.sqrt(head_width)

    def dot(left, right):
        return jnp.dot(left, right, preferred_element_type=jnp.float32)

    def dot_rows(left, right):
        return lax.dot_general(
            left, right, (((1,), (1,)), ((), ())), preferred_element_type=jnp.float32
        )

    def compressed(row, block):
        group = lax.broadcasted_iota(jnp.int32, (part_count, seq_len), 0)
        token_group = lax.broadcasted_iota(jnp.int32, (part_count, seq_len), 1) // stride_len
        band = jnp.where(token_group == group, taps[row : row + 1, :], 0.0)
        band = jnp.where(token_group == group + 1, taps[row + 1 : row + 2, :], band)
        high = band.astype(jnp.bfloat16)
        low = (band - high.astype(jnp.float32)).astype(jnp.bfloat16)
        return dot(high, block) + dot(low, block)

    for head in range(own):
        lanes = slice(head * head_width, (head + 1) * head_width)
        raw_keys = moved[:, row_count : 2 * row_count, lanes].reshape(seq_len, head_width)
        keys[...] = unit_rows(raw_keys.astype(jnp.float32)).astype(jnp.bfloat16)
        raw_values = moved[:, 2 * row_count : 3 * row_count, lanes].reshape(seq_len, head_width)
        values[...] = raw_values
        comp_keys = unit_rows(compressed(2 * head, raw_keys)).astype(jnp.bfloat16)
        comp_values = compressed(2 * (own + head), raw_values).astype(jnp.bfloat16)
        for block in range(ctx_count):
            query = moved[block, 0:row_count, lanes].astype(jnp.float32)
            query = unit_rows(query).astype(jnp.bfloat16)
            base = block * row_count
            rows = slice(base, base + row_count)
            spot = base + lax.broadcasted_iota(jnp.int32, (row_count, part_count), 0)
            ends = lax.broadcasted_iota(jnp.int32, (row_count, part_count), 1) * stride_len
            seen = ends + (block_len - 1) <= spot
            weight = jnp.where(seen, jnp.exp(scale * dot_rows(query, comp_keys)), 0.0)
            total = jnp.sum(weight, axis=1, keepdims=True)
            total = total + jnp.where(spot[:, :1] < block_len - 1, 1.0, 0.0)
            far = dot(weight.astype(jnp.bfloat16), comp_values) / total
            start = max(0, base - WINDOW)
            reach = base + row_count - start
            score = dot_rows(query, keys[start : start + reach, :])
            weight = jnp.exp(scale * score)
            edges = []
            for first in range(0, reach, row_count):
                piece = weight[:, first : first + row_count]
                offset = base - start - first
                ahead = lax.broadcasted_iota(jnp.int32, (row_count, row_count), 1)
                ahead = ahead - lax.broadcasted_iota(jnp.int32, (row_count, row_count), 0)
                if offset < row_count:
                    piece = jnp.where(ahead <= offset, piece, 0.0)
                if offset + row_count > WINDOW:
                    piece = jnp.where(ahead > offset - WINDOW, piece, 0.0)
                edges.append(piece)
            weight = jnp.concatenate(edges, 1)
            total = jnp.sum(weight, axis=1, keepdims=True)
            near = dot(weight.astype(jnp.bfloat16), values[start : start + reach, :]) / total
            mixed = (
                gates[rows, head : head + 1] * far
                + gates[rows, own + head : own + head + 1] * near
            ).astype(jnp.bfloat16)
            half = share // 2
            for part in range(row_count // share):
                for group in range(2):
                    target = (part * ctx_count + block) * half
                    base = part * share + group * half
                    (out_a, out_b)[group][target : target + half, lanes] = mixed[base : base + half]


def attend(moved, taps, gates, row_count, share, block_len, head_width):
    seq_len = moved.shape[0] * row_count
    width = moved.shape[2]
    return pl.pallas_call(
        functools.partial(attend_kernel, row_count, share, block_len, head_width),
        out_shape=[jax.ShapeDtypeStruct((seq_len // 2, width), jnp.bfloat16)] * 2,
        scratch_shapes=[
            pltpu.VMEM((seq_len, head_width), jnp.bfloat16),
            pltpu.VMEM((seq_len, head_width), jnp.bfloat16),
        ],
        compiler_params=pltpu.CompilerParams(vmem_limit_bytes=24 * 2**20),
        name="attend",
    )(moved, taps, gates)


def project_kernel(paired, spots, left_a, left_b, proj, table, out, total):
    step = pl.program_id(0)
    first = jnp.logical_or(paired, spots[0] == 0)
    parts = []
    for chip in range(left_a.shape[0]):
        if paired:
            parts += [left_a[chip, 0], left_a[chip, 1]]
        else:
            parts.append(jnp.where(first, left_a[chip, 0], left_b[chip, 0]))
            parts.append(jnp.where(first, left_b[chip, 0], left_a[chip, 0]))
    sums = jnp.dot(jnp.concatenate(parts, 1), proj[...], preferred_element_type=jnp.float32)

    @pl.when(step == 0)
    def _():
        total[...] = sums

    @pl.when(step == pl.num_programs(0) - 1)
    def _():
        exp_count = out.shape[0]
        tokens = total.shape[0] // exp_count
        for spot in range(exp_count):
            rows = slice(spot * tokens, (spot + 1) * tokens)
            out[spot, :tokens] = (total[rows] + sums[rows]).astype(jnp.bfloat16)
            if out.shape[1] > tokens:
                out[spot, tokens:] = table[spot]


def run_project(spots, left_a, left_b, paired, proj, table, exp_count, extra):
    depth, cols = proj.shape
    tokens, width = left_a.shape[1:]
    cores = 2 if paired else 1
    chips = depth // (2 * width)
    left_a = left_a.reshape(chips, cores, tokens, width)
    left_b = left_b.reshape(chips, cores, tokens, width)
    left = pl.BlockSpec((chips // 2, cores, tokens, width), lambda i, _: (i, 0, 0, 0))
    unused = pl.BlockSpec((1, 1, tokens, width), lambda i, _: (0, 0, 0, 0))
    rows = tokens // exp_count + (table.shape[1] if extra else 0)
    return pl.pallas_call(
        functools.partial(project_kernel, paired),
        grid_spec=pltpu.PrefetchScalarGridSpec(
            num_scalar_prefetch=1,
            grid=(2,),
            in_specs=[
                left,
                unused if paired else left,
                pl.BlockSpec((depth // 2, cols), lambda i, _: (i, 0)),
                pl.BlockSpec(table.shape, lambda i, _: (0, 0, 0)),
            ],
            out_specs=pl.BlockSpec((exp_count, rows, cols), lambda i, _: (0, 0, 0)),
            scratch_shapes=[pltpu.VMEM((tokens, cols), jnp.float32)],
        ),
        out_shape=jax.ShapeDtypeStruct((exp_count, rows, cols), jnp.bfloat16),
        compiler_params=pltpu.CompilerParams(vmem_limit_bytes=24 * 2**20),
        cost_estimate=pl.CostEstimate(
            flops=2 * tokens * depth * cols,
            bytes_accessed=2 * depth * (tokens + cols) + 2 * exp_count * rows * cols,
            transcendentals=0,
        ),
        name="project",
    )(spots, left_a, left_b, proj, table)


def expert_kernel(exp_dim, spots, own, along, across, far_a, far_b, gain, gate_w, up_w, gate_v, up_v, route, out, total, squares):
    step = pl.program_id(0)

    @pl.when(step == 0)
    def _():
        total[...] = jnp.zeros_like(total)
        squares[...] = jnp.zeros_like(squares)

    far = jnp.where(step < pl.num_programs(0) // 2, far_a[0], far_b[0])
    block = jnp.concatenate([own[0], along[0], across[0], far], 0)
    for spot, weight in enumerate((gate_w, up_w, gate_v, up_v)):
        total[spot] += jnp.dot(block, weight[...], preferred_element_type=jnp.float32)
    lane = squares.shape[1]
    collected = squares[...]
    for part in range(block.shape[1] // lane):
        lanes = slice(part * lane, (part + 1) * lane)
        plain = block[:, lanes].astype(jnp.float32) * (1.0 / gain[0, :, lanes])
        collected = collected + plain * plain
    squares[...] = collected

    @pl.when(step == pl.num_programs(0) - 1)
    def _():
        model_width = pl.num_programs(0) * block.shape[1]
        mean_square = jnp.sum(squares[...], axis=1, keepdims=True) / model_width
        inverse = lax.rsqrt(mean_square + norm_eps)
        tokens = own.shape[1]
        for core in range(2):
            gate_part = total[2 * core] * inverse
            up_part = total[2 * core + 1] * inverse
            active = gate_part / (1.0 + jnp.exp(-gate_part)) * up_part
            for source in range(block.shape[0] // tokens):
                spot = pl.ds(jnp.bitwise_xor(spots[1], source), 1)
                piece = active[source * tokens : (source + 1) * tokens] * route[spot][0]
                piece = piece.astype(jnp.bfloat16)
                if exp_dim == 0:
                    out[core, source] = piece.reshape(out.shape[2:])
                else:
                    out[core, :, spot] = piece.reshape(out.shape[1], 1, *out.shape[3:])


def run_expert(spots, blocks, gain, weights, route, half, exp_dim):
    chip_count, tokens, wide = blocks[0].shape
    cols = wide
    middle = chip_count // 2
    steps = chip_count
    units = weights[0].shape[1]
    exp_count = route.shape[0]
    row_total = exp_count * tokens
    lane = math.gcd(128, cols)
    lead = (exp_count, tokens // half) if exp_dim == 0 else (tokens // half, exp_count)
    by_chip = pl.BlockSpec((1, tokens, cols), lambda i, _: (i, 0, 0))
    by_cols = pl.BlockSpec((cols, units), lambda i, _: (i, 0))
    out = pl.pallas_call(
        functools.partial(expert_kernel, exp_dim),
        grid_spec=pltpu.PrefetchScalarGridSpec(
            num_scalar_prefetch=1,
            grid=(steps,),
            in_specs=[
                by_chip,
                by_chip,
                by_chip,
                pl.BlockSpec(
                    (1, tokens, cols), lambda i, _: (jnp.minimum(i, middle - 1), 0, 0)
                ),
                pl.BlockSpec(
                    (1, tokens, cols), lambda i, _: (jnp.maximum(i - middle, 0), 0, 0)
                ),
                pl.BlockSpec((1, 1, cols), lambda i, _: (i, 0, 0)),
                by_cols,
                by_cols,
                by_cols,
                by_cols,
                pl.BlockSpec((exp_count, tokens, 1), lambda i, _: (0, 0, 0)),
            ],
            out_specs=pl.BlockSpec((2,) + lead + (half, units), lambda i, _: (0, 0, 0, 0, 0)),
            scratch_shapes=[
                pltpu.VMEM((4, row_total, units), jnp.float32),
                pltpu.VMEM((row_total, lane), jnp.float32),
            ],
        ),
        out_shape=jax.ShapeDtypeStruct((2,) + lead + (half, units), jnp.bfloat16),
        compiler_params=pltpu.CompilerParams(vmem_limit_bytes=24 * 2**20),
        cost_estimate=pl.CostEstimate(
            flops=8 * row_total * units * steps * cols,
            bytes_accessed=2 * steps * cols * (row_total + 4 * units),
            transcendentals=2 * row_total * units,
        ),
        name="expert",
    )(spots, *blocks, gain.reshape(steps, 1, cols), *weights, route)
    return out.reshape(2, row_total, units)


def down_kernel(start, spots, active, down_w, down_v, hidden, *outs):
    left = jnp.concatenate([active[0], active[1]], 1)
    right = jnp.concatenate([down_w[...], down_v[...]], 0)
    sums = jnp.dot(left, right, preferred_element_type=jnp.float32).astype(jnp.bfloat16)
    kept = outs[0]
    if len(outs) == 1:
        kept[...] = sums.reshape(kept.shape)
    else:
        tokens = sums.shape[0] // len(outs)
        for source, out in enumerate(outs):
            out[...] = sums[source * tokens : (source + 1) * tokens].reshape(out.shape)

    @pl.when(pl.program_id(0) + start == spots[0])
    def _():
        place = (slice(None), pl.ds(spots[1], 1)) if len(outs) == 1 else ...
        piece = kept[place].astype(jnp.float32)
        kept[place] = (piece + hidden[...].reshape(piece.shape)).astype(kept.dtype)


def run_down(spots, active, down_w, down_v, hidden, exp_count, start, stop):
    units = down_w.shape[0]
    chip_count, half, cols = hidden.shape
    rows = active.shape[1]
    whole = stop - start == chip_count
    lead = (chip_count, exp_count) if whole else (chip_count,)
    zeros = (0,) * len(lead + (half,))
    by_cols = pl.BlockSpec((units, cols), lambda i, _: (0, i + start))
    count = 1 if whole else exp_count
    shape = lead + (half, (stop - start) * cols)
    return pl.pallas_call(
        functools.partial(down_kernel, start),
        grid_spec=pltpu.PrefetchScalarGridSpec(
            num_scalar_prefetch=1,
            grid=(stop - start,),
            in_specs=[
                pl.BlockSpec((2, rows, units), lambda i, _: (0, 0, 0)),
                by_cols,
                by_cols,
                pl.BlockSpec((chip_count, half, cols), lambda i, _: (0, 0, 0)),
            ],
            out_specs=[pl.BlockSpec(lead + (half, cols), lambda i, _: (*zeros, i))] * count,
        ),
        out_shape=[jax.ShapeDtypeStruct(shape, jnp.bfloat16)] * count,
        compiler_params=pltpu.CompilerParams(vmem_limit_bytes=24 * 2**20),
        cost_estimate=pl.CostEstimate(
            flops=4 * rows * units * cols * (stop - start),
            bytes_accessed=2 * cols * (stop - start) * (rows + 2 * units),
            transcendentals=0,
        ),
        name="down",
    )(spots, active, down_w, down_v, hidden)


def sibling(block):
    return lax.ppermute(block, "core", [(0, 1), (1, 0)])


def plane_step(block, step):
    count = lax.axis_size("exp")
    return lax.ppermute(block, "exp", [(i, i ^ step) for i in range(count)])


def by_heads(
    query_input,
    key_input,
    value_input,
    gate_logits,
    comp_weight,
    out_proj,
    residual_in,
    ffn_gain,
    expert_ids,
    route_gates,
    expert_gate,
    expert_up,
    expert_down,
):
    row_count = query_input.shape[0]
    head_count = comp_weight.shape[2]
    head_width = query_input.shape[1] // head_count
    block_len = comp_weight.shape[1]
    stride_len = block_len // 2
    ctx = ("z", "core")
    chip_count = lax.axis_size("z")
    ctx_count = chip_count * lax.axis_size("core")
    exp_count = lax.axis_size("exp")
    chip_index = lax.axis_index("z")
    core_index = lax.axis_index("core")
    ctx_index = 2 * chip_index + core_index
    exp_index = lax.axis_index("exp")
    own = head_count // ctx_count
    width = own * head_width
    share = row_count // exp_count
    half = share // 2
    seq_len = row_count * ctx_count
    cols = out_proj.shape[1]
    model_width = cols * ctx_count
    own_tokens = ctx_count * share

    other_gate = sibling(expert_gate[0])
    other_up = sibling(expert_up[0])
    other_down = sibling(expert_down[0])

    experts = jnp.arange(exp_count, dtype=jnp.int32)
    table = jnp.sum(
        jnp.where(expert_ids[:, :, None] == experts, route_gates[:, :, None], 0.0), axis=1
    )
    table = jnp.broadcast_to(high_low(table).reshape(1, -1), (ctx_count, 2 * share * exp_count))
    gates = high_low(jax.nn.sigmoid(gate_logits)).reshape(2, 2, row_count, ctx_count, own)
    gates = jnp.transpose(gates, (3, 0, 1, 2, 4)).reshape(ctx_count, -1)
    side = jnp.concatenate([gates, table], 1)
    side = jnp.pad(side, ((0, 0), (0, share * head_width - side.shape[1])))
    side = side.reshape(ctx_count, share, head_width)
    packed = pack(query_input, key_input, value_input, residual_in, side, width)
    moved = lax.all_to_all(packed, ctx, split_axis=0, concat_axis=0, tiled=True)
    spots = side_spots(cols // head_width + 1, own, row_count, share, head_width)
    parts = [moved[:, rows, lanes] for rows, lanes in spots]
    residual = jnp.concatenate(parts[:-1], 2).reshape(own_tokens, cols)
    side = parts[-1].reshape(ctx_count, -1).astype(jnp.float32)
    gate_size = 4 * row_count * own
    gates = side[:, :gate_size].reshape(ctx_count, 2, 2, row_count, own)
    gates = jnp.transpose(gates[:, 0] + gates[:, 1], (0, 2, 1, 3)).reshape(seq_len, 2 * own)
    table = side[:, gate_size : gate_size + 2 * share * exp_count]
    table = table.reshape(chip_count, 2, 2, share, exp_count)
    table = lax.dynamic_index_in_dim(table, core_index, 1, keepdims=False)

    taps = lax.dynamic_slice_in_dim(comp_weight, ctx_index * own, own, 2)
    taps = jnp.transpose(taps.reshape(2, 2, stride_len, own), (0, 3, 1, 2))
    taps = jnp.tile(taps.reshape(4 * own, stride_len), (1, seq_len // stride_len))
    attended = attend(moved, taps, gates, row_count, share, block_len, head_width)

    table = jnp.transpose(table, (3, 1, 0, 2)).reshape(exp_count, -1).astype(jnp.bfloat16)
    table_rows = -(-table.shape[1] // cols)
    table_rows += -table_rows % 16
    table = jnp.pad(table, ((0, 0), (0, table_rows * cols - table.shape[1])))
    table = table.reshape(exp_count, table_rows, cols)
    gain = lax.dynamic_slice_in_dim(ffn_gain, chip_index * 2 * cols, 2 * cols, 0)
    spots = jnp.stack([chip_index, exp_index]).astype(jnp.int32)
    group_tokens = ctx_count * half
    def exchange(pieces):
        return lax.all_to_all(pieces, "exp", split_axis=0, concat_axis=0, tiled=True)

    def settle(pieces, group):
        sums = jnp.sum(pieces[:, :group_tokens].astype(jnp.float32), axis=0)
        own_rows = residual.reshape(ctx_count, 2, half, cols)[:, group]
        sums = sums.reshape(ctx_count, half, cols) + own_rows.astype(jnp.float32)
        sums = sums.reshape(chip_count, 2, half, cols)
        kept = lax.dynamic_index_in_dim(sums, core_index, 1, keepdims=False)
        given = sibling(lax.dynamic_index_in_dim(sums, 1 - core_index, 1, keepdims=False))
        sums = jnp.concatenate(
            [jnp.where(core_index == 0, kept, given), jnp.where(core_index == 0, given, kept)], 2
        )
        scaled = (sums * gain).astype(jnp.bfloat16).reshape(chip_count * half, 2 * cols)
        return sums, scaled

    middle = chip_count // 2
    core_spot = core_index.astype(jnp.int32).reshape(1)
    spread_first = lax.all_gather(attended[0], "z", axis=0)
    spread_first, other_gate, other_up, other_down = lax.optimization_barrier(
        (spread_first, other_gate, other_up, other_down)
    )
    spread_other = sibling(spread_first)
    spread_first, later = lax.optimization_barrier((spread_first, attended[1]))
    spread_second = lax.all_gather(later, ctx, axis=0)
    pieces = exchange(
        run_project(
            core_spot, spread_first, spread_other, False, out_proj, table, exp_count, True
        )
    )
    route = pieces[:, group_tokens:].reshape(exp_count, -1)[:, : 2 * chip_count * share]
    route = jnp.sum(
        route.reshape(exp_count, 2, chip_count, 2, half).astype(jnp.float32), axis=1
    )
    sums_first, scaled_first = settle(pieces, 0)
    pieces = run_project(
        core_spot, spread_second, spread_second, True, out_proj, table, exp_count, False
    )
    pieces, sums_first = lax.optimization_barrier((pieces, sums_first))
    wide = 1 << (2 * cols - 1).bit_length()
    padded = jnp.pad(scaled_first, ((0, 0), (0, wide - 2 * cols)))
    plane_first = lax.all_gather(padded, "z", axis=0)[:, :, : 2 * cols]
    pieces, plane_first = lax.optimization_barrier((exchange(pieces), plane_first))
    sums_second, scaled_second = settle(pieces, 1)
    along, across = plane_step(plane_first, 1), plane_step(plane_first, 2)
    plane_second = lax.all_gather(scaled_second, "z", axis=0)
    along, across, plane_second = lax.optimization_barrier((along, across, plane_second))
    far_a, far_b = plane_step(along[:middle], 2), plane_step(across[middle:], 1)
    far_a, far_b, plane_second = lax.optimization_barrier((far_a, far_b, plane_second))
    weights = (expert_gate[0], expert_up[0], other_gate, other_up)

    def run_active(blocks, group):
        route_rows = route[:, :, group].reshape(exp_count, chip_count * half, 1)
        return run_expert(spots, blocks, ffn_gain, weights, route_rows, half, 1 - group)

    def run_outs(active, sums, start, stop):
        return run_down(
            spots, active, expert_down[0], other_down, sums, exp_count, start, stop
        )

    active = run_active((plane_first, along, across, far_a, far_b), 0)
    (first,) = run_outs(active, sums_first, 0, chip_count)
    along, across = plane_step(plane_second, 1), plane_step(plane_second, 2)
    first, along, across = lax.optimization_barrier((first, along, across))
    far_a, far_b = plane_step(along[:middle], 2), plane_step(across[middle:], 1)

    first = lax.psum_scatter(
        first.reshape(chip_count, exp_count * half, model_width),
        "z",
        scatter_dimension=0,
        tiled=True,
    )
    active = run_active((plane_second, along, across, far_a, far_b), 1)

    sides = []
    for start, stop in ((0, middle), (middle, chip_count)):
        own, *given = run_outs(active, sums_second, start, stop)
        total = own.astype(jnp.float32)
        for step, block in enumerate(given, 1):
            total = total + plane_step(block, step).astype(jnp.float32)
        sides.append(total.astype(jnp.bfloat16))
    second = jnp.concatenate(sides, 2)
    second, first = lax.optimization_barrier((second, first))
    second = lax.psum_scatter(second, "z", scatter_dimension=0, tiled=True)
    first = lax.all_to_all(
        first.reshape(exp_count, half, model_width), "exp", split_axis=0, concat_axis=0, tiled=True
    )
    first = jnp.sum(first.astype(jnp.float32), axis=0).astype(jnp.bfloat16)
    return jnp.concatenate([first, second.reshape(half, model_width)], 0)


def specs(ctx):
    in_specs = (
        P(ctx, "exp"),
        P(ctx, "exp"),
        P(ctx, "exp"),
        P(None, ctx, "exp"),
        P(None, None, "exp"),
        P("exp", ctx),
        P((*ctx, "exp"), None),
        P(),
        P((*ctx, "exp"), None),
        P((*ctx, "exp"), None),
        P("exp", None, ctx),
        P("exp", None, ctx),
        P("exp", ctx, None),
    )
    return in_specs, P((*ctx, "exp"), None)


def solution(mesh):
    ctx_count, exp_count = mesh.shape["ctx"], mesh.shape["exp"]

    def run(*args):
        head_count = args[4].shape[2] // exp_count
        share = args[0].shape[0] // (ctx_count * exp_count)
        body, axes, where = general, ("ctx",), mesh
        own = head_count // ctx_count
        head_width = args[0].shape[1] // args[4].shape[2]
        pieces = args[5].shape[1] // (ctx_count * head_width) + 1
        fits = head_count % ctx_count == 0 and share % 32 == 0 and ctx_count % 8 == 0
        fits = fits and exp_count.bit_length() == 3 and exp_count.bit_count() == 1
        fits = fits and args[5].shape[1] % (ctx_count * head_width) == 0
        if fits and pieces % own == 0:
            split = mesh.devices.reshape(ctx_count // 2, 2, exp_count)
            where = jax.sharding.Mesh(split, ("z", "core", "exp"))
            body, axes = by_heads, ("z", "core")
        in_specs, out_specs = specs(axes)
        return jax.shard_map(
            body, mesh=where, in_specs=in_specs, out_specs=out_specs, check_vma=False
        )(*args)

    return run
```

```python
import functools
import math

import jax
import jax.numpy as jnp
from jax import lax
from jax.experimental import pallas as pl
from jax.experimental.pallas import tpu as pltpu
from jax.sharding import PartitionSpec as P

WINDOW = 512


score_gain = 2.0
norm_eps = 1e-06


def passed_along(block, axis, distance):
    devices = range(lax.axis_size(axis))
    route = [(i - distance, i) for i in devices if i - distance in devices]
    return lax.ppermute(block, axis, route)


def head_norm(matrix, head_width):
    row_count = matrix.shape[0]
    shaped = matrix.reshape(row_count, -1, head_width).astype(jnp.float32)
    scaled = shaped * lax.rsqrt(jnp.mean(shaped * shaped, axis=2, keepdims=True) + norm_eps)
    return scaled.reshape(row_count, -1)


def compress(extended, position_weights, head_width):
    stride_len = position_weights.shape[0] // 2
    head_count = position_weights.shape[1]
    blocks = extended.reshape(-1, stride_len, head_count, head_width).astype(jnp.float32)
    first_half = jnp.einsum(
        "nshd,sh->nhd", blocks[:-1], position_weights[:stride_len], precision=lax.Precision.HIGHEST
    )
    second_half = jnp.einsum(
        "nshd,sh->nhd", blocks[1:], position_weights[stride_len:], precision=lax.Precision.HIGHEST
    )
    return (first_half + second_half).reshape(blocks.shape[0] - 1, head_count * head_width)


def window_attention(query_input, key_input, value_input, gate_logits, comp_weight):
    row_count = query_input.shape[0]
    head_count = comp_weight.shape[2]
    head_width = query_input.shape[1] // head_count
    block_len = comp_weight.shape[1]
    stride_len = block_len // 2
    exp_count = lax.axis_size("exp")
    ctx_index = lax.axis_index("ctx")
    scale = score_gain / math.sqrt(head_width)
    query_norm = head_norm(query_input, head_width).astype(jnp.bfloat16)
    key_norm = head_norm(key_input, head_width).astype(jnp.bfloat16)
    next_keys, next_values = passed_along(
        (key_input[:stride_len], value_input[:stride_len]), "ctx", -1
    )
    comp_keys = head_norm(
        compress(jnp.concatenate([key_input, next_keys], 0), comp_weight[0], head_width), head_width
    ).astype(jnp.bfloat16)
    comp_values = compress(
        jnp.concatenate([value_input, next_values], 0), comp_weight[1], head_width
    ).astype(jnp.bfloat16)
    query_pos = ctx_index * row_count + jnp.arange(row_count, dtype=jnp.int32)
    query_heads = query_norm.reshape(row_count, head_count, head_width)
    part_keys = lax.all_gather(comp_keys, "ctx", axis=0, tiled=True)
    part_values = lax.all_gather(comp_values, "ctx", axis=0, tiled=True)
    part_count = part_keys.shape[0]
    scores = jnp.einsum(
        "thd,nhd->htn",
        query_heads,
        part_keys.reshape(part_count, head_count, head_width),
        preferred_element_type=jnp.float32,
    )
    block_end = jnp.arange(part_count, dtype=jnp.int32) * stride_len + block_len - 1
    visible = block_end[None, :] <= query_pos[:, None]
    weights = jnp.where(visible[None], jnp.exp(scale * scores), 0.0)
    running_total = jnp.sum(weights, axis=2).T
    collected = jnp.einsum(
        "htn,nhd->thd",
        weights.astype(jnp.bfloat16),
        part_values.reshape(part_count, head_count, head_width),
        preferred_element_type=jnp.float32,
    )
    cmp_sum = collected.reshape(row_count, -1)
    no_block = (query_pos < block_len - 1).astype(jnp.float32)
    cmp_out = (
        cmp_sum.reshape(row_count, head_count, head_width)
        / (running_total + no_block[:, None])[:, :, None]
    )
    shift_count = max(1, WINDOW // row_count)
    earlier_keys = []
    earlier_values = []
    for distance in range(shift_count, 0, -1):
        moved_keys, moved_values = passed_along((key_norm, value_input), "ctx", distance)
        earlier_keys.append(moved_keys)
        earlier_values.append(moved_values)
    near_keys = jnp.concatenate(earlier_keys + [key_norm], 0)
    near_values = jnp.concatenate(earlier_values + [value_input], 0)
    key_pos = ctx_index * row_count - WINDOW + jnp.arange(near_keys.shape[0], dtype=jnp.int32)
    near_scores = jnp.einsum(
        "thd,shd->hts",
        query_heads,
        near_keys.reshape(-1, head_count, head_width),
        preferred_element_type=jnp.float32,
    )
    inside = (
        (key_pos[None, :] <= query_pos[:, None])
        & (key_pos[None, :] > query_pos[:, None] - WINDOW)
        & (key_pos[None, :] >= 0)
    )
    near_weights = jnp.where(inside[None], jnp.exp(scale * near_scores), 0.0)
    win_total = jnp.sum(near_weights, axis=2).T
    win_sum = jnp.einsum(
        "hts,shd->thd",
        near_weights.astype(jnp.bfloat16),
        near_values.reshape(-1, head_count, head_width),
        preferred_element_type=jnp.float32,
    )
    win_out = win_sum / win_total[:, :, None]
    branch_gates = jax.nn.sigmoid(gate_logits)
    attended = (
        (branch_gates[0][:, :, None] * cmp_out + branch_gates[1][:, :, None] * win_out)
        .reshape(row_count, -1)
        .astype(jnp.bfloat16)
    )
    return attended


def general(
    query_input,
    key_input,
    value_input,
    gate_logits,
    comp_weight,
    out_proj,
    residual_in,
    ffn_gain,
    expert_ids,
    route_gates,
    expert_gate,
    expert_up,
    expert_down,
):
    row_count = query_input.shape[0]
    ctx_count = lax.axis_size("ctx")
    exp_count = lax.axis_size("exp")
    ctx_index = lax.axis_index("ctx")
    exp_index = lax.axis_index("exp")
    share = row_count // exp_count
    seq_len = row_count * ctx_count
    cols = out_proj.shape[1]
    model_width = cols * ctx_count
    hidden_units = expert_gate.shape[2]
    own_tokens = ctx_count * share

    experts = jnp.arange(exp_count, dtype=jnp.int32)
    route_table = jnp.sum(
        jnp.where(expert_ids[:, :, None] == experts, route_gates[:, :, None], 0.0), axis=1
    )
    route_all = lax.all_gather(route_table, ("ctx", "exp"), axis=0, tiled=True)
    route_own = lax.dynamic_slice_in_dim(route_all, exp_index, 1, 1)
    residual = lax.all_to_all(residual_in, "ctx", split_axis=1, concat_axis=0, tiled=True)

    attention_args = (query_input, key_input, value_input, gate_logits, comp_weight)
    attended = window_attention(*attention_args)
    spread_rows = lax.all_gather(
        attended.reshape(1, exp_count, share, -1), "ctx", axis=0, tiled=True
    )
    partial = jnp.einsum(
        "cerh,hd->ecrd", spread_rows, out_proj, preferred_element_type=jnp.float32
    )
    pieces = lax.all_to_all(
        partial.astype(jnp.bfloat16).reshape(exp_count, own_tokens, cols),
        "exp",
        split_axis=0,
        concat_axis=0,
        tiled=True,
    )
    hidden_state = residual.reshape(own_tokens, cols).astype(jnp.float32) + jnp.sum(
        pieces.astype(jnp.float32), axis=0
    )
    gain = lax.dynamic_slice_in_dim(ffn_gain, ctx_index * cols, cols, 0)
    scaled = (hidden_state * gain).astype(jnp.bfloat16)
    squares = jnp.sum(hidden_state * hidden_state, axis=1)
    rows = lax.all_gather(scaled, ("ctx", "exp"), axis=0, tiled=True)
    rows = rows.reshape(ctx_count, seq_len, cols)
    squares = lax.all_gather(squares, ("ctx", "exp"), axis=0, tiled=True)
    mean_square = jnp.sum(squares.reshape(ctx_count, seq_len), axis=0) / model_width
    inverse = lax.rsqrt(mean_square + norm_eps)[:, None]

    gate_part = inverse * jnp.einsum(
        "ctk,ckf->tf",
        rows,
        expert_gate.reshape(ctx_count, cols, hidden_units),
        preferred_element_type=jnp.float32,
    )
    up_part = inverse * jnp.einsum(
        "ctk,ckf->tf",
        rows,
        expert_up.reshape(ctx_count, cols, hidden_units),
        preferred_element_type=jnp.float32,
    )
    activated = (jax.nn.silu(gate_part) * up_part).astype(jnp.bfloat16)
    activated = jnp.transpose(
        activated.reshape(exp_count, ctx_count, share, hidden_units), (1, 0, 2, 3)
    ).reshape(seq_len, hidden_units)
    outs = jnp.dot(activated, expert_down[0], preferred_element_type=jnp.float32)
    outs = (outs * route_own).astype(jnp.bfloat16)
    outs = outs.reshape(ctx_count, exp_count, share, model_width)
    place = (0, exp_index, 0, ctx_index * cols)
    mine = lax.dynamic_slice(outs, place, (ctx_count, 1, share, cols))
    mine = mine.astype(jnp.float32) + hidden_state.reshape(ctx_count, 1, share, cols)
    outs = lax.dynamic_update_slice(outs, mine.astype(jnp.bfloat16), place)
    return lax.psum_scatter(
        outs.reshape(seq_len, model_width), ("ctx", "exp"), scatter_dimension=0, tiled=True
    )


def high_low(values):
    high = lax.reduce_precision(values, 8, 7)
    return jnp.stack([high, values - high], 0).astype(jnp.bfloat16)


def unit_rows(block):
    return block * lax.rsqrt(jnp.mean(block * block, axis=1, keepdims=True) + norm_eps)


def side_spots(count, own, row_count, share, head_width):
    spots = []
    for piece in range(count):
        first = 3 * row_count + piece // own * share
        lane = piece % own * head_width
        spots.append((slice(first, first + share), slice(lane, lane + head_width)))
    return spots


def pack_kernel(query, key, value, residual, side, out):
    row_count, width = query.shape
    share, head_width = side.shape[1:]
    for spot, block in enumerate((query, key, value)):
        out[0, spot * row_count : (spot + 1) * row_count, :] = block[...]
    count = residual.shape[1] // head_width
    spots = side_spots(count + 1, width // head_width, row_count, share, head_width)
    for piece, (rows, lanes) in enumerate(spots[:-1]):
        out[0, rows, lanes] = residual[:, piece * head_width : (piece + 1) * head_width]
    rows, lanes = spots[-1]
    out[0, rows, lanes] = side[0]


def pack(query, key, value, residual, side, width):
    ctx_count, share, head_width = side.shape
    row_count = query.shape[0]
    cols = residual.shape[1] // ctx_count
    rows = 3 * row_count + (cols // head_width + 1) * head_width // width * share
    heads = pl.BlockSpec((row_count, width), lambda i: (0, i))
    return pl.pallas_call(
        pack_kernel,
        grid=(ctx_count,),
        in_specs=[
            heads,
            heads,
            heads,
            pl.BlockSpec((share, cols), lambda i: (0, i)),
            pl.BlockSpec((1, share, head_width), lambda i: (i, 0, 0)),
        ],
        out_specs=pl.BlockSpec((1, rows, width), lambda i: (i, 0, 0)),
        out_shape=jax.ShapeDtypeStruct((ctx_count, rows, width), jnp.bfloat16),
        compiler_params=pltpu.CompilerParams(vmem_limit_bytes=32 * 2**20),
        name="pack",
    )(query, key, value, residual, side)


def attend_kernel(row_count, share, block_len, head_width, moved, taps, gates, out_a, out_b, keys, values):
    ctx_count = moved.shape[0]
    own = moved.shape[2] // head_width
    seq_len = row_count * ctx_count
    stride_len = block_len // 2
    part_count = seq_len // stride_len
    scale = score_gain / math.sqrt(head_width)

    def dot(left, right):
        return jnp.dot(left, right, preferred_element_type=jnp.float32)

    def dot_rows(left, right):
        return lax.dot_general(
            left, right, (((1,), (1,)), ((), ())), preferred_element_type=jnp.float32
        )

    def compressed(row, block):
        group = lax.broadcasted_iota(jnp.int32, (part_count, seq_len), 0)
        token_group = lax.broadcasted_iota(jnp.int32, (part_count, seq_len), 1) // stride_len
        band = jnp.where(token_group == group, taps[row : row + 1, :], 0.0)
        band = jnp.where(token_group == group + 1, taps[row + 1 : row + 2, :], band)
        high = band.astype(jnp.bfloat16)
        low = (band - high.astype(jnp.float32)).astype(jnp.bfloat16)
        return dot(high, block) + dot(low, block)

    for head in range(own):
        lanes = slice(head * head_width, (head + 1) * head_width)
        raw_keys = moved[:, row_count : 2 * row_count, lanes].reshape(seq_len, head_width)
        keys[...] = unit_rows(raw_keys.astype(jnp.float32)).astype(jnp.bfloat16)
        raw_values = moved[:, 2 * row_count : 3 * row_count, lanes].reshape(seq_len, head_width)
        values[...] = raw_values
        comp_keys = unit_rows(compressed(2 * head, raw_keys)).astype(jnp.bfloat16)
        comp_values = compressed(2 * (own + head), raw_values).astype(jnp.bfloat16)
        for block in range(ctx_count):
            query = moved[block, 0:row_count, lanes].astype(jnp.float32)
            query = unit_rows(query).astype(jnp.bfloat16)
            base = block * row_count
            rows = slice(base, base + row_count)
            spot = base + lax.broadcasted_iota(jnp.int32, (row_count, part_count), 0)
            ends = lax.broadcasted_iota(jnp.int32, (row_count, part_count), 1) * stride_len
            seen = ends + (block_len - 1) <= spot
            weight = jnp.where(seen, jnp.exp(scale * dot_rows(query, comp_keys)), 0.0)
            total = jnp.sum(weight, axis=1, keepdims=True)
            total = total + jnp.where(spot[:, :1] < block_len - 1, 1.0, 0.0)
            far = dot(weight.astype(jnp.bfloat16), comp_values) / total
            start = max(0, base - WINDOW)
            reach = base + row_count - start
            score = dot_rows(query, keys[start : start + reach, :])
            weight = jnp.exp(scale * score)
            edges = []
            for first in range(0, reach, row_count):
                piece = weight[:, first : first + row_count]
                offset = base - start - first
                ahead = lax.broadcasted_iota(jnp.int32, (row_count, row_count), 1)
                ahead = ahead - lax.broadcasted_iota(jnp.int32, (row_count, row_count), 0)
                if offset < row_count:
                    piece = jnp.where(ahead <= offset, piece, 0.0)
                if offset + row_count > WINDOW:
                    piece = jnp.where(ahead > offset - WINDOW, piece, 0.0)
                edges.append(piece)
            weight = jnp.concatenate(edges, 1)
            total = jnp.sum(weight, axis=1, keepdims=True)
            near = dot(weight.astype(jnp.bfloat16), values[start : start + reach, :]) / total
            mixed = (
                gates[rows, head : head + 1] * far
                + gates[rows, own + head : own + head + 1] * near
            ).astype(jnp.bfloat16)
            half = share // 2
            for part in range(row_count // share):
                for group in range(2):
                    target = (part * ctx_count + block) * half
                    base = part * share + group * half
                    (out_a, out_b)[group][target : target + half, lanes] = mixed[base : base + half]


def attend(moved, taps, gates, row_count, share, block_len, head_width):
    seq_len = moved.shape[0] * row_count
    width = moved.shape[2]
    return pl.pallas_call(
        functools.partial(attend_kernel, row_count, share, block_len, head_width),
        out_shape=[jax.ShapeDtypeStruct((seq_len // 2, width), jnp.bfloat16)] * 2,
        scratch_shapes=[
            pltpu.VMEM((seq_len, head_width), jnp.bfloat16),
            pltpu.VMEM((seq_len, head_width), jnp.bfloat16),
        ],
        compiler_params=pltpu.CompilerParams(vmem_limit_bytes=48 * 2**20),
        name="attend",
    )(moved, taps, gates)


def project_kernel(paired, spots, left_a, left_b, proj, table, out, total):
    step = pl.program_id(0)
    first = jnp.logical_or(paired, spots[0] == 0)
    parts = []
    for chip in range(left_a.shape[0]):
        if paired:
            parts += [left_a[chip, 0], left_a[chip, 1]]
        else:
            parts.append(jnp.where(first, left_a[chip, 0], left_b[chip, 0]))
            parts.append(jnp.where(first, left_b[chip, 0], left_a[chip, 0]))
    sums = jnp.dot(jnp.concatenate(parts, 1), proj[...], preferred_element_type=jnp.float32)

    @pl.when(step == 0)
    def _():
        total[...] = sums

    @pl.when(step == pl.num_programs(0) - 1)
    def _():
        exp_count = out.shape[0]
        tokens = total.shape[0] // exp_count
        for spot in range(exp_count):
            rows = slice(spot * tokens, (spot + 1) * tokens)
            out[spot, :tokens] = (total[rows] + sums[rows]).astype(jnp.bfloat16)
            if out.shape[1] > tokens:
                out[spot, tokens:] = table[spot]


def run_project(spots, left_a, left_b, paired, proj, table, exp_count, extra):
    depth, cols = proj.shape
    tokens, width = left_a.shape[1:]
    cores = 2 if paired else 1
    chips = depth // (2 * width)
    left_a = left_a.reshape(chips, cores, tokens, width)
    left_b = left_b.reshape(chips, cores, tokens, width)
    left = pl.BlockSpec((chips // 2, cores, tokens, width), lambda i, _: (i, 0, 0, 0))
    unused = pl.BlockSpec((1, 1, tokens, width), lambda i, _: (0, 0, 0, 0))
    rows = tokens // exp_count + (table.shape[1] if extra else 0)
    return pl.pallas_call(
        functools.partial(project_kernel, paired),
        grid_spec=pltpu.PrefetchScalarGridSpec(
            num_scalar_prefetch=1,
            grid=(2,),
            in_specs=[
                left,
                unused if paired else left,
                pl.BlockSpec((depth // 2, cols), lambda i, _: (i, 0)),
                pl.BlockSpec(table.shape, lambda i, _: (0, 0, 0)),
            ],
            out_specs=pl.BlockSpec((exp_count, rows, cols), lambda i, _: (0, 0, 0)),
            scratch_shapes=[pltpu.VMEM((tokens, cols), jnp.float32)],
        ),
        out_shape=jax.ShapeDtypeStruct((exp_count, rows, cols), jnp.bfloat16),
        compiler_params=pltpu.CompilerParams(vmem_limit_bytes=56 * 2**20),
        cost_estimate=pl.CostEstimate(
            flops=2 * tokens * depth * cols,
            bytes_accessed=2 * depth * (tokens + cols) + 2 * exp_count * rows * cols,
            transcendentals=0,
        ),
        name="project",
    )(spots, left_a, left_b, proj, table)


def hold_kernel(count, *refs):
    sources, targets, token, arrivals = refs[:count], refs[count : 2 * count], refs[-2], refs[-1]
    copies = [
        pltpu.make_async_copy(source, target, arrivals.at[spot])
        for spot, (source, target) in enumerate(zip(sources, targets))
    ]
    for copy in copies:
        copy.start()
    token[...] = jnp.zeros_like(token)
    for copy in copies:
        copy.wait()


def hold(blocks):
    count = len(blocks)
    *held, token = pl.pallas_call(
        functools.partial(hold_kernel, count),
        in_specs=[pl.BlockSpec(memory_space=pl.ANY)] * count,
        out_specs=[pl.BlockSpec(memory_space=pltpu.VMEM)] * (count + 1),
        out_shape=[pltpu.VMEM(block.shape, block.dtype) for block in blocks]
        + [jax.ShapeDtypeStruct((8, 128), jnp.float32)],
        scratch_shapes=[pltpu.SemaphoreType.DMA((count,))],
        compiler_params=pltpu.CompilerParams(vmem_limit_bytes=4 * 2**20),
        name="hold",
    )(*blocks)
    return held, token


def expert_kernel(exp_dim, spots, own, along, across, far_a, far_b, gain, gate_w, up_w, gate_v, up_v, route, out, total, squares):
    step = pl.program_id(0)

    @pl.when(step == 0)
    def _():
        total[...] = jnp.zeros_like(total)
        squares[...] = jnp.zeros_like(squares)

    far = jnp.where(step < pl.num_programs(0) // 2, far_a[0], far_b[0])
    block = jnp.concatenate([own[0], along[0], across[0], far], 0)
    first = pl.multiple_of(step * block.shape[1], block.shape[1])
    for spot, weight in enumerate((gate_w, up_w, gate_v, up_v)):
        piece = weight[pl.ds(first, block.shape[1]), :]
        total[spot] += jnp.dot(block, piece, preferred_element_type=jnp.float32)
    lane = squares.shape[1]
    collected = squares[...]
    for part in range(block.shape[1] // lane):
        lanes = slice(part * lane, (part + 1) * lane)
        plain = block[:, lanes].astype(jnp.float32) * (1.0 / gain[0, :, lanes])
        collected = collected + plain * plain
    squares[...] = collected

    @pl.when(step == pl.num_programs(0) - 1)
    def _():
        model_width = pl.num_programs(0) * block.shape[1]
        mean_square = jnp.sum(squares[...], axis=1, keepdims=True) / model_width
        inverse = lax.rsqrt(mean_square + norm_eps)
        tokens = own.shape[1]
        for core in range(2):
            gate_part = total[2 * core] * inverse
            up_part = total[2 * core + 1] * inverse
            active = gate_part / (1.0 + jnp.exp(-gate_part)) * up_part
            for source in range(block.shape[0] // tokens):
                spot = pl.ds(jnp.bitwise_xor(spots[1], source), 1)
                piece = active[source * tokens : (source + 1) * tokens] * route[spot][0]
                piece = piece.astype(jnp.bfloat16)
                if exp_dim == 0:
                    out[core, source] = piece.reshape(out.shape[2:])
                else:
                    out[core, :, spot] = piece.reshape(out.shape[1], 1, *out.shape[3:])


def run_expert(spots, blocks, gain, weights, route, half, exp_dim):
    chip_count, tokens, wide = blocks[0].shape
    cols = wide
    middle = chip_count // 2
    steps = chip_count
    units = weights[0].shape[1]
    exp_count = route.shape[0]
    row_total = exp_count * tokens
    lane = math.gcd(128, cols)
    lead = (exp_count, tokens // half) if exp_dim == 0 else (tokens // half, exp_count)
    by_chip = pl.BlockSpec((1, tokens, cols), lambda i, _: (i, 0, 0))
    by_cols = pl.BlockSpec(memory_space=pltpu.VMEM)
    out = pl.pallas_call(
        functools.partial(expert_kernel, exp_dim),
        grid_spec=pltpu.PrefetchScalarGridSpec(
            num_scalar_prefetch=1,
            grid=(steps,),
            in_specs=[
                by_chip,
                by_chip,
                by_chip,
                pl.BlockSpec(
                    (1, tokens, cols), lambda i, _: (jnp.minimum(i, middle - 1), 0, 0)
                ),
                pl.BlockSpec(
                    (1, tokens, cols), lambda i, _: (jnp.maximum(i - middle, 0), 0, 0)
                ),
                pl.BlockSpec((1, 1, cols), lambda i, _: (i, 0, 0)),
                by_cols,
                by_cols,
                by_cols,
                by_cols,
                pl.BlockSpec((exp_count, tokens, 1), lambda i, _: (0, 0, 0)),
            ],
            out_specs=pl.BlockSpec((2,) + lead + (half, units), lambda i, _: (0, 0, 0, 0, 0)),
            scratch_shapes=[
                pltpu.VMEM((4, row_total, units), jnp.float32),
                pltpu.VMEM((row_total, lane), jnp.float32),
            ],
        ),
        out_shape=jax.ShapeDtypeStruct((2,) + lead + (half, units), jnp.bfloat16),
        compiler_params=pltpu.CompilerParams(vmem_limit_bytes=16 * 2**20),
        cost_estimate=pl.CostEstimate(
            flops=8 * row_total * units * steps * cols,
            bytes_accessed=2 * steps * cols * (row_total + 4 * units),
            transcendentals=2 * row_total * units,
        ),
        name="expert",
    )(spots, *blocks, gain.reshape(steps, 1, cols), *weights, route)
    return out.reshape(2, row_total, units)


def down_kernel(start, spots, active, down_w, down_v, hidden, *outs):
    left = jnp.concatenate([active[0], active[1]], 1)
    cols = hidden.shape[2]
    lanes = pl.ds(pl.multiple_of((pl.program_id(0) + start) * cols, cols), cols)
    right = jnp.concatenate([down_w[:, lanes], down_v[:, lanes]], 0)
    sums = jnp.dot(left, right, preferred_element_type=jnp.float32).astype(jnp.bfloat16)
    kept = outs[0]
    if len(outs) == 1:
        kept[...] = sums.reshape(kept.shape)
    else:
        tokens = sums.shape[0] // len(outs)
        for source, out in enumerate(outs):
            out[...] = sums[source * tokens : (source + 1) * tokens].reshape(out.shape)

    @pl.when(pl.program_id(0) + start == spots[0])
    def _():
        place = (slice(None), pl.ds(spots[1], 1)) if len(outs) == 1 else ...
        piece = kept[place].astype(jnp.float32)
        kept[place] = (piece + hidden[...].reshape(piece.shape)).astype(kept.dtype)


def run_down(spots, active, down_w, down_v, hidden, exp_count, start, stop):
    units = down_w.shape[0]
    chip_count, half, cols = hidden.shape
    rows = active.shape[1]
    whole = stop - start == chip_count
    lead = (chip_count, exp_count) if whole else (chip_count,)
    zeros = (0,) * len(lead + (half,))
    by_cols = pl.BlockSpec(memory_space=pltpu.VMEM)
    count = 1 if whole else exp_count
    shape = lead + (half, (stop - start) * cols)
    return pl.pallas_call(
        functools.partial(down_kernel, start),
        grid_spec=pltpu.PrefetchScalarGridSpec(
            num_scalar_prefetch=1,
            grid=(stop - start,),
            in_specs=[
                pl.BlockSpec((2, rows, units), lambda i, _: (0, 0, 0)),
                by_cols,
                by_cols,
                pl.BlockSpec((chip_count, half, cols), lambda i, _: (0, 0, 0)),
            ],
            out_specs=[pl.BlockSpec(lead + (half, cols), lambda i, _: (*zeros, i))] * count,
        ),
        out_shape=[jax.ShapeDtypeStruct(shape, jnp.bfloat16)] * count,
        compiler_params=pltpu.CompilerParams(vmem_limit_bytes=16 * 2**20),
        cost_estimate=pl.CostEstimate(
            flops=4 * rows * units * cols * (stop - start),
            bytes_accessed=2 * cols * (stop - start) * (rows + 2 * units),
            transcendentals=0,
        ),
        name="down",
    )(spots, active, down_w, down_v, hidden)


def sibling(block):
    return lax.ppermute(block, "core", [(0, 1), (1, 0)])


def plane_step(block, step):
    count = lax.axis_size("exp")
    return lax.ppermute(block, "exp", [(i, i ^ step) for i in range(count)])


def by_heads(
    query_input,
    key_input,
    value_input,
    gate_logits,
    comp_weight,
    out_proj,
    residual_in,
    ffn_gain,
    expert_ids,
    route_gates,
    expert_gate,
    expert_up,
    expert_down,
):
    row_count = query_input.shape[0]
    head_count = comp_weight.shape[2]
    head_width = query_input.shape[1] // head_count
    block_len = comp_weight.shape[1]
    stride_len = block_len // 2
    ctx = ("z", "core")
    chip_count = lax.axis_size("z")
    ctx_count = chip_count * lax.axis_size("core")
    exp_count = lax.axis_size("exp")
    chip_index = lax.axis_index("z")
    core_index = lax.axis_index("core")
    ctx_index = 2 * chip_index + core_index
    exp_index = lax.axis_index("exp")
    own = head_count // ctx_count
    width = own * head_width
    share = row_count // exp_count
    half = share // 2
    seq_len = row_count * ctx_count
    cols = out_proj.shape[1]
    model_width = cols * ctx_count
    own_tokens = ctx_count * share

    other_gate = sibling(expert_gate[0])
    other_up = sibling(expert_up[0])
    other_down = sibling(expert_down[0])

    experts = jnp.arange(exp_count, dtype=jnp.int32)
    table = jnp.sum(
        jnp.where(expert_ids[:, :, None] == experts, route_gates[:, :, None], 0.0), axis=1
    )
    table = jnp.broadcast_to(high_low(table).reshape(1, -1), (ctx_count, 2 * share * exp_count))
    gates = high_low(jax.nn.sigmoid(gate_logits)).reshape(2, 2, row_count, ctx_count, own)
    gates = jnp.transpose(gates, (3, 0, 1, 2, 4)).reshape(ctx_count, -1)
    side = jnp.concatenate([gates, table], 1)
    side = jnp.pad(side, ((0, 0), (0, share * head_width - side.shape[1])))
    side = side.reshape(ctx_count, share, head_width)
    packed = pack(query_input, key_input, value_input, residual_in, side, width)
    moved = lax.all_to_all(packed, ctx, split_axis=0, concat_axis=0, tiled=True)
    spots = side_spots(cols // head_width + 1, own, row_count, share, head_width)
    parts = [moved[:, rows, lanes] for rows, lanes in spots]
    residual = jnp.concatenate(parts[:-1], 2).reshape(own_tokens, cols)
    side = parts[-1].reshape(ctx_count, -1).astype(jnp.float32)
    gate_size = 4 * row_count * own
    gates = side[:, :gate_size].reshape(ctx_count, 2, 2, row_count, own)
    gates = jnp.transpose(gates[:, 0] + gates[:, 1], (0, 2, 1, 3)).reshape(seq_len, 2 * own)
    table = side[:, gate_size : gate_size + 2 * share * exp_count]
    table = table.reshape(chip_count, 2, 2, share, exp_count)
    table = lax.dynamic_index_in_dim(table, core_index, 1, keepdims=False)

    taps = lax.dynamic_slice_in_dim(comp_weight, ctx_index * own, own, 2)
    taps = jnp.transpose(taps.reshape(2, 2, stride_len, own), (0, 3, 1, 2))
    taps = jnp.tile(taps.reshape(4 * own, stride_len), (1, seq_len // stride_len))
    attended = attend(moved, taps, gates, row_count, share, block_len, head_width)

    table = jnp.transpose(table, (3, 1, 0, 2)).reshape(exp_count, -1).astype(jnp.bfloat16)
    table_rows = -(-table.shape[1] // cols)
    table_rows += -table_rows % 16
    table = jnp.pad(table, ((0, 0), (0, table_rows * cols - table.shape[1])))
    table = table.reshape(exp_count, table_rows, cols)
    gain = lax.dynamic_slice_in_dim(ffn_gain, chip_index * 2 * cols, 2 * cols, 0)
    spots = jnp.stack([chip_index, exp_index]).astype(jnp.int32)
    group_tokens = ctx_count * half
    def exchange(pieces):
        return lax.all_to_all(pieces, "exp", split_axis=0, concat_axis=0, tiled=True)

    def settle(pieces, group):
        sums = jnp.sum(pieces[:, :group_tokens].astype(jnp.float32), axis=0)
        own_rows = residual.reshape(ctx_count, 2, half, cols)[:, group]
        sums = sums.reshape(ctx_count, half, cols) + own_rows.astype(jnp.float32)
        sums = sums.reshape(chip_count, 2, half, cols)
        kept = lax.dynamic_index_in_dim(sums, core_index, 1, keepdims=False)
        given = sibling(lax.dynamic_index_in_dim(sums, 1 - core_index, 1, keepdims=False))
        sums = jnp.concatenate(
            [jnp.where(core_index == 0, kept, given), jnp.where(core_index == 0, given, kept)], 2
        )
        scaled = (sums * gain).astype(jnp.bfloat16).reshape(chip_count * half, 2 * cols)
        return sums, scaled

    middle = chip_count // 2
    core_spot = core_index.astype(jnp.int32).reshape(1)
    spread_first = lax.all_gather(attended[0], "z", axis=0)
    spread_first, other_gate, other_up, other_down = lax.optimization_barrier(
        (spread_first, other_gate, other_up, other_down)
    )
    spread_other = sibling(spread_first)
    spread_first, later = lax.optimization_barrier((spread_first, attended[1]))
    spread_second = lax.all_gather(later, ctx, axis=0)
    pieces = exchange(
        run_project(
            core_spot, spread_first, spread_other, False, out_proj, table, exp_count, True
        )
    )
    route = pieces[:, group_tokens:].reshape(exp_count, -1)[:, : 2 * chip_count * share]
    route = jnp.sum(
        route.reshape(exp_count, 2, chip_count, 2, half).astype(jnp.float32), axis=1
    )
    sums_first, scaled_first = settle(pieces, 0)
    pieces = run_project(
        core_spot, spread_second, spread_second, True, out_proj, table, exp_count, False
    )
    pieces, sums_first = lax.optimization_barrier((pieces, sums_first))
    weights = (expert_gate[0], expert_up[0], other_gate, other_up, expert_down[0], other_down)
    *weights, pieces = lax.optimization_barrier((*weights, pieces))
    (*weights, down_w, down_v), token = hold(weights)
    wide = 1 << (2 * cols - 1).bit_length()
    padded = jnp.pad(scaled_first, ((0, 0), (0, wide - 2 * cols)))
    plane_first = lax.all_gather(padded, "z", axis=0)[:, :, : 2 * cols]
    pieces, plane_first, token = lax.optimization_barrier((exchange(pieces), plane_first, token))
    spots = spots + token[0, :2].astype(jnp.int32)
    sums_second, scaled_second = settle(pieces, 1)
    along, across = plane_step(plane_first, 1), plane_step(plane_first, 2)
    plane_second = lax.all_gather(scaled_second, "z", axis=0)
    along, across, plane_second = lax.optimization_barrier((along, across, plane_second))
    far_a, far_b = plane_step(along[:middle], 2), plane_step(across[middle:], 1)
    far_a, far_b, plane_second = lax.optimization_barrier((far_a, far_b, plane_second))

    def run_active(blocks, group):
        route_rows = route[:, :, group].reshape(exp_count, chip_count * half, 1)
        return run_expert(spots, blocks, ffn_gain, weights, route_rows, half, 1 - group)

    def run_outs(active, sums, start, stop):
        return run_down(
            spots, active, down_w, down_v, sums, exp_count, start, stop
        )

    active = run_active((plane_first, along, across, far_a, far_b), 0)
    (first,) = run_outs(active, sums_first, 0, chip_count)
    along, across = plane_step(plane_second, 1), plane_step(plane_second, 2)
    first, along, across = lax.optimization_barrier((first, along, across))
    far_a, far_b = plane_step(along[:middle], 2), plane_step(across[middle:], 1)

    first = lax.psum_scatter(
        first.reshape(chip_count, exp_count * half, model_width),
        "z",
        scatter_dimension=0,
        tiled=True,
    )
    active = run_active((plane_second, along, across, far_a, far_b), 1)

    sides = []
    for start, stop in ((0, middle), (middle, chip_count)):
        own, *given = run_outs(active, sums_second, start, stop)
        total = own.astype(jnp.float32)
        for step, block in enumerate(given, 1):
            total = total + plane_step(block, step).astype(jnp.float32)
        sides.append(total.astype(jnp.bfloat16))
    second = jnp.concatenate(sides, 2)
    second, first = lax.optimization_barrier((second, first))
    second = lax.psum_scatter(second, "z", scatter_dimension=0, tiled=True)
    first = lax.all_to_all(
        first.reshape(exp_count, half, model_width), "exp", split_axis=0, concat_axis=0, tiled=True
    )
    first = jnp.sum(first.astype(jnp.float32), axis=0).astype(jnp.bfloat16)
    return jnp.concatenate([first, second.reshape(half, model_width)], 0)


def specs(ctx):
    in_specs = (
        P(ctx, "exp"),
        P(ctx, "exp"),
        P(ctx, "exp"),
        P(None, ctx, "exp"),
        P(None, None, "exp"),
        P("exp", ctx),
        P((*ctx, "exp"), None),
        P(),
        P((*ctx, "exp"), None),
        P((*ctx, "exp"), None),
        P("exp", None, ctx),
        P("exp", None, ctx),
        P("exp", ctx, None),
    )
    return in_specs, P((*ctx, "exp"), None)


def solution(mesh):
    ctx_count, exp_count = mesh.shape["ctx"], mesh.shape["exp"]

    def run(*args):
        head_count = args[4].shape[2] // exp_count
        share = args[0].shape[0] // (ctx_count * exp_count)
        body, axes, where = general, ("ctx",), mesh
        own = head_count // ctx_count
        head_width = args[0].shape[1] // args[4].shape[2]
        pieces = args[5].shape[1] // (ctx_count * head_width) + 1
        fits = head_count % ctx_count == 0 and share % 32 == 0 and ctx_count % 8 == 0
        fits = fits and exp_count.bit_length() == 3 and exp_count.bit_count() == 1
        fits = fits and args[5].shape[1] % (ctx_count * head_width) == 0
        if fits and pieces % own == 0:
            split = mesh.devices.reshape(ctx_count // 2, 2, exp_count)
            where = jax.sharding.Mesh(split, ("z", "core", "exp"))
            body, axes = by_heads, ("z", "core")
        in_specs, out_specs = specs(axes)
        return jax.shard_map(
            body, mesh=where, in_specs=in_specs, out_specs=out_specs, check_vma=False
        )(*args)

    return run
```

```python
import functools
import math

import jax
import jax.numpy as jnp
from jax import lax
from jax.experimental import pallas as pl
from jax.experimental.pallas import tpu as pltpu
from jax.sharding import PartitionSpec as P

WINDOW = 512


score_gain = 2.0
norm_eps = 1e-06


def passed_along(block, axis, distance):
    devices = range(lax.axis_size(axis))
    route = [(i - distance, i) for i in devices if i - distance in devices]
    return lax.ppermute(block, axis, route)


def head_norm(matrix, head_width):
    row_count = matrix.shape[0]
    shaped = matrix.reshape(row_count, -1, head_width).astype(jnp.float32)
    scaled = shaped * lax.rsqrt(jnp.mean(shaped * shaped, axis=2, keepdims=True) + norm_eps)
    return scaled.reshape(row_count, -1)


def compress(extended, position_weights, head_width):
    stride_len = position_weights.shape[0] // 2
    head_count = position_weights.shape[1]
    blocks = extended.reshape(-1, stride_len, head_count, head_width).astype(jnp.float32)
    first_half = jnp.einsum(
        "nshd,sh->nhd", blocks[:-1], position_weights[:stride_len], precision=lax.Precision.HIGHEST
    )
    second_half = jnp.einsum(
        "nshd,sh->nhd", blocks[1:], position_weights[stride_len:], precision=lax.Precision.HIGHEST
    )
    return (first_half + second_half).reshape(blocks.shape[0] - 1, head_count * head_width)


def window_attention(query_input, key_input, value_input, gate_logits, comp_weight):
    row_count = query_input.shape[0]
    head_count = comp_weight.shape[2]
    head_width = query_input.shape[1] // head_count
    block_len = comp_weight.shape[1]
    stride_len = block_len // 2
    exp_count = lax.axis_size("exp")
    ctx_index = lax.axis_index("ctx")
    scale = score_gain / math.sqrt(head_width)
    query_norm = head_norm(query_input, head_width).astype(jnp.bfloat16)
    key_norm = head_norm(key_input, head_width).astype(jnp.bfloat16)
    next_keys, next_values = passed_along(
        (key_input[:stride_len], value_input[:stride_len]), "ctx", -1
    )
    comp_keys = head_norm(
        compress(jnp.concatenate([key_input, next_keys], 0), comp_weight[0], head_width), head_width
    ).astype(jnp.bfloat16)
    comp_values = compress(
        jnp.concatenate([value_input, next_values], 0), comp_weight[1], head_width
    ).astype(jnp.bfloat16)
    query_pos = ctx_index * row_count + jnp.arange(row_count, dtype=jnp.int32)
    query_heads = query_norm.reshape(row_count, head_count, head_width)
    part_keys = lax.all_gather(comp_keys, "ctx", axis=0, tiled=True)
    part_values = lax.all_gather(comp_values, "ctx", axis=0, tiled=True)
    part_count = part_keys.shape[0]
    scores = jnp.einsum(
        "thd,nhd->htn",
        query_heads,
        part_keys.reshape(part_count, head_count, head_width),
        preferred_element_type=jnp.float32,
    )
    block_end = jnp.arange(part_count, dtype=jnp.int32) * stride_len + block_len - 1
    visible = block_end[None, :] <= query_pos[:, None]
    weights = jnp.where(visible[None], jnp.exp(scale * scores), 0.0)
    running_total = jnp.sum(weights, axis=2).T
    collected = jnp.einsum(
        "htn,nhd->thd",
        weights.astype(jnp.bfloat16),
        part_values.reshape(part_count, head_count, head_width),
        preferred_element_type=jnp.float32,
    )
    cmp_sum = collected.reshape(row_count, -1)
    no_block = (query_pos < block_len - 1).astype(jnp.float32)
    cmp_out = (
        cmp_sum.reshape(row_count, head_count, head_width)
        / (running_total + no_block[:, None])[:, :, None]
    )
    shift_count = max(1, WINDOW // row_count)
    earlier_keys = []
    earlier_values = []
    for distance in range(shift_count, 0, -1):
        moved_keys, moved_values = passed_along((key_norm, value_input), "ctx", distance)
        earlier_keys.append(moved_keys)
        earlier_values.append(moved_values)
    near_keys = jnp.concatenate(earlier_keys + [key_norm], 0)
    near_values = jnp.concatenate(earlier_values + [value_input], 0)
    key_pos = ctx_index * row_count - WINDOW + jnp.arange(near_keys.shape[0], dtype=jnp.int32)
    near_scores = jnp.einsum(
        "thd,shd->hts",
        query_heads,
        near_keys.reshape(-1, head_count, head_width),
        preferred_element_type=jnp.float32,
    )
    inside = (
        (key_pos[None, :] <= query_pos[:, None])
        & (key_pos[None, :] > query_pos[:, None] - WINDOW)
        & (key_pos[None, :] >= 0)
    )
    near_weights = jnp.where(inside[None], jnp.exp(scale * near_scores), 0.0)
    win_total = jnp.sum(near_weights, axis=2).T
    win_sum = jnp.einsum(
        "hts,shd->thd",
        near_weights.astype(jnp.bfloat16),
        near_values.reshape(-1, head_count, head_width),
        preferred_element_type=jnp.float32,
    )
    win_out = win_sum / win_total[:, :, None]
    branch_gates = jax.nn.sigmoid(gate_logits)
    attended = (
        (branch_gates[0][:, :, None] * cmp_out + branch_gates[1][:, :, None] * win_out)
        .reshape(row_count, -1)
        .astype(jnp.bfloat16)
    )
    return attended


def general(
    query_input,
    key_input,
    value_input,
    gate_logits,
    comp_weight,
    out_proj,
    residual_in,
    ffn_gain,
    expert_ids,
    route_gates,
    expert_gate,
    expert_up,
    expert_down,
):
    row_count = query_input.shape[0]
    ctx_count = lax.axis_size("ctx")
    exp_count = lax.axis_size("exp")
    ctx_index = lax.axis_index("ctx")
    exp_index = lax.axis_index("exp")
    share = row_count // exp_count
    seq_len = row_count * ctx_count
    cols = out_proj.shape[1]
    model_width = cols * ctx_count
    hidden_units = expert_gate.shape[2]
    own_tokens = ctx_count * share

    experts = jnp.arange(exp_count, dtype=jnp.int32)
    route_table = jnp.sum(
        jnp.where(expert_ids[:, :, None] == experts, route_gates[:, :, None], 0.0), axis=1
    )
    route_all = lax.all_gather(route_table, ("ctx", "exp"), axis=0, tiled=True)
    route_own = lax.dynamic_slice_in_dim(route_all, exp_index, 1, 1)
    residual = lax.all_to_all(residual_in, "ctx", split_axis=1, concat_axis=0, tiled=True)

    attention_args = (query_input, key_input, value_input, gate_logits, comp_weight)
    attended = window_attention(*attention_args)
    spread_rows = lax.all_gather(
        attended.reshape(1, exp_count, share, -1), "ctx", axis=0, tiled=True
    )
    partial = jnp.einsum(
        "cerh,hd->ecrd", spread_rows, out_proj, preferred_element_type=jnp.float32
    )
    pieces = lax.all_to_all(
        partial.astype(jnp.bfloat16).reshape(exp_count, own_tokens, cols),
        "exp",
        split_axis=0,
        concat_axis=0,
        tiled=True,
    )
    hidden_state = residual.reshape(own_tokens, cols).astype(jnp.float32) + jnp.sum(
        pieces.astype(jnp.float32), axis=0
    )
    gain = lax.dynamic_slice_in_dim(ffn_gain, ctx_index * cols, cols, 0)
    scaled = (hidden_state * gain).astype(jnp.bfloat16)
    squares = jnp.sum(hidden_state * hidden_state, axis=1)
    rows = lax.all_gather(scaled, ("ctx", "exp"), axis=0, tiled=True)
    rows = rows.reshape(ctx_count, seq_len, cols)
    squares = lax.all_gather(squares, ("ctx", "exp"), axis=0, tiled=True)
    mean_square = jnp.sum(squares.reshape(ctx_count, seq_len), axis=0) / model_width
    inverse = lax.rsqrt(mean_square + norm_eps)[:, None]

    gate_part = inverse * jnp.einsum(
        "ctk,ckf->tf",
        rows,
        expert_gate.reshape(ctx_count, cols, hidden_units),
        preferred_element_type=jnp.float32,
    )
    up_part = inverse * jnp.einsum(
        "ctk,ckf->tf",
        rows,
        expert_up.reshape(ctx_count, cols, hidden_units),
        preferred_element_type=jnp.float32,
    )
    activated = (jax.nn.silu(gate_part) * up_part).astype(jnp.bfloat16)
    activated = jnp.transpose(
        activated.reshape(exp_count, ctx_count, share, hidden_units), (1, 0, 2, 3)
    ).reshape(seq_len, hidden_units)
    outs = jnp.dot(activated, expert_down[0], preferred_element_type=jnp.float32)
    outs = (outs * route_own).astype(jnp.bfloat16)
    outs = outs.reshape(ctx_count, exp_count, share, model_width)
    place = (0, exp_index, 0, ctx_index * cols)
    mine = lax.dynamic_slice(outs, place, (ctx_count, 1, share, cols))
    mine = mine.astype(jnp.float32) + hidden_state.reshape(ctx_count, 1, share, cols)
    outs = lax.dynamic_update_slice(outs, mine.astype(jnp.bfloat16), place)
    return lax.psum_scatter(
        outs.reshape(seq_len, model_width), ("ctx", "exp"), scatter_dimension=0, tiled=True
    )


def high_low(values):
    high = lax.reduce_precision(values, 8, 7)
    return jnp.stack([high, values - high], 0).astype(jnp.bfloat16)


def unit_rows(block):
    return block * lax.rsqrt(jnp.mean(block * block, axis=1, keepdims=True) + norm_eps)


def side_spots(count, own, row_count, share, head_width):
    spots = []
    for piece in range(count):
        first = 3 * row_count + piece // own * share
        lane = piece % own * head_width
        spots.append((slice(first, first + share), slice(lane, lane + head_width)))
    return spots


def pack_kernel(query, key, value, residual, side, out):
    row_count, width = query.shape
    share, head_width = side.shape[1:]
    for spot, block in enumerate((query, key, value)):
        out[0, spot * row_count : (spot + 1) * row_count, :] = block[...]
    count = residual.shape[1] // head_width
    spots = side_spots(count + 1, width // head_width, row_count, share, head_width)
    for piece, (rows, lanes) in enumerate(spots[:-1]):
        out[0, rows, lanes] = residual[:, piece * head_width : (piece + 1) * head_width]
    rows, lanes = spots[-1]
    out[0, rows, lanes] = side[0]


def pack(query, key, value, residual, side, width):
    ctx_count, share, head_width = side.shape
    row_count = query.shape[0]
    cols = residual.shape[1] // ctx_count
    rows = 3 * row_count + (cols // head_width + 1) * head_width // width * share
    heads = pl.BlockSpec((row_count, width), lambda i: (0, i))
    return pl.pallas_call(
        pack_kernel,
        grid=(ctx_count,),
        in_specs=[
            heads,
            heads,
            heads,
            pl.BlockSpec((share, cols), lambda i: (0, i)),
            pl.BlockSpec((1, share, head_width), lambda i: (i, 0, 0)),
        ],
        out_specs=pl.BlockSpec((1, rows, width), lambda i: (i, 0, 0)),
        out_shape=jax.ShapeDtypeStruct((ctx_count, rows, width), jnp.bfloat16),
        compiler_params=pltpu.CompilerParams(vmem_limit_bytes=56 * 2**20),
        name="pack",
    )(query, key, value, residual, side)


def attend_kernel(row_count, share, block_len, head_width, moved, taps, gates, out_a, out_b, keys, values):
    ctx_count = moved.shape[0]
    own = moved.shape[2] // head_width
    seq_len = row_count * ctx_count
    stride_len = block_len // 2
    part_count = seq_len // stride_len
    scale = score_gain / math.sqrt(head_width)

    def dot(left, right):
        return jnp.dot(left, right, preferred_element_type=jnp.float32)

    def dot_rows(left, right):
        return lax.dot_general(
            left, right, (((1,), (1,)), ((), ())), preferred_element_type=jnp.float32
        )

    def compressed(row, block):
        group = lax.broadcasted_iota(jnp.int32, (part_count, seq_len), 0)
        token_group = lax.broadcasted_iota(jnp.int32, (part_count, seq_len), 1) // stride_len
        band = jnp.where(token_group == group, taps[row : row + 1, :], 0.0)
        band = jnp.where(token_group == group + 1, taps[row + 1 : row + 2, :], band)
        high = band.astype(jnp.bfloat16)
        low = (band - high.astype(jnp.float32)).astype(jnp.bfloat16)
        return dot(high, block) + dot(low, block)

    for head in range(own):
        lanes = slice(head * head_width, (head + 1) * head_width)
        raw_keys = moved[:, row_count : 2 * row_count, lanes].reshape(seq_len, head_width)
        keys[...] = unit_rows(raw_keys.astype(jnp.float32)).astype(jnp.bfloat16)
        raw_values = moved[:, 2 * row_count : 3 * row_count, lanes].reshape(seq_len, head_width)
        values[...] = raw_values
        comp_keys = unit_rows(compressed(2 * head, raw_keys)).astype(jnp.bfloat16)
        comp_values = compressed(2 * (own + head), raw_values).astype(jnp.bfloat16)
        for block in range(ctx_count):
            query = moved[block, 0:row_count, lanes].astype(jnp.float32)
            query = unit_rows(query).astype(jnp.bfloat16)
            base = block * row_count
            rows = slice(base, base + row_count)
            spot = base + lax.broadcasted_iota(jnp.int32, (row_count, part_count), 0)
            ends = lax.broadcasted_iota(jnp.int32, (row_count, part_count), 1) * stride_len
            seen = ends + (block_len - 1) <= spot
            weight = jnp.where(seen, jnp.exp(scale * dot_rows(query, comp_keys)), 0.0)
            total = jnp.sum(weight, axis=1, keepdims=True)
            total = total + jnp.where(spot[:, :1] < block_len - 1, 1.0, 0.0)
            far = dot(weight.astype(jnp.bfloat16), comp_values) / total
            start = max(0, base - WINDOW)
            reach = base + row_count - start
            score = dot_rows(query, keys[start : start + reach, :])
            weight = jnp.exp(scale * score)
            edges = []
            for first in range(0, reach, row_count):
                piece = weight[:, first : first + row_count]
                offset = base - start - first
                ahead = lax.broadcasted_iota(jnp.int32, (row_count, row_count), 1)
                ahead = ahead - lax.broadcasted_iota(jnp.int32, (row_count, row_count), 0)
                if offset < row_count:
                    piece = jnp.where(ahead <= offset, piece, 0.0)
                if offset + row_count > WINDOW:
                    piece = jnp.where(ahead > offset - WINDOW, piece, 0.0)
                edges.append(piece)
            weight = jnp.concatenate(edges, 1)
            total = jnp.sum(weight, axis=1, keepdims=True)
            near = dot(weight.astype(jnp.bfloat16), values[start : start + reach, :]) / total
            mixed = (
                gates[rows, head : head + 1] * far
                + gates[rows, own + head : own + head + 1] * near
            ).astype(jnp.bfloat16)
            half = share // 2
            for part in range(row_count // share):
                for group in range(2):
                    target = (part * ctx_count + block) * half
                    base = part * share + group * half
                    (out_a, out_b)[group][target : target + half, lanes] = mixed[base : base + half]


def attend(moved, taps, gates, row_count, share, block_len, head_width):
    seq_len = moved.shape[0] * row_count
    width = moved.shape[2]
    return pl.pallas_call(
        functools.partial(attend_kernel, row_count, share, block_len, head_width),
        out_shape=[jax.ShapeDtypeStruct((seq_len // 2, width), jnp.bfloat16)] * 2,
        scratch_shapes=[
            pltpu.VMEM((seq_len, head_width), jnp.bfloat16),
            pltpu.VMEM((seq_len, head_width), jnp.bfloat16),
        ],
        compiler_params=pltpu.CompilerParams(vmem_limit_bytes=48 * 2**20),
        name="attend",
    )(moved, taps, gates)


def project_kernel(paired, spots, left_a, left_b, proj, table, out, total):
    step = pl.program_id(0)
    first = jnp.logical_or(paired, spots[0] == 0)
    parts = []
    for chip in range(left_a.shape[0]):
        if paired:
            parts += [left_a[chip, 0], left_a[chip, 1]]
        else:
            parts.append(jnp.where(first, left_a[chip, 0], left_b[chip, 0]))
            parts.append(jnp.where(first, left_b[chip, 0], left_a[chip, 0]))
    sums = jnp.dot(jnp.concatenate(parts, 1), proj[...], preferred_element_type=jnp.float32)

    @pl.when(step == 0)
    def _():
        total[...] = sums

    @pl.when(step == pl.num_programs(0) - 1)
    def _():
        exp_count = out.shape[0]
        tokens = total.shape[0] // exp_count
        for spot in range(exp_count):
            rows = slice(spot * tokens, (spot + 1) * tokens)
            out[spot, :tokens] = (total[rows] + sums[rows]).astype(jnp.bfloat16)
            if out.shape[1] > tokens:
                out[spot, tokens:] = table[spot]


def run_project(spots, left_a, left_b, paired, proj, table, exp_count, extra):
    depth, cols = proj.shape
    tokens, width = left_a.shape[1:]
    cores = 2 if paired else 1
    chips = depth // (2 * width)
    left_a = left_a.reshape(chips, cores, tokens, width)
    left_b = left_b.reshape(chips, cores, tokens, width)
    left = pl.BlockSpec((chips // 2, cores, tokens, width), lambda i, _: (i, 0, 0, 0))
    unused = pl.BlockSpec((1, 1, tokens, width), lambda i, _: (0, 0, 0, 0))
    rows = tokens // exp_count + (table.shape[1] if extra else 0)
    return pl.pallas_call(
        functools.partial(project_kernel, paired),
        grid_spec=pltpu.PrefetchScalarGridSpec(
            num_scalar_prefetch=1,
            grid=(2,),
            in_specs=[
                left,
                unused if paired else left,
                pl.BlockSpec((depth // 2, cols), lambda i, _: (i, 0)),
                pl.BlockSpec(table.shape, lambda i, _: (0, 0, 0)),
            ],
            out_specs=pl.BlockSpec((exp_count, rows, cols), lambda i, _: (0, 0, 0)),
            scratch_shapes=[pltpu.VMEM((tokens, cols), jnp.float32)],
        ),
        out_shape=jax.ShapeDtypeStruct((exp_count, rows, cols), jnp.bfloat16),
        compiler_params=pltpu.CompilerParams(vmem_limit_bytes=56 * 2**20),
        cost_estimate=pl.CostEstimate(
            flops=2 * tokens * depth * cols,
            bytes_accessed=2 * depth * (tokens + cols) + 2 * exp_count * rows * cols,
            transcendentals=0,
        ),
        name="project",
    )(spots, left_a, left_b, proj, table)


def expert_kernel(exp_dim, spots, own, along, across, far_a, far_b, gain, gate_w, up_w, gate_v, up_v, route, out, total, squares):
    step = pl.program_id(0)

    @pl.when(step == 0)
    def _():
        total[...] = jnp.zeros_like(total)
        squares[...] = jnp.zeros_like(squares)

    far = jnp.where(step < pl.num_programs(0) // 2, far_a[0], far_b[0])
    block = jnp.concatenate([own[0], along[0], across[0], far], 0)
    for spot, weight in enumerate((gate_w, up_w, gate_v, up_v)):
        total[spot] += jnp.dot(block, weight[...], preferred_element_type=jnp.float32)
    lane = squares.shape[1]
    collected = squares[...]
    for part in range(block.shape[1] // lane):
        lanes = slice(part * lane, (part + 1) * lane)
        plain = block[:, lanes].astype(jnp.float32) * (1.0 / gain[0, :, lanes])
        collected = collected + plain * plain
    squares[...] = collected

    @pl.when(step == pl.num_programs(0) - 1)
    def _():
        model_width = pl.num_programs(0) * block.shape[1]
        mean_square = jnp.sum(squares[...], axis=1, keepdims=True) / model_width
        inverse = lax.rsqrt(mean_square + norm_eps)
        tokens = own.shape[1]
        for core in range(2):
            gate_part = total[2 * core] * inverse
            up_part = total[2 * core + 1] * inverse
            active = gate_part / (1.0 + jnp.exp(-gate_part)) * up_part
            for source in range(block.shape[0] // tokens):
                spot = pl.ds(jnp.bitwise_xor(spots[1], source), 1)
                piece = active[source * tokens : (source + 1) * tokens] * route[spot][0]
                piece = piece.astype(jnp.bfloat16)
                if exp_dim == 0:
                    out[core, source] = piece.reshape(out.shape[2:])
                else:
                    out[core, :, spot] = piece.reshape(out.shape[1], 1, *out.shape[3:])


def run_expert(spots, blocks, gain, weights, route, half, exp_dim):
    chip_count, tokens, wide = blocks[0].shape
    cols = wide
    middle = chip_count // 2
    steps = chip_count
    units = weights[0].shape[1]
    exp_count = route.shape[0]
    row_total = exp_count * tokens
    lane = math.gcd(128, cols)
    lead = (exp_count, tokens // half) if exp_dim == 0 else (tokens // half, exp_count)
    by_chip = pl.BlockSpec((1, tokens, cols), lambda i, _: (i, 0, 0))
    by_cols = pl.BlockSpec((cols, units), lambda i, _: (i, 0))
    out = pl.pallas_call(
        functools.partial(expert_kernel, exp_dim),
        grid_spec=pltpu.PrefetchScalarGridSpec(
            num_scalar_prefetch=1,
            grid=(steps,),
            in_specs=[
                by_chip,
                by_chip,
                by_chip,
                pl.BlockSpec(
                    (1, tokens, cols), lambda i, _: (jnp.minimum(i, middle - 1), 0, 0)
                ),
                pl.BlockSpec(
                    (1, tokens, cols), lambda i, _: (jnp.maximum(i - middle, 0), 0, 0)
                ),
                pl.BlockSpec((1, 1, cols), lambda i, _: (i, 0, 0)),
                by_cols,
                by_cols,
                by_cols,
                by_cols,
                pl.BlockSpec((exp_count, tokens, 1), lambda i, _: (0, 0, 0)),
            ],
            out_specs=pl.BlockSpec((2,) + lead + (half, units), lambda i, _: (0, 0, 0, 0, 0)),
            scratch_shapes=[
                pltpu.VMEM((4, row_total, units), jnp.float32),
                pltpu.VMEM((row_total, lane), jnp.float32),
            ],
        ),
        out_shape=jax.ShapeDtypeStruct((2,) + lead + (half, units), jnp.bfloat16),
        compiler_params=pltpu.CompilerParams(vmem_limit_bytes=56 * 2**20),
        cost_estimate=pl.CostEstimate(
            flops=8 * row_total * units * steps * cols,
            bytes_accessed=2 * steps * cols * (row_total + 4 * units),
            transcendentals=2 * row_total * units,
        ),
        name="expert",
    )(spots, *blocks, gain.reshape(steps, 1, cols), *weights, route)
    return out.reshape(2, row_total, units)


def down_kernel(start, spots, active, down_w, down_v, hidden, *outs):
    left = jnp.concatenate([active[0], active[1]], 1)
    right = jnp.concatenate([down_w[...], down_v[...]], 0)
    sums = jnp.dot(left, right, preferred_element_type=jnp.float32).astype(jnp.bfloat16)
    kept = outs[0]
    if len(outs) == 1:
        kept[...] = sums.reshape(kept.shape)
    else:
        tokens = sums.shape[0] // len(outs)
        for source, out in enumerate(outs):
            out[...] = sums[source * tokens : (source + 1) * tokens].reshape(out.shape)

    @pl.when(pl.program_id(0) + start == spots[0])
    def _():
        place = (slice(None), pl.ds(spots[1], 1)) if len(outs) == 1 else ...
        piece = kept[place].astype(jnp.float32)
        kept[place] = (piece + hidden[...].reshape(piece.shape)).astype(kept.dtype)


def run_down(spots, active, down_w, down_v, hidden, exp_count, start, stop):
    units = down_w.shape[0]
    chip_count, half, cols = hidden.shape
    rows = active.shape[1]
    whole = stop - start == chip_count
    lead = (chip_count, exp_count) if whole else (chip_count,)
    zeros = (0,) * len(lead + (half,))
    by_cols = pl.BlockSpec((units, cols), lambda i, _: (0, i + start))
    count = 1 if whole else exp_count
    shape = lead + (half, (stop - start) * cols)
    return pl.pallas_call(
        functools.partial(down_kernel, start),
        grid_spec=pltpu.PrefetchScalarGridSpec(
            num_scalar_prefetch=1,
            grid=(stop - start,),
            in_specs=[
                pl.BlockSpec((2, rows, units), lambda i, _: (0, 0, 0)),
                by_cols,
                by_cols,
                pl.BlockSpec((chip_count, half, cols), lambda i, _: (0, 0, 0)),
            ],
            out_specs=[pl.BlockSpec(lead + (half, cols), lambda i, _: (*zeros, i))] * count,
        ),
        out_shape=[jax.ShapeDtypeStruct(shape, jnp.bfloat16)] * count,
        compiler_params=pltpu.CompilerParams(vmem_limit_bytes=56 * 2**20),
        cost_estimate=pl.CostEstimate(
            flops=4 * rows * units * cols * (stop - start),
            bytes_accessed=2 * cols * (stop - start) * (rows + 2 * units),
            transcendentals=0,
        ),
        name="down",
    )(spots, active, down_w, down_v, hidden)


def sibling(block):
    return lax.ppermute(block, "core", [(0, 1), (1, 0)])


def plane_step(block, step):
    count = lax.axis_size("exp")
    return lax.ppermute(block, "exp", [(i, i ^ step) for i in range(count)])


def by_heads(
    query_input,
    key_input,
    value_input,
    gate_logits,
    comp_weight,
    out_proj,
    residual_in,
    ffn_gain,
    expert_ids,
    route_gates,
    expert_gate,
    expert_up,
    expert_down,
):
    row_count = query_input.shape[0]
    head_count = comp_weight.shape[2]
    head_width = query_input.shape[1] // head_count
    block_len = comp_weight.shape[1]
    stride_len = block_len // 2
    ctx = ("z", "core")
    chip_count = lax.axis_size("z")
    ctx_count = chip_count * lax.axis_size("core")
    exp_count = lax.axis_size("exp")
    chip_index = lax.axis_index("z")
    core_index = lax.axis_index("core")
    ctx_index = 2 * chip_index + core_index
    exp_index = lax.axis_index("exp")
    own = head_count // ctx_count
    width = own * head_width
    share = row_count // exp_count
    half = share // 2
    seq_len = row_count * ctx_count
    cols = out_proj.shape[1]
    model_width = cols * ctx_count
    own_tokens = ctx_count * share

    other_gate = sibling(expert_gate[0])
    other_up = sibling(expert_up[0])
    other_down = sibling(expert_down[0])

    experts = jnp.arange(exp_count, dtype=jnp.int32)
    table = jnp.sum(
        jnp.where(expert_ids[:, :, None] == experts, route_gates[:, :, None], 0.0), axis=1
    )
    table = jnp.broadcast_to(high_low(table).reshape(1, -1), (ctx_count, 2 * share * exp_count))
    gates = high_low(jax.nn.sigmoid(gate_logits)).reshape(2, 2, row_count, ctx_count, own)
    gates = jnp.transpose(gates, (3, 0, 1, 2, 4)).reshape(ctx_count, -1)
    side = jnp.concatenate([gates, table], 1)
    side = jnp.pad(side, ((0, 0), (0, share * head_width - side.shape[1])))
    side = side.reshape(ctx_count, share, head_width)
    packed = pack(query_input, key_input, value_input, residual_in, side, width)
    moved = lax.all_to_all(packed, ctx, split_axis=0, concat_axis=0, tiled=True)
    spots = side_spots(cols // head_width + 1, own, row_count, share, head_width)
    parts = [moved[:, rows, lanes] for rows, lanes in spots]
    residual = jnp.concatenate(parts[:-1], 2).reshape(own_tokens, cols)
    side = parts[-1].reshape(ctx_count, -1).astype(jnp.float32)
    gate_size = 4 * row_count * own
    gates = side[:, :gate_size].reshape(ctx_count, 2, 2, row_count, own)
    gates = jnp.transpose(gates[:, 0] + gates[:, 1], (0, 2, 1, 3)).reshape(seq_len, 2 * own)
    table = side[:, gate_size : gate_size + 2 * share * exp_count]
    table = table.reshape(chip_count, 2, 2, share, exp_count)
    table = lax.dynamic_index_in_dim(table, core_index, 1, keepdims=False)

    taps = lax.dynamic_slice_in_dim(comp_weight, ctx_index * own, own, 2)
    taps = jnp.transpose(taps.reshape(2, 2, stride_len, own), (0, 3, 1, 2))
    taps = jnp.tile(taps.reshape(4 * own, stride_len), (1, seq_len // stride_len))
    attended = attend(moved, taps, gates, row_count, share, block_len, head_width)

    table = jnp.transpose(table, (3, 1, 0, 2)).reshape(exp_count, -1).astype(jnp.bfloat16)
    table_rows = -(-table.shape[1] // cols)
    table_rows += -table_rows % 16
    table = jnp.pad(table, ((0, 0), (0, table_rows * cols - table.shape[1])))
    table = table.reshape(exp_count, table_rows, cols)
    gain = lax.dynamic_slice_in_dim(ffn_gain, chip_index * 2 * cols, 2 * cols, 0)
    spots = jnp.stack([chip_index, exp_index]).astype(jnp.int32)
    group_tokens = ctx_count * half
    def exchange(pieces):
        return lax.all_to_all(pieces, "exp", split_axis=0, concat_axis=0, tiled=True)

    def settle(pieces, group):
        sums = jnp.sum(pieces[:, :group_tokens].astype(jnp.float32), axis=0)
        own_rows = residual.reshape(ctx_count, 2, half, cols)[:, group]
        sums = sums.reshape(ctx_count, half, cols) + own_rows.astype(jnp.float32)
        sums = sums.reshape(chip_count, 2, half, cols)
        kept = lax.dynamic_index_in_dim(sums, core_index, 1, keepdims=False)
        given = sibling(lax.dynamic_index_in_dim(sums, 1 - core_index, 1, keepdims=False))
        sums = jnp.concatenate(
            [jnp.where(core_index == 0, kept, given), jnp.where(core_index == 0, given, kept)], 2
        )
        scaled = (sums * gain).astype(jnp.bfloat16).reshape(chip_count * half, 2 * cols)
        return sums, scaled

    middle = chip_count // 2
    core_spot = core_index.astype(jnp.int32).reshape(1)
    spread_first = lax.all_gather(attended[0], "z", axis=0)
    spread_first, other_gate, other_up, other_down = lax.optimization_barrier(
        (spread_first, other_gate, other_up, other_down)
    )
    spread_other = sibling(spread_first)
    spread_first, later = lax.optimization_barrier((spread_first, attended[1]))
    spread_second = lax.all_gather(later, ctx, axis=0)
    pieces = exchange(
        run_project(
            core_spot, spread_first, spread_other, False, out_proj, table, exp_count, True
        )
    )
    route = pieces[:, group_tokens:].reshape(exp_count, -1)[:, : 2 * chip_count * share]
    route = jnp.sum(
        route.reshape(exp_count, 2, chip_count, 2, half).astype(jnp.float32), axis=1
    )
    sums_first, scaled_first = settle(pieces, 0)
    pieces = run_project(
        core_spot, spread_second, spread_second, True, out_proj, table, exp_count, False
    )
    pieces, sums_first = lax.optimization_barrier((pieces, sums_first))
    wide = 1 << (2 * cols - 1).bit_length()
    padded = jnp.pad(scaled_first, ((0, 0), (0, wide - 2 * cols)))
    plane_first = lax.all_gather(padded, "z", axis=0)[:, :, : 2 * cols]
    pieces, plane_first = lax.optimization_barrier((exchange(pieces), plane_first))
    sums_second, scaled_second = settle(pieces, 1)
    along, across = plane_step(plane_first, 1), plane_step(plane_first, 2)
    plane_second = lax.all_gather(scaled_second, "z", axis=0)
    along, across, plane_second = lax.optimization_barrier((along, across, plane_second))
    far_a, far_b = plane_step(along[:middle], 2), plane_step(across[middle:], 1)
    far_a, far_b, plane_second = lax.optimization_barrier((far_a, far_b, plane_second))
    weights = (expert_gate[0], expert_up[0], other_gate, other_up)

    def run_active(blocks, group):
        route_rows = route[:, :, group].reshape(exp_count, chip_count * half, 1)
        return run_expert(spots, blocks, ffn_gain, weights, route_rows, half, 1 - group)

    def run_outs(active, sums, start, stop):
        return run_down(
            spots, active, expert_down[0], other_down, sums, exp_count, start, stop
        )

    active = run_active((plane_first, along, across, far_a, far_b), 0)
    (first,) = run_outs(active, sums_first, 0, chip_count)
    along, across = plane_step(plane_second, 1), plane_step(plane_second, 2)
    first, along, across = lax.optimization_barrier((first, along, across))
    far_a, far_b = plane_step(along[:middle], 2), plane_step(across[middle:], 1)

    first = lax.psum_scatter(
        first.reshape(chip_count, exp_count * half, model_width),
        "z",
        scatter_dimension=0,
        tiled=True,
    )
    active = run_active((plane_second, along, across, far_a, far_b), 1)

    sides = []
    for start, stop in ((0, middle), (middle, chip_count)):
        own, *given = run_outs(active, sums_second, start, stop)
        total = own.astype(jnp.float32)
        for step, block in enumerate(given, 1):
            total = total + plane_step(block, step).astype(jnp.float32)
        sides.append(total.astype(jnp.bfloat16))
    second = jnp.concatenate(sides, 2)
    second, first = lax.optimization_barrier((second, first))
    second = lax.psum_scatter(second, "z", scatter_dimension=0, tiled=True)
    first = lax.all_to_all(
        first.reshape(exp_count, half, model_width), "exp", split_axis=0, concat_axis=0, tiled=True
    )
    first = jnp.sum(first.astype(jnp.float32), axis=0).astype(jnp.bfloat16)
    return jnp.concatenate([first, second.reshape(half, model_width)], 0)


def specs(ctx):
    in_specs = (
        P(ctx, "exp"),
        P(ctx, "exp"),
        P(ctx, "exp"),
        P(None, ctx, "exp"),
        P(None, None, "exp"),
        P("exp", ctx),
        P((*ctx, "exp"), None),
        P(),
        P((*ctx, "exp"), None),
        P((*ctx, "exp"), None),
        P("exp", None, ctx),
        P("exp", None, ctx),
        P("exp", ctx, None),
    )
    return in_specs, P((*ctx, "exp"), None)


def solution(mesh):
    ctx_count, exp_count = mesh.shape["ctx"], mesh.shape["exp"]

    def run(*args):
        head_count = args[4].shape[2] // exp_count
        share = args[0].shape[0] // (ctx_count * exp_count)
        body, axes, where = general, ("ctx",), mesh
        own = head_count // ctx_count
        head_width = args[0].shape[1] // args[4].shape[2]
        pieces = args[5].shape[1] // (ctx_count * head_width) + 1
        fits = head_count % ctx_count == 0 and share % 32 == 0 and ctx_count % 8 == 0
        fits = fits and exp_count.bit_length() == 3 and exp_count.bit_count() == 1
        fits = fits and args[5].shape[1] % (ctx_count * head_width) == 0
        if fits and pieces % own == 0:
            split = mesh.devices.reshape(ctx_count // 2, 2, exp_count)
            where = jax.sharding.Mesh(split, ("z", "core", "exp"))
            body, axes = by_heads, ("z", "core")
        in_specs, out_specs = specs(axes)
        return jax.shard_map(
            body, mesh=where, in_specs=in_specs, out_specs=out_specs, check_vma=False
        )(*args)

    return run
```
